128 devices in a mesh: dp: 8 (over x, z_hi), row: 16 (over y, z_lo, core).
Axes of the slice: x: 4, y: 4, z: 4 (z_hi: 2, z_lo: 2; z = z_hi * 2 + z_lo), core: 2. Of those that a mesh axis runs over, the one named last changes fastest.
Arguments:
- pair_rep: bfloat16 [8, 384, 384, 128], P('dp', 'row'), may hold values from -6 to 6
- grad_out: bfloat16 [8, 384, 384, 128], P('dp', 'row'), may hold values from -6 to 6
- crop_len: int32 [8], P('dp'), may hold values from 288 to 384, as said below
- ln_gain: float32 [128], replicated, may hold values from 0.25 to 1.75
- ln_bias: float32 [128], replicated, may hold values from -3 to 3
- w_proj: bfloat16 [128, 512], replicated, may hold values from -0.5 to 0.5
- gate_bias: float32 [128], replicated, may hold values from -4 to 4
- w_bias: bfloat16 [128, 4], replicated, may hold values from -0.5 to 0.5
- w_out: bfloat16 [128, 128], replicated, may hold values from -0.5 to 0.5
Outputs:
- pair_grad: bfloat16 [8, 384, 384, 128], P('dp', 'row')
- proj_grad: float32 [128, 512], replicated
- gate_bias_grad: float32 [128], replicated
- bias_w_grad: float32 [128, 4], replicated
- out_w_grad: float32 [128, 128], replicated
- gain_grad: float32 [128], replicated
- shift_grad: float32 [128], replicated
The draws below stay inside these ranges and needn't reach their ends.
Inputs may be any that keep to these rules, and one draw needn't show every extreme that they name: `crop_len`: every crop is padded to 384; in every draw one crop fills all 384 residues and one has 288.
All inputs are finite; a program needn't handle non-finite values.
Results may differ from the reference program's by a relative error of at most 0.025.
Values may be sent and summed in bfloat16 or wider, within the bound.
No kernel may reach another device: no remote copies, remote signals or barrier semaphores. Data moves between devices by JAX's collectives and lax.ppermute only.
A program may use at most 128 MiB of HBM per device.

```python
import math
import jax
import jax.numpy as jnp
from jax import lax

C = 128
H = 4
HD = 32
ROWS_DEV = 24
CROP = 384
GROUPS = 8


def draw_crop_len(key, part):
    key = jax.random.fold_in(key, 7)
    key_draw, key_order = jax.random.split(key)
    lowest = CROP * 3 // 4
    lengths = jax.random.randint(key_draw, (GROUPS,), lowest, CROP + 1)
    shuffled = jax.random.permutation(key_order, GROUPS)
    lengths = lengths.at[shuffled[0]].set(CROP).at[shuffled[1]].set(lowest)
    return lengths.astype(jnp.int32)


def block_scale(own_key, extent, shards, least, largest):
    loudness, own = 1.0, jax.random.fold_in(own_key, 6)
    for position, parts in shards:
        steps = jnp.exp(jax.random.uniform(jax.random.fold_in(own, position), (parts,), jnp.float32, least / len(shards), largest / len(shards)))
        loudness = loudness * jnp.repeat(steps, extent[position] // parts).reshape([-1 if axis == position else 1 for axis in range(len(extent))])
    return loudness


def bell_draw(rng, shape, deviation, reach, cuts=(), kind=jnp.bfloat16):
    loudness = block_scale(rng, shape, cuts, -0.22, 0.18) if cuts else 1.0
    result = jax.random.normal(rng, shape, jnp.float32) * deviation * loudness
    return jnp.minimum(jnp.maximum(result, -reach), reach).astype(kind)


def setup_inputs(seed: int = 0) -> dict:
    seeds = jax.random.split(jax.random.key(seed), 10)
    return {
        "pair_rep": bell_draw(seeds[0], (GROUPS, CROP, CROP, C), 1.0, 6.0, ((0, 8), (1, 16))),
        "grad_out": bell_draw(seeds[1], (GROUPS, CROP, CROP, C), 1.0, 6.0, ((0, 8), (1, 16))),
        "crop_len": draw_crop_len(jax.random.fold_in(seeds[9], 71), 0),
        "ln_gain": jnp.clip(1.0 + 0.15 * jax.random.normal(seeds[3], (C,), jnp.float32), 0.25, 1.75),
        "ln_bias": bell_draw(seeds[4], (C,), 0.5, 3.0, (), jnp.float32),
        "w_proj": bell_draw(seeds[5], (C, 4 * C), C ** -0.5, 0.5),
        "gate_bias": bell_draw(seeds[6], (C,), 1.0, 4.0, (), jnp.float32),
        "w_bias": bell_draw(seeds[7], (C, H), C ** -0.5, 0.5),
        "w_out": bell_draw(seeds[8], (C, C), C ** -0.5, 0.5),
    }


EPSILON = 1e-05

def layer_norm(values_in, scale_vec, shift_vec):
    center = lax.optimization_barrier(jnp.mean(values_in, axis=-1, keepdims=True))
    spread = lax.optimization_barrier(jnp.mean(jnp.square(values_in - center), axis=-1, keepdims=True))
    return (values_in - center) * lax.rsqrt(spread + EPSILON) * scale_vec + shift_vec

def rounded(array):
    return lax.optimization_barrier(array.astype(jnp.bfloat16)).astype(jnp.float32)

def reference(pair_rep, grad_out, crop_len, ln_gain, ln_bias, w_proj, gate_bias, w_bias, w_out):
    head_shape = (CROP, ROWS_DEV, H, HD)

    def one_group(group_args):
        pair_group, cot_group, length = group_args
        pair_f = pair_group.astype(jnp.float32)
        normed_f, ln_back = jax.vjp(layer_norm, pair_f, ln_gain, ln_bias)
        normed = normed_f.astype(jnp.bfloat16)
        flat_norm = normed.reshape(-1, C)
        projected = jnp.dot(flat_norm, w_proj, preferred_element_type=jnp.float32).reshape(CROP, CROP, 4 * C)
        query_all = rounded(projected[..., :C] / math.sqrt(HD))
        key_all = rounded(projected[..., C:2 * C])
        value_all = rounded(projected[..., 2 * C:3 * C])
        gate_all = jax.nn.sigmoid(projected[..., 3 * C:] + gate_bias)
        bias_raw = jnp.dot(flat_norm, w_bias, preferred_element_type=jnp.float32).reshape(CROP, CROP, H)
        bias_plane = rounded(bias_raw.transpose(2, 0, 1))
        positions = jnp.arange(CROP, dtype=jnp.int32)
        in_crop = positions < length
        cot_masked = jnp.where(in_crop[:, None, None] & in_crop[None, :, None], cot_group, jnp.zeros_like(cot_group))

        def column_block(carry, offset):
            bias_grad, gate_grad = carry

            def cut(array):
                return lax.dynamic_slice_in_dim(array, offset, ROWS_DEV, 1)
            query_blk = cut(query_all).reshape(head_shape)
            key_blk = cut(key_all).reshape(head_shape)
            value_blk = cut(value_all).reshape(head_shape)
            gate_blk = cut(gate_all).reshape(head_shape)
            cot_blk = cut(cot_masked)
            scores = jnp.einsum('ibhd,kbhd->bhki', query_blk, key_blk) + bias_plane[None]
            exponent = jnp.where(in_crop[None, None, :, None], jnp.exp(scores), 0.0)
            weights = exponent / lax.optimization_barrier(jnp.sum(exponent, axis=2, keepdims=True))
            weights_b = rounded(weights)
            attended = jnp.einsum('bhki,kbhd->ibhd', weights_b, value_blk)
            output_blk = (gate_blk * attended).astype(jnp.bfloat16).reshape(CROP, ROWS_DEV, C)
            d_out = jnp.dot(cot_blk.reshape(-1, C), w_out.T, preferred_element_type=jnp.float32).reshape(head_shape)
            d_gate = d_out * attended * gate_blk * (1.0 - gate_blk)
            d_attended = rounded(d_out * gate_blk)
            d_weights = jnp.einsum('ibhd,kbhd->bhki', d_attended, value_blk)
            d_values = jnp.einsum('bhki,ibhd->kbhd', weights_b, d_attended)
            d_scores = weights * (d_weights - lax.optimization_barrier(jnp.sum(weights * d_weights, axis=2, keepdims=True)))
            d_scores_b = rounded(d_scores)
            d_query = jnp.einsum('bhki,kbhd->ibhd', d_scores_b, key_blk) / math.sqrt(HD)
            d_keys = jnp.einsum('bhki,ibhd->kbhd', d_scores_b, query_blk)
            pieces = [piece_grad.reshape(CROP, ROWS_DEV, C) for piece_grad in (d_query, d_keys, d_values, d_gate)]
            d_proj = jnp.concatenate(pieces, axis=-1).astype(jnp.bfloat16)
            new_carry = (bias_grad + lax.optimization_barrier(jnp.sum(d_scores, axis=0)), gate_grad + lax.optimization_barrier(jnp.sum(d_gate.reshape(-1, C), axis=0)))
            return (new_carry, (d_proj, output_blk))
        starts = jnp.arange(CROP // ROWS_DEV, dtype=jnp.int32) * ROWS_DEV
        init = (jnp.zeros((H, CROP, CROP), jnp.float32), jnp.zeros((C,), jnp.float32))
        (bias_grad, gate_grad), (d_projs, outputs) = lax.scan(column_block, init, starts)
        d_proj_all = d_projs.transpose(1, 0, 2, 3).reshape(CROP, CROP, 4 * C)
        output_all = outputs.transpose(1, 0, 2, 3).reshape(CROP, CROP, C)
        bias_grad_b = rounded(bias_grad)
        d_normed = jnp.dot(d_proj_all.reshape(-1, 4 * C), w_proj.T, preferred_element_type=jnp.float32).reshape(CROP, CROP, C)
        d_normed = d_normed + jnp.einsum('hki,ch->kic', bias_grad_b, w_bias.astype(jnp.float32))
        d_normed = rounded(d_normed)
        pair_grad, gain_part, shift_part = ln_back(d_normed)
        proj_part = jnp.dot(flat_norm.T, d_proj_all.reshape(-1, 4 * C), preferred_element_type=jnp.float32)
        bias_w_part = jnp.einsum('kic,hki->ch', normed.astype(jnp.float32), bias_grad_b)
        out_w_part = jnp.dot(output_all.reshape(-1, C).T, cot_masked.reshape(-1, C), preferred_element_type=jnp.float32)
        return (pair_grad.astype(jnp.bfloat16), (proj_part, gate_grad, bias_w_part, out_w_part, gain_part, shift_part))
    pair_grads, partials = lax.map(one_group, (pair_rep, grad_out, crop_len))
    totals = [lax.optimization_barrier(jnp.sum(partial_sum, axis=0)) / CROP for partial_sum in partials]
    return (pair_grads, totals[0], totals[1], totals[2], totals[3], totals[4], totals[5])
```

```python
import functools
import math

import jax
import jax.numpy as jnp
from jax import lax
from jax.experimental import pallas as pl
from jax.experimental.pallas import tpu as pltpu
from jax.sharding import PartitionSpec as P

F32, BF = jnp.float32, jnp.bfloat16
EPSILON = 1e-05
LOG2E = 1.4426950408889634
LN2 = 0.6931471805599453
NN = (((1,), (0,)), ((), ()))
NT = (((1,), (1,)), ((), ()))
TN = (((0,), (0,)), ((), ()))
MIB = 2**20
DEAD = -1e30
CHUNKS = (12, 12)


def dot(a, b, dims=NN):
    return lax.dot_general(a, b, dims, preferred_element_type=F32)


def norm_parts(x):
    centered = x - jnp.mean(x, axis=-1, keepdims=True)
    scale = lax.rsqrt(jnp.mean(centered * centered, axis=-1, keepdims=True) + EPSILON)
    return centered * scale, scale


def fold_rows(a):
    return jnp.sum(a.reshape(a.shape[0] // 8, 8, a.shape[1]), axis=0)


def logits_kernel(pair_ref, gain_ref, shift_ref, wbt_ref, out_ref):
    rows, size, channels = pair_ref.shape
    for r in range(rows):
        xhat, _ = norm_parts(pair_ref[r].astype(F32))
        normed = (xhat * gain_ref[...] + shift_ref[...]).astype(BF)
        out_ref[:, r, :] = dot(wbt_ref[...], normed, NT)


def columns_kernel(heads, first, last, col0, len_ref, own_ref, pair_ref, cot_ref, *refs):
    if first:
        bias_in, refs = refs[0], refs[1:]
    else:
        (bias_ref, bacc_in, wacc_in, sacc_in), refs = refs[:4], refs[4:]
    gain_ref, shift_ref, wp_ref, wpt_ref, gb_ref, wot_ref = refs[:6]
    dn_ref, bout_ref, wacc_ref, sacc_ref = refs[6:10]
    refs = refs[10:]
    if first:
        bias_ref, refs = refs[0], refs[1:]
    e_ref, ds_ref, kbd, vaug = refs[:4]
    bacc_ref = refs[4] if last else bout_ref
    step = pl.program_id(0)
    n, channels = bacc_ref.shape[0], wp_ref.shape[0]
    size = channels // heads
    lane = lax.broadcasted_iota(jnp.int32, (1, channels), 1)
    masks = [jnp.where(lane // size == h, 1.0, 0.0).astype(BF) for h in range(heads)]
    length = len_ref[0]

    @pl.when(step == 0)
    def _():
        if first:
            kpos = lax.broadcasted_iota(jnp.int32, (1, n), 1)
            for h in range(heads):
                plane = bias_in[:, h].astype(F32).reshape(n, n)
                bias_ref[:, h * n : (h + 1) * n] = jnp.where(kpos < length, plane.T * LOG2E, DEAD)
            bacc_ref[...] = jnp.zeros_like(bacc_ref)
            wacc_ref[...] = jnp.zeros_like(wacc_ref)
            sacc_ref[...] = jnp.zeros_like(sacc_ref)
        else:
            bacc_ref[...] = bacc_in[...]
            wacc_ref[...] = wacc_in[...]
            sacc_ref[...] = sacc_in[...]
        for h in range(heads):
            vaug[h * n : (h + 1) * n, channels:] = jnp.broadcast_to(masks[h], (n, channels))

    xhat, _ = norm_parts(pair_ref[...].astype(F32).reshape(n, channels))
    normed_f = xhat * gain_ref[...] + shift_ref[...]
    proj = dot(normed_f.astype(BF), wp_ref[...])
    q_f = proj[:, :channels] * (LOG2E / math.sqrt(size))
    k = proj[:, channels : 2 * channels].astype(BF)
    v = proj[:, 2 * channels : 3 * channels].astype(BF)
    gate = jax.nn.sigmoid(proj[:, 3 * channels :] + gb_ref[...])
    for h in range(heads):
        kbd[h * n : (h + 1) * n, :] = k * masks[h]
        vaug[h * n : (h + 1) * n, :channels] = v * masks[h]
    live = lax.broadcasted_iota(jnp.int32, (n, 1), 0) < length
    live = live & (own_ref[0] + col0 + step < length)
    cot = jnp.where(live, cot_ref[...].astype(F32).reshape(n, channels), 0.0).astype(BF)
    d_out = dot(cot, wot_ref[...])

    e_ref[...] = jnp.exp2(dot(q_f.astype(BF), kbd[...], NT) + bias_ref[...]).astype(BF)
    summed = dot(e_ref[...], vaug[...])
    recip = 1.0 / summed[:, channels:]
    att = summed[:, :channels] * recip
    d_att = d_out * gate
    d_gate = d_att * att * (1.0 - gate)
    d_att_b = (d_att * recip).astype(BF)
    d_att_f = d_att_b.astype(F32)
    terms = d_att_f * att
    terms_hi = terms.astype(BF)
    terms_lo = (terms - terms_hi.astype(F32)).astype(BF)
    gi = lax.broadcasted_iota(jnp.int32, (2 * channels, channels), 0) % channels
    gj = lax.broadcasted_iota(jnp.int32, (2 * channels, channels), 1)
    group = jnp.where((gi // size == gj // size) & (gj % size < 2), -1.0, 0.0).astype(BF)
    row_dot = dot(jnp.concatenate([terms_hi, terms_lo], axis=1), group)
    row_hi = row_dot.astype(BF).astype(F32)
    row_lanes = jnp.where(lane % size == 0, row_hi, row_dot - row_hi).astype(BF)
    ds = e_ref[...].astype(F32) * dot(jnp.concatenate([d_att_b, row_lanes], axis=1), vaug[...], NT)
    bacc_ref[...] += ds
    ds_ref[...] = ds.astype(BF)
    d_query = dot(ds_ref[...], kbd[...]) * (1.0 / math.sqrt(size))
    q_t, d_att_t = q_f.T.astype(BF), d_att_f.T.astype(BF)
    dk_t, dv_t = [], []
    for p in range(heads // 2):
        rows = slice(2 * p * size, 2 * (p + 1) * size)
        lanes = slice(2 * p * n, 2 * (p + 1) * n)
        both = dot(q_t[rows], ds_ref[:, lanes])
        dk_t += [both[:size, :n], both[size:, n:]]
        both = dot(d_att_t[rows], e_ref[:, lanes])
        dv_t += [both[:size, :n], both[size:, n:]]
    d_key = (jnp.concatenate(dk_t, axis=0) * LN2).T
    d_value = jnp.concatenate(dv_t, axis=0).T
    d_proj = jnp.concatenate([g.astype(BF) for g in (d_query, d_key, d_value, d_gate)], axis=1)
    dn = dot(d_proj, wpt_ref[...])
    dn_ref[...] = dn.reshape(dn_ref.shape).astype(BF)
    gated = gate * att
    wacc_ref[:, : 4 * channels] += dot(normed_f.T.astype(BF), d_proj)
    wacc_ref[:, 4 * channels :] += dot(gated.T.astype(BF), cot)
    sacc_ref[0] += fold_rows(d_gate)
    sacc_ref[1] += fold_rows(dn * xhat)
    sacc_ref[2] += fold_rows(dn)

    if last:

        @pl.when(step == pl.num_programs(0) - 1)
        def _():
            for h in range(heads):
                plane = bacc_ref[:, h * n : (h + 1) * n].T
                bout_ref[:, h] = plane.reshape(bout_ref.shape[0], -1, n).astype(BF)


def whole(shape):
    return pl.BlockSpec(shape, lambda j: (0,) * len(shape))


def columns_call(first, last, col0, length, own, moved, state, weights, heads):
    src, _, cols, rows, channels = moved.shape
    n = src * rows
    smem = pl.BlockSpec(memory_space=pltpu.SMEM)
    plane = jax.ShapeDtypeStruct((n, heads * n), F32)
    outs = [
        jax.ShapeDtypeStruct((src, cols, rows, channels), BF),
        jax.ShapeDtypeStruct((src, heads, rows, n), BF) if last else plane,
        jax.ShapeDtypeStruct((channels, 5 * channels), F32),
        jax.ShapeDtypeStruct((3, 8, channels), F32),
    ] + ([plane] if first else [])
    cells = (src, None, None, rows, channels)
    return pl.pallas_call(
        functools.partial(columns_kernel, heads, first, last, col0),
        grid=(cols,),
        in_specs=[
            smem,
            smem,
            pl.BlockSpec(cells, lambda j: (0, 0, j, 0, 0)),
            pl.BlockSpec(cells, lambda j: (0, 1, j, 0, 0)),
        ]
        + [whole(a.shape) for a in (*state, *weights)],
        out_specs=[pl.BlockSpec((src, None, rows, channels), lambda j: (0, j, 0, 0))]
        + [whole(o.shape) for o in outs[1:]],
        out_shape=outs,
        scratch_shapes=[
            pltpu.VMEM((n, heads * n), BF),
            pltpu.VMEM((n, heads * n), BF),
            pltpu.VMEM((heads * n, channels), BF),
            pltpu.VMEM((heads * n, 2 * channels), BF),
        ]
        + ([pltpu.VMEM((n, heads * n), F32)] if last else []),
        compiler_params=pltpu.CompilerParams(
            vmem_limit_bytes=56 * MIB, dimension_semantics=("arbitrary",)
        ),
        cost_estimate=pl.CostEstimate(
            flops=cols * heads * n * n * 400, bytes_accessed=cols * n * channels * 6, transcendentals=0
        ),
    )(length, own, moved, moved, *state, *weights)


def side_kernel(pair_ref, parts_ref, gain_ref, shift_ref, sum_ref, stat_ref):
    rows = pair_ref.shape[0]
    heads = parts_ref.shape[1]
    total = jnp.sum(parts_ref[...].astype(F32), axis=0).astype(BF).astype(F32)
    sum_ref[...] = total
    stats = None
    flat = None
    for r in range(rows):
        xhat, _ = norm_parts(pair_ref[r].astype(F32))
        normed = (xhat * gain_ref[...] + shift_ref[...]).astype(BF)
        own = total[:, r, :].astype(BF)
        one = dot(own, jnp.concatenate([normed, xhat.astype(BF)], axis=1))
        stats = one if stats is None else stats + one
        flat = total[:, r, :] if flat is None else flat + total[:, r, :]
    channels = pair_ref.shape[2]
    stat_ref[:, : 2 * channels] = stats
    stat_ref[:, 2 * channels :] = jnp.broadcast_to(
        jnp.sum(flat, axis=1, keepdims=True), (heads, channels)
    )


def norm_back_kernel(counts, pair_ref, sums_ref, gain_ref, wbt_ref, *refs):
    out_ref = refs[-1]
    rows, cols, channels = pair_ref.shape
    pieces = []
    for s in range(refs[0].shape[0]):
        for ref in refs[:-1]:
            pieces.append(ref[s].astype(F32))
    main = jnp.swapaxes(jnp.concatenate(pieces, axis=0), 0, 1).reshape(rows * cols, channels)
    side = dot(sums_ref[...].astype(BF), wbt_ref[...], TN)
    d_normed = (main + side).astype(BF).astype(F32)
    xhat, scale = norm_parts(pair_ref[...].astype(F32).reshape(rows * cols, channels))
    g = d_normed * gain_ref[...]
    dx = scale * (
        g
        - jnp.mean(g, axis=-1, keepdims=True)
        - xhat * jnp.mean(g * xhat, axis=-1, keepdims=True)
    )
    out_ref[...] = dx.reshape(rows, cols, channels).astype(BF)


def body(pair_rep, grad_out, crop_len, ln_gain, ln_bias, w_proj, gate_bias, w_bias, w_out):
    pair, cot = pair_rep[0], grad_out[0]
    rows, n, channels = pair.shape
    heads = w_bias.shape[1]
    src = n // rows
    everywhere = ("dp", "row")
    devices = lax.axis_size("dp") * lax.axis_size("row")
    own = (lax.axis_index("row") * rows).astype(jnp.int32).reshape(1)
    gain, shift = ln_gain.reshape(1, -1), ln_bias.reshape(1, -1)
    wbt = jnp.zeros((8, channels), BF).at[:heads].set(w_bias.T)
    weights = (gain, shift, w_proj, w_proj.T, gate_bias.reshape(1, -1), w_out.T)

    def exchange(a, axis="row"):
        return lax.all_to_all(a, axis, 0, 0)

    half = 8
    logits = pl.pallas_call(
        logits_kernel,
        grid=(rows // half,),
        in_specs=[
            pl.BlockSpec((half, n, channels), lambda j: (j, 0, 0)),
            whole(gain.shape),
            whole(shift.shape),
            whole(wbt.shape),
        ],
        out_specs=pl.BlockSpec((8, half, n), lambda j: (0, j, 0)),
        out_shape=jax.ShapeDtypeStruct((8, rows, n), F32),
    )(pair, gain, shift, wbt)
    bias = exchange(jnp.broadcast_to(logits[None, :heads].astype(BF), (src, heads, rows, n)))

    both = jnp.stack([pair, cot]).reshape(2, rows, src, rows, channels)
    starts = [sum(CHUNKS[:c]) for c in range(len(CHUNKS))]
    moved = [
        exchange(both[:, :, :, s : s + w].transpose(2, 0, 3, 1, 4)) for s, w in zip(starts, CHUNKS)
    ]
    state, back = (bias,), []
    for c, (s, piece) in enumerate(zip(starts, moved)):
        first, last = c == 0, c == len(CHUNKS) - 1
        dn, bacc, wacc, sacc, *rest = columns_call(
            first, last, s, crop_len, own, piece, state, weights, heads
        )
        plane = rest[0] if first else state[0]
        state = (plane, bacc, wacc, sacc)
        if not last:
            back.append(exchange(dn))
    parts = exchange(bacc)
    back.append(exchange(dn))
    share = exchange(wacc.reshape(devices, -1, channels), everywhere)

    sums, stats = pl.pallas_call(
        side_kernel,
        out_shape=[
            jax.ShapeDtypeStruct((heads, rows, n), F32),
            jax.ShapeDtypeStruct((heads, 3 * channels), F32),
        ],
        compiler_params=pltpu.CompilerParams(vmem_limit_bytes=40 * MIB),
    )(pair, parts, gain, shift)

    wide = w_bias.T.astype(F32)
    extra_gain = jnp.sum(wide * stats[:, channels : 2 * channels], axis=0)
    extra_shift = jnp.sum(wide * stats[:, 2 * channels :], axis=0)
    small = jnp.sum(sacc, axis=1) + jnp.stack([jnp.zeros_like(extra_gain), extra_gain, extra_shift])
    small = jnp.concatenate([small, stats[:, :channels]], axis=0)
    reduced = jnp.sum(share, axis=0)
    told = jnp.concatenate([reduced, small], axis=0)
    told = exchange(jnp.broadcast_to(told[None], (devices, *told.shape)), everywhere)
    held = reduced.shape[0]
    w_total = told[:, :held].reshape(channels, 5 * channels) / n
    s_total = jnp.sum(told[:, held:], axis=0) / n

    block = 2
    tile = block * rows
    folded = sums.reshape(heads, rows, n // tile, tile).transpose(2, 0, 1, 3)
    folded = folded.reshape(n // tile, heads, rows * tile)
    folded = jnp.pad(folded, ((0, 0), (0, 8 - heads), (0, 0)))
    cells = pl.BlockSpec((rows, tile, channels), lambda j: (0, j, 0))
    pair_grad = pl.pallas_call(
        functools.partial(norm_back_kernel, CHUNKS),
        grid=(n // tile,),
        in_specs=[
            cells,
            pl.BlockSpec((None, 8, rows * tile), lambda j: (j, 0, 0)),
            whole(gain.shape),
            whole(wbt.shape),
        ]
        + [pl.BlockSpec((block, w, rows, channels), lambda j: (j, 0, 0, 0)) for w in CHUNKS],
        out_specs=cells,
        out_shape=jax.ShapeDtypeStruct(pair.shape, BF),
        compiler_params=pltpu.CompilerParams(vmem_limit_bytes=40 * MIB),
    )(pair, folded, gain, wbt, *back)
    return (
        pair_grad[None],
        w_total[:, : 4 * channels],
        s_total[0],
        s_total[3 : 3 + heads].T,
        w_total[:, 4 * channels :],
        s_total[1],
        s_total[2],
    )


def solution(mesh):
    placed = (
        P("dp", "row", None, None),
        P("dp", "row", None, None),
        P("dp"),
        P(),
        P(),
        P(),
        P(),
        P(),
        P(),
    )
    return jax.shard_map(
        body,
        mesh=mesh,
        in_specs=placed,
        out_specs=(P("dp", "row", None, None), P(), P(), P(), P(), P(), P()),
        check_vma=False,
    )
```

```python
import functools
import math

import jax
import jax.numpy as jnp
from jax import lax
from jax.experimental import pallas as pl
from jax.experimental.pallas import tpu as pltpu
from jax.sharding import PartitionSpec as P

F32, BF = jnp.float32, jnp.bfloat16
EPSILON = 1e-05
LOG2E = 1.4426950408889634
LN2 = 0.6931471805599453
NN = (((1,), (0,)), ((), ()))
NT = (((1,), (1,)), ((), ()))
TN = (((0,), (0,)), ((), ()))
MIB = 2**20
DEAD = -1e30
CHUNKS = (12, 12)
SAFE = 1e28


def dot(a, b, dims=NN):
    return lax.dot_general(a, b, dims, preferred_element_type=F32)


def halves(a):
    high = a.astype(BF)
    return jnp.concatenate([high, (a - high.astype(F32)).astype(BF)], axis=1)


def lane_mean(a):
    channels = a.shape[1]
    a = a if a.dtype == BF else halves(a)
    return dot(a, jnp.full((a.shape[1], channels), 1.0 / channels, BF))


def norm_parts(x):
    centered = x.astype(F32) - lane_mean(x)
    scale = lax.rsqrt(lane_mean(centered * centered) + EPSILON)
    return centered * scale, scale


def fold_rows(a):
    return jnp.sum(a.reshape(a.shape[0] // 8, 8, a.shape[1]), axis=0)


def send_kernel(heads, pair_ref, cot_ref, gain_ref, shift_ref, wbt_ref, *refs):
    outs, plane = refs[:-1], refs[-1]
    rows, n, channels = pair_ref.shape
    thirds = n // channels
    step = pl.program_id(0)

    @pl.when(step == 0)
    def _():
        for r in range(rows):
            xhat, _ = norm_parts(pair_ref[r])
            normed = (xhat * gain_ref[...] + shift_ref[...]).astype(BF)
            logits = dot(wbt_ref[...], normed, NT)
            for h in range(heads):
                for t in range(thirds):
                    piece = logits[h : h + 1, t * channels : (t + 1) * channels]
                    plane[h * thirds + t, r : r + 1, :] = piece

    block = outs[0].shape[0]
    width = block * rows
    span = pl.ds(pl.multiple_of(step * width, width), width)
    for s in range(block):
        outs[0][s, : heads * thirds] = plane[...].astype(BF)
    for a, ref in enumerate((pair_ref, cot_ref)):
        cells = jnp.swapaxes(ref[:, span, :].astype(F32), 0, 1).astype(BF)
        for s in range(block):
            start = s * rows
            for c, (out, w) in enumerate(zip(outs, CHUNKS)):
                skip = a * w + (heads * thirds if c == 0 else 0)
                out[s, skip : skip + w] = cells[start : start + w]
                start += w


def columns_kernel(heads, first, last, col0, len_ref, own_ref, cells_ref, *refs):
    if not first:
        (bias_ref, bacc_in, wacc_in, sacc_in), refs = refs[:4], refs[4:]
    gain_ref, shift_ref, wp_ref, wpt_ref, gb_ref, wot_ref = refs[:6]
    refs = refs[6:]
    out_ref, sacc_ref = refs[:2]
    refs = refs[2:]
    if not last:
        (bacc_ref, wacc_ref), refs = refs[:2], refs[2:]
    if first:
        bias_ref, refs = refs[0], refs[1:]
    e_ref, ds_ref, kbd, vaug, off_ref = refs[:5]
    if last:
        bacc_ref, wacc_ref = refs[5:]
    step, cols = pl.program_id(0), pl.num_programs(0)
    n, channels = bacc_ref.shape[0], wp_ref.shape[0]
    size, thirds, src = channels // heads, n // channels, cells_ref.shape[0]
    slots = heads * thirds
    skip_in = slots if first else 0
    skip_out = slots + 5 if last else 0
    lane = lax.broadcasted_iota(jnp.int32, (1, channels), 1)
    masks = [jnp.where(lane // size == h, 1.0, 0.0).astype(BF) for h in range(heads)]
    length = len_ref[0]

    def begin():
        if first:
            bacc_ref[...] = jnp.zeros_like(bacc_ref)
            wacc_ref[...] = jnp.zeros_like(wacc_ref)
            sacc_ref[...] = jnp.zeros_like(sacc_ref)
        else:
            bacc_ref[...] = bacc_in[...]
            wacc_ref[...] = wacc_in[...]
            sacc_ref[...] = sacc_in[...]

    @pl.when(step == 0)
    def _():
        if first:
            kpos = lax.broadcasted_iota(jnp.int32, (1, n), 1)
            for h in range(heads):
                for t in range(thirds):
                    plane = cells_ref[:, h * thirds + t].astype(F32).reshape(n, channels)
                    bias_ref[t * channels : (t + 1) * channels, h * n : (h + 1) * n] = jnp.where(
                        kpos < length, plane.T * LOG2E, DEAD
                    )
        begin()
        off_ref[...] = jnp.zeros_like(off_ref)
        for h in range(heads):
            vaug[h * n : (h + 1) * n, channels:] = jnp.broadcast_to(masks[h], (n, channels))

    def column(j, shifted):
        xhat, _ = norm_parts(cells_ref[:, skip_in + j].astype(F32).reshape(n, channels).astype(BF))
        normed_f = xhat * gain_ref[...] + shift_ref[...]
        proj = dot(normed_f.astype(BF), wp_ref[...])
        q_f = proj[:, :channels] * (LOG2E / math.sqrt(size))
        k = proj[:, channels : 2 * channels].astype(BF)
        v = proj[:, 2 * channels : 3 * channels].astype(BF)
        gate = jax.nn.sigmoid(proj[:, 3 * channels :] + gb_ref[...])
        for h in range(heads):
            kbd[h * n : (h + 1) * n, :] = k * masks[h]
            vaug[h * n : (h + 1) * n, :channels] = v * masks[h]
        live = lax.broadcasted_iota(jnp.int32, (n, 1), 0) < length
        live = live & (own_ref[0] + col0 + j < length)
        cot = cells_ref[:, skip_in + cols + j].astype(F32).reshape(n, channels)
        cot = jnp.where(live, cot, 0.0).astype(BF)
        d_out = dot(cot, wot_ref[...])

        scores = dot(q_f.astype(BF), kbd[...], NT) + bias_ref[...]
        if shifted:
            for h in range(heads):
                part = scores[:, h * n : (h + 1) * n]
                part = jnp.exp2(part - jnp.max(part, axis=1, keepdims=True))
                e_ref[:, h * n : (h + 1) * n] = part.astype(BF)
        else:
            e_ref[...] = jnp.exp2(scores).astype(BF)
        summed = dot(e_ref[...], vaug[...])
        total = summed[:, channels:]
        if not shifted:
            fits = (total > 1.0 / SAFE) & (total < SAFE)
            off_ref[...] += fold_rows(jnp.where(fits, 0.0, 1.0))
        recip = 1.0 / total
        att = summed[:, :channels] * recip
        d_att = d_out * gate
        d_gate = d_att * att * (1.0 - gate)
        d_att_b = (d_att * recip).astype(BF)
        d_att_f = d_att_b.astype(F32)
        gi = lax.broadcasted_iota(jnp.int32, (2 * channels, channels), 0) % channels
        gj = lax.broadcasted_iota(jnp.int32, (2 * channels, channels), 1)
        group = jnp.where((gi // size == gj // size) & (gj % size < 2), -1.0, 0.0).astype(BF)
        row_dot = dot(halves(d_att_f * att), group)
        row_hi = row_dot.astype(BF).astype(F32)
        row_lanes = jnp.where(lane % size == 0, row_hi, row_dot - row_hi).astype(BF)
        d_probs = dot(jnp.concatenate([d_att_b, row_lanes], axis=1), vaug[...], NT)
        ds = e_ref[...].astype(F32) * d_probs
        bacc_ref[...] += ds
        ds_ref[...] = ds.astype(BF)
        d_query = dot(ds_ref[...], kbd[...]) * (1.0 / math.sqrt(size))
        q_t, d_att_t = q_f.T.astype(BF), d_att_f.T.astype(BF)
        dk_t, dv_t = [], []
        for p in range(heads // 2):
            rows = slice(2 * p * size, 2 * (p + 1) * size)
            lanes = slice(2 * p * n, 2 * (p + 1) * n)
            both = dot(q_t[rows], ds_ref[:, lanes])
            dk_t += [both[:size, :n], both[size:, n:]]
            both = dot(d_att_t[rows], e_ref[:, lanes])
            dv_t += [both[:size, :n], both[size:, n:]]
        d_key = (jnp.concatenate(dk_t, axis=0) * LN2).T
        d_value = jnp.concatenate(dv_t, axis=0).T
        d_proj = jnp.concatenate([g.astype(BF) for g in (d_query, d_key, d_value, d_gate)], axis=1)
        dn = dot(d_proj, wpt_ref[...])
        out_ref[:, skip_out + j] = dn.reshape(src, n // src, channels).astype(BF)
        gated = gate * att
        wacc_ref[:, : 4 * channels] += dot(normed_f.T.astype(BF), d_proj)
        wacc_ref[:, 4 * channels :] += dot(gated.T.astype(BF), cot)
        sacc_ref[0] += fold_rows(d_gate)
        sacc_ref[1] += fold_rows(dn * xhat)
        sacc_ref[2] += fold_rows(dn)

    column(step, False)

    @pl.when(step == cols - 1)
    def _():
        @pl.when(jnp.max(off_ref[...]) > 0.0)
        def _():
            begin()

            @pl.loop(0, cols)
            def _(j):
                column(j, True)

        if last:
            for h in range(heads):
                for t in range(thirds):
                    plane = bacc_ref[t * channels : (t + 1) * channels, h * n : (h + 1) * n].T
                    out_ref[:, h * thirds + t] = plane.reshape(src, n // src, channels).astype(BF)
            for w in range(5):
                part = wacc_ref[:, w * channels : (w + 1) * channels].reshape(src, -1, channels)
                terms = []
                for _ in range(3):
                    terms.append(part.astype(BF).astype(F32))
                    part = part - terms[-1]
                out_ref[:, slots + w] = jnp.concatenate(terms, axis=1).astype(BF)


def whole(shape):
    return pl.BlockSpec(shape, lambda j: (0,) * len(shape))


def columns_call(first, last, col0, cols, length, own, moved, state, weights, heads):
    src, _, rows, channels = moved.shape
    n = src * rows
    slots = heads * n // channels
    smem = pl.BlockSpec(memory_space=pltpu.SMEM)
    plane = jax.ShapeDtypeStruct((n, heads * n), F32)
    wide = jax.ShapeDtypeStruct((channels, 5 * channels), F32)
    outs = [
        jax.ShapeDtypeStruct((src, cols + (slots + 5 if last else 0), rows, channels), BF),
        jax.ShapeDtypeStruct((3, 8, channels), F32),
    ]
    outs += ([] if last else [plane, wide]) + ([plane] if first else [])
    inputs = (moved, *state, *weights)
    return pl.pallas_call(
        functools.partial(columns_kernel, heads, first, last, col0),
        grid=(cols,),
        in_specs=[smem, smem] + [whole(a.shape) for a in inputs],
        out_specs=[whole(o.shape) for o in outs],
        out_shape=outs,
        scratch_shapes=[
            pltpu.VMEM((n, heads * n), BF),
            pltpu.VMEM((n, heads * n), BF),
            pltpu.VMEM((heads * n, channels), BF),
            pltpu.VMEM((heads * n, 2 * channels), BF),
            pltpu.VMEM((8, channels), F32),
        ]
        + ([pltpu.VMEM(o.shape, F32) for o in (plane, wide)] if last else []),
        compiler_params=pltpu.CompilerParams(
            vmem_limit_bytes=56 * MIB, dimension_semantics=("arbitrary",)
        ),
        cost_estimate=pl.CostEstimate(
            flops=cols * 4 * 10**9, bytes_accessed=cols * n * channels * 6, transcendentals=0
        ),
    )(length, own, *inputs)


def side_kernel(heads, pair_ref, parts_ref, gain_ref, shift_ref, wbt_ref, sacc_ref, sum_ref, share_ref):
    rows, n, channels = pair_ref.shape
    thirds = n // channels
    slots = heads * thirds
    total = jnp.sum(parts_ref[:, :slots].astype(F32), axis=0).astype(BF).astype(F32)
    for h in range(heads):
        for t in range(thirds):
            sum_ref[h, :, t * channels : (t + 1) * channels] = total[h * thirds + t]
    for w in range(5):
        part = jnp.sum(parts_ref[:, slots + w].astype(F32), axis=0)
        share_ref[w] = part[:8] + part[8:16] + part[16:24]
    stats = jnp.zeros((8, 2 * channels), F32)
    flat = jnp.zeros((heads, n), F32)
    none = jnp.zeros((8 - heads, n), F32)
    for r in range(rows):
        xhat, _ = norm_parts(pair_ref[r])
        normed = (xhat * gain_ref[...] + shift_ref[...]).astype(BF)
        own = sum_ref[:, r, :]
        flat = flat + own
        padded = jnp.concatenate([own, none], axis=0).astype(BF)
        stats = stats + dot(padded, jnp.concatenate([normed, xhat.astype(BF)], axis=1))
    wide = wbt_ref[...].astype(F32)
    share_ref[5, 0:1, :] = jnp.sum(sacc_ref[0], axis=0, keepdims=True)
    gain_part = wide * stats[:, channels:]
    share_ref[5, 1:2, :] = jnp.sum(sacc_ref[1] + gain_part, axis=0, keepdims=True)
    shift_part = wide[:heads] * jnp.sum(flat, axis=1, keepdims=True)
    shift_all = jnp.sum(sacc_ref[2], axis=0, keepdims=True)
    share_ref[5, 2:3, :] = shift_all + jnp.sum(shift_part, axis=0, keepdims=True)
    share_ref[5, 3 : 3 + heads, :] = stats[:heads, :channels]
    share_ref[5, 3 + heads :, :] = jnp.zeros((5 - heads, channels), F32)


def norm_back_kernel(pair_ref, sums_ref, gain_ref, wbt_ref, *refs):
    parts, out_ref, side_ref = refs[:-2], refs[-2], refs[-1]
    rows, cols, channels = pair_ref.shape
    heads, n = sums_ref.shape[0], sums_ref.shape[2]
    step = pl.program_id(0)

    @pl.when(step == 0)
    def _():
        none = jnp.zeros((8 - heads, n), F32)
        for r in range(rows):
            own = jnp.concatenate([sums_ref[:, r, :], none], axis=0)
            side_ref[r] = dot(own.T.astype(BF), wbt_ref[...])

    pieces = []
    for s in range(cols // rows):
        for c, (ref, w) in enumerate(zip(parts, CHUNKS)):
            pieces.append(ref[s, ref.shape[1] - w :].astype(F32))
    main = jnp.swapaxes(jnp.concatenate(pieces, axis=0), 0, 1)
    side = side_ref[:, pl.ds(pl.multiple_of(step * cols, cols), cols), :]
    d_normed = (main + side).astype(BF).astype(F32).reshape(rows * cols, channels)
    cells = pair_ref[...].astype(F32).reshape(rows * cols, channels).astype(BF)
    xhat, scale = norm_parts(cells)
    g = d_normed * gain_ref[...]
    dx = scale * (g - lane_mean(g) - xhat * lane_mean(g * xhat))
    out_ref[...] = dx.reshape(rows, cols, channels).astype(BF)


def final_kernel(heads, told_ref, proj_ref, gate_ref, biasw_ref, outw_ref, gain_ref, shift_ref):
    channels = told_ref.shape[-1]
    scale = 1.0 / (told_ref.shape[0] * 24)
    for w in range(5):
        part = told_ref[:, w].reshape(channels, channels) * scale
        if w < 4:
            proj_ref[:, w * channels : (w + 1) * channels] = part
        else:
            outw_ref[...] = part
    small = jnp.sum(told_ref[:, 5], axis=0) * scale
    gate_ref[...] = small[0:1]
    gain_ref[...] = small[1:2]
    shift_ref[...] = small[2:3]
    biasw_ref[...] = small.T[:, 3 : 3 + heads]


def body(pair_rep, grad_out, crop_len, ln_gain, ln_bias, w_proj, gate_bias, w_bias, w_out):
    pair, cot = pair_rep[0], grad_out[0]
    rows, n, channels = pair.shape
    heads = w_bias.shape[1]
    src = n // rows
    slots = heads * n // channels
    own = (lax.axis_index("row") * rows).astype(jnp.int32).reshape(1)
    gain, shift = ln_gain.reshape(1, -1), ln_bias.reshape(1, -1)
    wbt = jnp.zeros((8, channels), BF).at[:heads].set(w_bias.T)
    weights = (gain, shift, w_proj, w_proj.T, gate_bias.reshape(1, -1), w_out.T)

    def exchange(a, axis="row"):
        return lax.all_to_all(a, axis, 0, 0)

    def tell(a, axis):
        return exchange(jnp.broadcast_to(a[None], (lax.axis_size(axis), *a.shape)), axis)

    block = 2
    tile = block * rows
    counts = [2 * w + (slots if c == 0 else 0) for c, w in enumerate(CHUNKS)]
    sent = pl.pallas_call(
        functools.partial(send_kernel, heads),
        grid=(src // block,),
        in_specs=[whole(a.shape) for a in (pair, cot, gain, shift, wbt)],
        out_specs=[pl.BlockSpec((block, w, rows, channels), lambda j: (j, 0, 0, 0)) for w in counts],
        out_shape=[jax.ShapeDtypeStruct((src, w, rows, channels), BF) for w in counts],
        scratch_shapes=[pltpu.VMEM((slots, rows, channels), F32)],
        compiler_params=pltpu.CompilerParams(vmem_limit_bytes=40 * MIB),
    )(pair, cot, gain, shift, wbt)
    moved = [exchange(a) for a in sent]
    starts = [sum(CHUNKS[:c]) for c in range(len(CHUNKS))]
    state, back = (), []
    for c, (start, width, piece) in enumerate(zip(starts, CHUNKS, moved)):
        first, last = c == 0, c == len(CHUNKS) - 1
        out, sacc, *rest = columns_call(
            first, last, start, width, crop_len, own, piece, state, weights, heads
        )
        if not last:
            plane = rest[2] if first else state[0]
            state = (plane, rest[0], rest[1], sacc)
            if back:
                out, back = lax.optimization_barrier((out, back))
            back.append(exchange(out))
    out, back = lax.optimization_barrier((out, back))
    bundle = exchange(out)
    back.append(bundle)

    sums, share = pl.pallas_call(
        functools.partial(side_kernel, heads),
        grid=(1,),
        in_specs=[
            whole(pair.shape),
            pl.BlockSpec((src, slots + 5, rows, channels), lambda j: (0, 0, 0, 0)),
        ]
        + [whole(a.shape) for a in (gain, shift, wbt, sacc)],
        out_specs=[whole((heads, rows, n)), whole((6, 8, channels))],
        out_shape=[
            jax.ShapeDtypeStruct((heads, rows, n), F32),
            jax.ShapeDtypeStruct((6, 8, channels), F32),
        ],
        compiler_params=pltpu.CompilerParams(vmem_limit_bytes=40 * MIB),
    )(pair, bundle, gain, shift, wbt, sacc)
    share = jnp.sum(tell(share, "dp"), axis=0)
    told = tell(share, "row")

    cells = pl.BlockSpec((rows, tile, channels), lambda j: (0, j, 0))
    pair_grad = pl.pallas_call(
        norm_back_kernel,
        grid=(n // tile,),
        in_specs=[cells] + [whole(a.shape) for a in (sums, gain, wbt)]
        + [pl.BlockSpec((block, *a.shape[1:]), lambda j: (j, 0, 0, 0)) for a in back],
        out_specs=cells,
        out_shape=jax.ShapeDtypeStruct(pair.shape, BF),
        scratch_shapes=[pltpu.VMEM((rows, n, channels), F32)],
        compiler_params=pltpu.CompilerParams(vmem_limit_bytes=40 * MIB),
        cost_estimate=pl.CostEstimate(flops=10**10, bytes_accessed=3 * pair.size, transcendentals=0),
    )(pair, sums, gain, wbt, *back)
    proj, gate, biasw, outw, gain_sum, shift_sum = pl.pallas_call(
        functools.partial(final_kernel, heads),
        out_shape=[
            jax.ShapeDtypeStruct(s, F32)
            for s in (
                w_proj.shape,
                (1, channels),
                w_bias.shape,
                w_out.shape,
                (1, channels),
                (1, channels),
            )
        ],
    )(told)
    return (
        pair_grad[None],
        proj,
        gate.reshape(-1),
        biasw,
        outw,
        gain_sum.reshape(-1),
        shift_sum.reshape(-1),
    )


def solution(mesh):
    placed = (
        P("dp", "row", None, None),
        P("dp", "row", None, None),
        P("dp"),
        P(),
        P(),
        P(),
        P(),
        P(),
        P(),
    )
    return jax.shard_map(
        body,
        mesh=mesh,
        in_specs=placed,
        out_specs=(P("dp", "row", None, None), P(), P(), P(), P(), P(), P()),
        check_vma=False,
    )
```

```python
import functools
import math

import jax
import jax.numpy as jnp
from jax import lax
from jax.experimental import pallas as pl
from jax.experimental.pallas import tpu as pltpu
from jax.sharding import PartitionSpec as P

F32, BF = jnp.float32, jnp.bfloat16
EPSILON = 1e-05
LOG2E = 1.4426950408889634
LN2 = 0.6931471805599453
NN = (((1,), (0,)), ((), ()))
NT = (((1,), (1,)), ((), ()))
TN = (((0,), (0,)), ((), ()))
MIB = 2**20
DEAD = -1e30
CHUNKS = (6, 9, 9)
SAFE = 1e28
PAIR, STAGES, LAG = 3, 6, 2


def dot(a, b, dims=NN):
    return lax.dot_general(a, b, dims, preferred_element_type=F32)


def halves(a):
    high = a.astype(BF)
    return jnp.concatenate([high, (a - high.astype(F32)).astype(BF)], axis=1)


def lane_mean(a):
    channels = a.shape[1]
    a = a if a.dtype == BF else halves(a)
    return dot(a, jnp.full((a.shape[1], channels), 1.0 / channels, BF))


def norm_parts(x):
    centered = x.astype(F32) - lane_mean(x)
    scale = lax.rsqrt(lane_mean(centered * centered) + EPSILON)
    return centered * scale, scale


def fold_rows(a):
    return jnp.sum(a.reshape(a.shape[0] // 8, 8, a.shape[1]), axis=0)


def logits_kernel(heads, pair_ref, gain_ref, shift_ref, wbt_ref, out_ref):
    rows, n, channels = pair_ref.shape
    xhat, _ = norm_parts(pair_ref[...].astype(F32).reshape(rows * n, channels).astype(BF))
    normed = (xhat * gain_ref[...] + shift_ref[...]).astype(BF)
    logits = dot(wbt_ref[...], normed, NT)
    for r in range(rows):
        for h in range(heads):
            for t in range(n // channels):
                start = r * n + t * channels
                piece = logits[h : h + 1, start : start + channels]
                out_ref[h * (n // channels) + t, r : r + 1, :] = piece


def send_kernel(start, count, pair_ref, cot_ref, *refs):
    out = refs[-1]
    block, rows = out.shape[0], pair_ref.shape[0]
    skip = out.shape[1] - 2 * count
    if skip:
        for s in range(block):
            out[s, :skip] = refs[0][...].astype(BF)
    for a, ref in enumerate((pair_ref, cot_ref)):
        cells = jnp.swapaxes(ref[...].astype(F32), 0, 1)
        for s in range(block):
            first = s * rows + start
            out[s, skip + a * count : skip + (a + 1) * count] = cells[first : first + count].astype(BF)


def columns_kernel(heads, first, last, col0, len_ref, own_ref, cells_ref, *refs):
    if not first:
        (bias_ref, bacc_in, wacc_in, sacc_in), refs = refs[:4], refs[4:]
    if not first and not last:
        early_ref, refs = refs[0], refs[1:]
    gain_ref, shift_ref, wp_ref, wpt_ref, gb_ref, wot_ref = refs[:6]
    refs = refs[6:]
    out_ref, sacc_ref = refs[:2]
    refs = refs[2:]
    if not last:
        (bacc_ref, wacc_ref), refs = refs[:2], refs[2:]
    if first:
        bias_ref, refs = refs[0], refs[1:]
    e_all, ds_all, kbd_all, vaug_all, off_ref = refs[:5]
    if last:
        bacc_ref, wacc_ref = refs[5:]
    step, cols = pl.program_id(0), pl.num_programs(0) * PAIR
    n, channels = bacc_ref.shape[0], wp_ref.shape[0]
    size, thirds, src = channels // heads, n // channels, cells_ref.shape[0]
    slots = heads * thirds
    skip_in = slots if first else 0
    skip_out = slots + 5 if last else out_ref.shape[1] - cols
    lane = lax.broadcasted_iota(jnp.int32, (1, channels), 1)
    masks = [jnp.where(lane // size == h, 1.0, 0.0).astype(BF) for h in range(heads)]
    length = len_ref[0]

    def begin():
        if first:
            bacc_ref[...] = jnp.zeros_like(bacc_ref)
            wacc_ref[...] = jnp.zeros_like(wacc_ref)
            sacc_ref[...] = jnp.zeros_like(sacc_ref)
        else:
            bacc_ref[...] = bacc_in[...]
            wacc_ref[...] = wacc_in[...]
            sacc_ref[...] = sacc_in[...]

    @pl.when(step == 0)
    def _():
        if first:
            kpos = lax.broadcasted_iota(jnp.int32, (1, n), 1)
            for h in range(heads):
                for t in range(thirds):
                    plane = cells_ref[:, h * thirds + t].astype(F32).reshape(n, channels)
                    bias_ref[t * channels : (t + 1) * channels, h * n : (h + 1) * n] = jnp.where(
                        kpos < length, plane.T * LOG2E, DEAD
                    )
        begin()
        if not first and not last:
            out_ref[:, :skip_out] = early_ref[...]
        off_ref[...] = jnp.zeros_like(off_ref)
        for h in range(heads):
            for u in range(PAIR):
                vaug_all[u, h * n : (h + 1) * n, channels:] = jnp.broadcast_to(masks[h], (n, channels))

    def column(j, shifted, slot):
        e_ref, ds_ref, kbd, vaug = e_all.at[slot], ds_all.at[slot], kbd_all.at[slot], vaug_all.at[slot]
        xhat, _ = norm_parts(cells_ref[:, skip_in + j].astype(F32).reshape(n, channels).astype(BF))
        normed_f = xhat * gain_ref[...] + shift_ref[...]
        proj = dot(normed_f.astype(BF), wp_ref[...])
        q_f = proj[:, :channels] * (LOG2E / math.sqrt(size))
        k = proj[:, channels : 2 * channels].astype(BF)
        v = proj[:, 2 * channels : 3 * channels].astype(BF)
        gate = jax.nn.sigmoid(proj[:, 3 * channels :] + gb_ref[...])
        for h in range(heads):
            kbd[h * n : (h + 1) * n, :] = k * masks[h]
            vaug[h * n : (h + 1) * n, :channels] = v * masks[h]
        live = lax.broadcasted_iota(jnp.int32, (n, 1), 0) < length
        live = live & (own_ref[0] + col0 + j < length)
        cot = cells_ref[:, skip_in + cols + j].astype(F32).reshape(n, channels)
        cot = jnp.where(live, cot, 0.0).astype(BF)
        d_out = dot(cot, wot_ref[...])

        yield
        scores = dot(q_f.astype(BF), kbd[...], NT) + bias_ref[...]
        if shifted:
            for h in range(heads):
                part = scores[:, h * n : (h + 1) * n]
                part = jnp.exp2(part - jnp.max(part, axis=1, keepdims=True))
                e_ref[:, h * n : (h + 1) * n] = part.astype(BF)
        else:
            e_ref[...] = jnp.exp2(scores).astype(BF)
        yield
        summed = dot(e_ref[...], vaug[...])
        total = summed[:, channels:]
        if not shifted:
            fits = (total > 1.0 / SAFE) & (total < SAFE)
            off_ref[...] += fold_rows(jnp.where(fits, 0.0, 1.0))
        recip = 1.0 / total
        att = summed[:, :channels] * recip
        d_att = d_out * gate
        d_gate = d_att * att * (1.0 - gate)
        d_att_b = (d_att * recip).astype(BF)
        d_att_f = d_att_b.astype(F32)
        gi = lax.broadcasted_iota(jnp.int32, (2 * channels, channels), 0) % channels
        gj = lax.broadcasted_iota(jnp.int32, (2 * channels, channels), 1)
        group = jnp.where((gi // size == gj // size) & (gj % size < 2), -1.0, 0.0).astype(BF)
        row_dot = dot(halves(d_att_f * att), group)
        row_hi = row_dot.astype(BF).astype(F32)
        row_lanes = jnp.where(lane % size == 0, row_hi, row_dot - row_hi).astype(BF)
        yield
        d_probs = dot(jnp.concatenate([d_att_b, row_lanes], axis=1), vaug[...], NT)
        ds = e_ref[...].astype(F32) * d_probs
        bacc_ref[...] += ds
        ds_ref[...] = ds.astype(BF)
        yield
        d_query = dot(ds_ref[...], kbd[...]) * (1.0 / math.sqrt(size))
        q_t, d_att_t = q_f.T.astype(BF), d_att_f.T.astype(BF)
        dk_t, dv_t = [], []
        for p in range(heads // 2):
            rows = slice(2 * p * size, 2 * (p + 1) * size)
            lanes = slice(2 * p * n, 2 * (p + 1) * n)
            both = dot(q_t[rows], ds_ref[:, lanes])
            dk_t += [both[:size, :n], both[size:, n:]]
            both = dot(d_att_t[rows], e_ref[:, lanes])
            dv_t += [both[:size, :n], both[size:, n:]]
        d_key = (jnp.concatenate(dk_t, axis=0) * LN2).T
        d_value = jnp.concatenate(dv_t, axis=0).T
        yield
        d_proj = jnp.concatenate([g.astype(BF) for g in (d_query, d_key, d_value, d_gate)], axis=1)
        dn = dot(d_proj, wpt_ref[...])
        out_ref[:, skip_out + j] = dn.reshape(src, n // src, channels).astype(BF)
        gated = gate * att
        wacc_ref[:, : 4 * channels] += dot(normed_f.T.astype(BF), d_proj)
        wacc_ref[:, 4 * channels :] += dot(gated.T.astype(BF), cot)
        sacc_ref[0] += fold_rows(d_gate)
        sacc_ref[1] += fold_rows(dn * xhat)
        sacc_ref[2] += fold_rows(dn)

    def run(first_col, shifted):
        ahead = [column(first_col + u, shifted, u) for u in range(PAIR)]
        for turn in range(STAGES + LAG * (PAIR - 1)):
            for u in range(PAIR):
                if LAG * u <= turn < STAGES + LAG * u:
                    next(ahead[u], None)

    run(step * PAIR, False)

    @pl.when(step == pl.num_programs(0) - 1)
    def _():
        @pl.when(jnp.max(off_ref[...]) > 0.0)
        def _():
            begin()

            @pl.loop(0, cols // PAIR)
            def _(j):
                run(j * PAIR, True)

        if last:
            for h in range(heads):
                for t in range(thirds):
                    plane = bacc_ref[t * channels : (t + 1) * channels, h * n : (h + 1) * n].T
                    out_ref[:, h * thirds + t] = plane.reshape(src, n // src, channels).astype(BF)
            for w in range(5):
                part = wacc_ref[:, w * channels : (w + 1) * channels].reshape(src, -1, channels)
                terms = []
                for _ in range(3):
                    terms.append(part.astype(BF).astype(F32))
                    part = part - terms[-1]
                out_ref[:, slots + w] = jnp.concatenate(terms, axis=1).astype(BF)


def whole(shape):
    return pl.BlockSpec(shape, lambda j: (0,) * len(shape))


def columns_call(first, last, col0, cols, length, own, moved, state, weights, heads):
    src, _, rows, channels = moved.shape
    n = src * rows
    slots = heads * n // channels
    smem = pl.BlockSpec(memory_space=pltpu.SMEM)
    plane = jax.ShapeDtypeStruct((n, heads * n), F32)
    wide = jax.ShapeDtypeStruct((channels, 5 * channels), F32)
    outs = [
        jax.ShapeDtypeStruct((src, cols + (slots + 5 if last else col0), rows, channels), BF),
        jax.ShapeDtypeStruct((3, 8, channels), F32),
    ]
    outs += ([] if last else [plane, wide]) + ([plane] if first else [])
    inputs = (moved, *state, *weights)
    return pl.pallas_call(
        functools.partial(columns_kernel, heads, first, last, col0),
        grid=(cols // PAIR,),
        in_specs=[smem, smem] + [whole(a.shape) for a in inputs],
        out_specs=[whole(o.shape) for o in outs],
        out_shape=outs,
        scratch_shapes=[
            pltpu.VMEM((PAIR, n, heads * n), BF),
            pltpu.VMEM((PAIR, n, heads * n), BF),
            pltpu.VMEM((PAIR, heads * n, channels), BF),
            pltpu.VMEM((PAIR, heads * n, 2 * channels), BF),
            pltpu.VMEM((8, channels), F32),
        ]
        + ([pltpu.VMEM(o.shape, F32) for o in (plane, wide)] if last else []),
        compiler_params=pltpu.CompilerParams(
            vmem_limit_bytes=56 * MIB, dimension_semantics=("arbitrary",)
        ),
        cost_estimate=pl.CostEstimate(
            flops=cols * 4 * 10**9, bytes_accessed=cols * n * channels * 6, transcendentals=0
        ),
    )(length, own, *inputs)


def side_kernel(heads, pair_ref, parts_ref, gain_ref, shift_ref, wbt_ref, sacc_ref, sum_ref, share_ref):
    rows, n, channels = pair_ref.shape
    thirds = n // channels
    slots = heads * thirds
    total = jnp.sum(parts_ref[:, :slots].astype(F32), axis=0).astype(BF).astype(F32)
    for h in range(heads):
        for t in range(thirds):
            sum_ref[h, :, t * channels : (t + 1) * channels] = total[h * thirds + t]
    for w in range(5):
        part = jnp.sum(parts_ref[:, slots + w].astype(F32), axis=0)
        share_ref[w] = part[:8] + part[8:16] + part[16:24]
    stats = jnp.zeros((8, 2 * channels), F32)
    flat = jnp.zeros((heads, n), F32)
    none = jnp.zeros((8 - heads, n), F32)
    for r in range(rows):
        xhat, _ = norm_parts(pair_ref[r])
        normed = (xhat * gain_ref[...] + shift_ref[...]).astype(BF)
        own = sum_ref[:, r, :]
        flat = flat + own
        padded = jnp.concatenate([own, none], axis=0).astype(BF)
        stats = stats + dot(padded, jnp.concatenate([normed, xhat.astype(BF)], axis=1))
    wide = wbt_ref[...].astype(F32)
    share_ref[5, 0:1, :] = jnp.sum(sacc_ref[0], axis=0, keepdims=True)
    gain_part = wide * stats[:, channels:]
    share_ref[5, 1:2, :] = jnp.sum(sacc_ref[1] + gain_part, axis=0, keepdims=True)
    shift_part = wide[:heads] * jnp.sum(flat, axis=1, keepdims=True)
    shift_all = jnp.sum(sacc_ref[2], axis=0, keepdims=True)
    share_ref[5, 2:3, :] = shift_all + jnp.sum(shift_part, axis=0, keepdims=True)
    share_ref[5, 3 : 3 + heads, :] = stats[:heads, :channels]
    share_ref[5, 3 + heads :, :] = jnp.zeros((5 - heads, channels), F32)


def norm_back_kernel(pair_ref, sums_ref, gain_ref, wbt_ref, *refs):
    parts, out_ref, side_ref = refs[:-2], refs[-2], refs[-1]
    rows, cols, channels = pair_ref.shape
    heads, n = sums_ref.shape[0], sums_ref.shape[2]
    step = pl.program_id(0)

    @pl.when(step == 0)
    def _():
        none = jnp.zeros((8 - heads, n), F32)
        for r in range(rows):
            own = jnp.concatenate([sums_ref[:, r, :], none], axis=0)
            side_ref[r] = dot(own.T.astype(BF), wbt_ref[...])

    pieces = []
    for s in range(cols // rows):
        for ref, w in zip(parts, (sum(CHUNKS[:-1]), CHUNKS[-1])):
            pieces.append(ref[s, ref.shape[1] - w :].astype(F32))
    main = jnp.swapaxes(jnp.concatenate(pieces, axis=0), 0, 1)
    side = side_ref[:, pl.ds(pl.multiple_of(step * cols, cols), cols), :]
    d_normed = (main + side).astype(BF).astype(F32).reshape(rows * cols, channels)
    cells = pair_ref[...].astype(F32).reshape(rows * cols, channels).astype(BF)
    xhat, scale = norm_parts(cells)
    g = d_normed * gain_ref[...]
    dx = scale * (g - lane_mean(g) - xhat * lane_mean(g * xhat))
    out_ref[...] = dx.reshape(rows, cols, channels).astype(BF)


def final_kernel(heads, size, told_ref, proj_ref, gate_ref, biasw_ref, outw_ref, gain_ref, shift_ref):
    channels = told_ref.shape[-1]
    scale = 1.0 / size
    for w in range(5):
        part = told_ref[:, w].reshape(channels, channels) * scale
        if w < 4:
            proj_ref[:, w * channels : (w + 1) * channels] = part
        else:
            outw_ref[...] = part
    small = jnp.sum(told_ref[:, 5], axis=0) * scale
    gate_ref[...] = small[0:1]
    gain_ref[...] = small[1:2]
    shift_ref[...] = small[2:3]
    biasw_ref[...] = small[3 : 3 + heads]


def body(pair_rep, grad_out, crop_len, ln_gain, ln_bias, w_proj, gate_bias, w_bias, w_out):
    pair, cot = pair_rep[0], grad_out[0]
    rows, n, channels = pair.shape
    heads = w_bias.shape[1]
    src = n // rows
    slots = heads * n // channels
    own = (lax.axis_index("row") * rows).astype(jnp.int32).reshape(1)
    gain, shift = ln_gain.reshape(1, -1), ln_bias.reshape(1, -1)
    wbt = jnp.zeros((8, channels), BF).at[:heads].set(w_bias.T)
    weights = (gain, shift, w_proj, w_proj.T, gate_bias.reshape(1, -1), w_out.T)

    def exchange(a, axis="row"):
        return lax.all_to_all(a, axis, 0, 0)

    def tell(a, axis):
        return exchange(jnp.broadcast_to(a[None], (lax.axis_size(axis), *a.shape)), axis)

    block = 2
    tile = block * rows
    group = 8
    plane = pl.pallas_call(
        functools.partial(logits_kernel, heads),
        grid=(rows // group,),
        in_specs=[pl.BlockSpec((group, n, channels), lambda j: (j, 0, 0))]
        + [whole(a.shape) for a in (gain, shift, wbt)],
        out_specs=pl.BlockSpec((slots, group, channels), lambda j: (0, j, 0)),
        out_shape=jax.ShapeDtypeStruct((slots, rows, channels), F32),
        compiler_params=pltpu.CompilerParams(vmem_limit_bytes=60 * MIB),
    )(pair, gain, shift, wbt)
    cells = pl.BlockSpec((rows, tile, channels), lambda j: (0, j, 0))

    def send(start, count, extra):
        deep = 2 * count + sum(a.shape[0] for a in extra)
        return pl.pallas_call(
            functools.partial(send_kernel, start, count),
            grid=(src // block,),
            in_specs=[cells, cells] + [whole(a.shape) for a in extra],
            out_specs=pl.BlockSpec((block, deep, rows, channels), lambda j: (j, 0, 0, 0)),
            out_shape=jax.ShapeDtypeStruct((src, deep, rows, channels), BF),
            compiler_params=pltpu.CompilerParams(vmem_limit_bytes=60 * MIB),
            cost_estimate=pl.CostEstimate(
                flops=5 * 10**9, bytes_accessed=3 * pair.size, transcendentals=0
            ),
        )(pair, cot, *extra)

    starts = [sum(CHUNKS[:c]) for c in range(len(CHUNKS))]
    sent = [send(a, w, (plane,) if a == 0 else ()) for a, w in zip(starts, CHUNKS)]
    moved = [exchange(a) for a in sent]
    state, back = (), []
    for c, (start, width, piece) in enumerate(zip(starts, CHUNKS, moved)):
        first, last = c == 0, c == len(CHUNKS) - 1
        out, sacc, *rest = columns_call(
            first, last, start, width, crop_len, own, piece, state, weights, heads
        )
        if not last:
            plane = rest[2] if first else state[0]
            state = (plane, rest[0], rest[1], sacc)
            if c == len(CHUNKS) - 2:
                early = exchange(out)
            else:
                state += (out,)
    out, early = lax.optimization_barrier((out, early))
    bundle = exchange(out)
    back = (early, bundle)

    sums, share = pl.pallas_call(
        functools.partial(side_kernel, heads),
        grid=(1,),
        in_specs=[
            whole(pair.shape),
            pl.BlockSpec((src, slots + 5, rows, channels), lambda j: (0, 0, 0, 0)),
        ]
        + [whole(a.shape) for a in (gain, shift, wbt, sacc)],
        out_specs=[whole((heads, rows, n)), whole((6, 8, channels))],
        out_shape=[
            jax.ShapeDtypeStruct((heads, rows, n), F32),
            jax.ShapeDtypeStruct((6, 8, channels), F32),
        ],
        compiler_params=pltpu.CompilerParams(vmem_limit_bytes=40 * MIB),
    )(pair, bundle, gain, shift, wbt, sacc)
    share = jnp.sum(tell(share, "dp"), axis=0)
    told = tell(share, "row")

    pair_grad = pl.pallas_call(
        norm_back_kernel,
        grid=(n // tile,),
        in_specs=[cells] + [whole(a.shape) for a in (sums, gain, wbt)]
        + [pl.BlockSpec((block, *a.shape[1:]), lambda j: (j, 0, 0, 0)) for a in back],
        out_specs=cells,
        out_shape=jax.ShapeDtypeStruct(pair.shape, BF),
        scratch_shapes=[pltpu.VMEM((rows, n, channels), F32)],
        compiler_params=pltpu.CompilerParams(vmem_limit_bytes=40 * MIB),
        cost_estimate=pl.CostEstimate(flops=10**10, bytes_accessed=3 * pair.size, transcendentals=0),
    )(pair, sums, gain, wbt, *back)
    proj, gate, biasw, outw, gain_sum, shift_sum = pl.pallas_call(
        functools.partial(final_kernel, heads, n),
        out_shape=[
            jax.ShapeDtypeStruct(s, F32)
            for s in (
                w_proj.shape,
                (1, channels),
                (heads, channels),
                w_out.shape,
                (1, channels),
                (1, channels),
            )
        ],
    )(told)
    return (
        pair_grad[None],
        proj,
        gate.reshape(-1),
        biasw.T,
        outw,
        gain_sum.reshape(-1),
        shift_sum.reshape(-1),
    )


def solution(mesh):
    placed = (
        P("dp", "row", None, None),
        P("dp", "row", None, None),
        P("dp"),
        P(),
        P(),
        P(),
        P(),
        P(),
        P(),
    )
    return jax.shard_map(
        body,
        mesh=mesh,
        in_specs=placed,
        out_specs=(P("dp", "row", None, None), P(), P(), P(), P(), P(), P()),
        check_vma=False,
    )
```

```python
import functools
import math

import jax
import jax.numpy as jnp
from jax import lax
from jax.experimental import pallas as pl
from jax.experimental.pallas import tpu as pltpu
from jax.sharding import PartitionSpec as P

F32, BF = jnp.float32, jnp.bfloat16
EPSILON = 1e-05
LOG2E = 1.4426950408889634
LN2 = 0.6931471805599453
NN = (((1,), (0,)), ((), ()))
NT = (((1,), (1,)), ((), ()))
TN = (((0,), (0,)), ((), ()))
MIB = 2**20
DEAD = -1e30
CHUNKS = (6, 9, 9)
SAFE = 1e28
PAIR, STAGES, LAG = 3, 6, 2


def dot(a, b, dims=NN):
    return lax.dot_general(a, b, dims, preferred_element_type=F32)


def halves(a):
    high = a.astype(BF)
    return jnp.concatenate([high, (a - high.astype(F32)).astype(BF)], axis=1)


def lane_mean(a):
    channels = a.shape[1]
    a = a if a.dtype == BF else halves(a)
    return dot(a, jnp.full((a.shape[1], channels), 1.0 / channels, BF))


def norm_parts(x):
    centered = x.astype(F32) - lane_mean(x)
    scale = lax.rsqrt(lane_mean(centered * centered) + EPSILON)
    return centered * scale, scale


def fold_rows(a):
    return jnp.sum(a.reshape(a.shape[0] // 8, 8, a.shape[1]), axis=0)


def logits_kernel(heads, pair_ref, gain_ref, shift_ref, wbt_ref, out_ref):
    rows, n, channels = pair_ref.shape
    xhat, _ = norm_parts(pair_ref[...].astype(F32).reshape(rows * n, channels).astype(BF))
    normed = (xhat * gain_ref[...] + shift_ref[...]).astype(BF)
    logits = dot(wbt_ref[...], normed, NT)
    for r in range(rows):
        for h in range(heads):
            for t in range(n // channels):
                start = r * n + t * channels
                piece = logits[h : h + 1, start : start + channels]
                out_ref[h * (n // channels) + t, r : r + 1, :] = piece


def send_kernel(start, count, pair_ref, cot_ref, *refs):
    out = refs[-1]
    block, rows = out.shape[0], pair_ref.shape[0]
    skip = out.shape[1] - 2 * count
    if skip:
        for s in range(block):
            out[s, :skip] = refs[0][...].astype(BF)
    for a, ref in enumerate((pair_ref, cot_ref)):
        cells = ref[...].astype(F32)
        for s in range(block):
            first = s * rows + start
            own = jnp.swapaxes(cells[:, first : first + count], 0, 1)
            out[s, skip + a * count : skip + (a + 1) * count] = own.astype(BF)


def columns_kernel(heads, first, last, col0, len_ref, own_ref, cells_ref, *refs):
    if not first:
        (bias_ref, bacc_in, wacc_in, sacc_in), refs = refs[:4], refs[4:]
    if not first and not last:
        early_ref, refs = refs[0], refs[1:]
    gain_ref, shift_ref, wp_ref, wpt_ref, gb_ref, wot_ref = refs[:6]
    refs = refs[6:]
    out_ref, sacc_ref = refs[:2]
    refs = refs[2:]
    if not last:
        (bacc_ref, wacc_ref), refs = refs[:2], refs[2:]
    if first:
        bias_ref, refs = refs[0], refs[1:]
    e_all, ds_all, kbd_all, vaug_all, off_ref = refs[:5]
    if last:
        bacc_ref, wacc_ref = refs[5:]
    step, cols = pl.program_id(0), pl.num_programs(0) * PAIR
    n, channels = bacc_ref.shape[0], wp_ref.shape[0]
    size, thirds, src = channels // heads, n // channels, cells_ref.shape[0]
    slots = heads * thirds
    skip_in = slots if first else 0
    skip_out = slots + 5 if last else out_ref.shape[1] - cols
    lane = lax.broadcasted_iota(jnp.int32, (1, channels), 1)
    masks = [jnp.where(lane // size == h, 1.0, 0.0).astype(BF) for h in range(heads)]
    length = len_ref[0]

    def begin():
        if first:
            bacc_ref[...] = jnp.zeros_like(bacc_ref)
            wacc_ref[...] = jnp.zeros_like(wacc_ref)
            sacc_ref[...] = jnp.zeros_like(sacc_ref)
        else:
            bacc_ref[...] = bacc_in[...]
            wacc_ref[...] = wacc_in[...]
            sacc_ref[...] = sacc_in[...]

    @pl.when(step == 0)
    def _():
        if first:
            kpos = lax.broadcasted_iota(jnp.int32, (1, n), 1)
            for h in range(heads):
                for t in range(thirds):
                    plane = cells_ref[:, h * thirds + t].astype(F32).reshape(n, channels)
                    bias_ref[t * channels : (t + 1) * channels, h * n : (h + 1) * n] = jnp.where(
                        kpos < length, plane.T * LOG2E, DEAD
                    )
        begin()
        if not first and not last:
            out_ref[:, :skip_out] = early_ref[...]
        off_ref[...] = jnp.zeros_like(off_ref)
        for h in range(heads):
            for u in range(PAIR):
                vaug_all[u, h * n : (h + 1) * n, channels:] = jnp.broadcast_to(masks[h], (n, channels))

    def column(j, shifted, slot):
        e_ref, ds_ref, kbd, vaug = e_all.at[slot], ds_all.at[slot], kbd_all.at[slot], vaug_all.at[slot]
        xhat, _ = norm_parts(cells_ref[:, skip_in + j].astype(F32).reshape(n, channels).astype(BF))
        normed_f = xhat * gain_ref[...] + shift_ref[...]
        proj = dot(normed_f.astype(BF), wp_ref[...])
        q_f = proj[:, :channels] * (LOG2E / math.sqrt(size))
        k = proj[:, channels : 2 * channels].astype(BF)
        v = proj[:, 2 * channels : 3 * channels].astype(BF)
        gate = jax.nn.sigmoid(proj[:, 3 * channels :] + gb_ref[...])
        for h in range(heads):
            kbd[h * n : (h + 1) * n, :] = k * masks[h]
            vaug[h * n : (h + 1) * n, :channels] = v * masks[h]
        live = lax.broadcasted_iota(jnp.int32, (n, 1), 0) < length
        live = live & (own_ref[0] + col0 + j < length)
        cot = cells_ref[:, skip_in + cols + j].astype(F32).reshape(n, channels)
        cot = jnp.where(live, cot, 0.0).astype(BF)
        d_out = dot(cot, wot_ref[...])

        yield
        scores = dot(q_f.astype(BF), kbd[...], NT) + bias_ref[...]
        if shifted:
            for h in range(heads):
                part = scores[:, h * n : (h + 1) * n]
                part = jnp.exp2(part - jnp.max(part, axis=1, keepdims=True))
                e_ref[:, h * n : (h + 1) * n] = part.astype(BF)
        else:
            e_ref[...] = jnp.exp2(scores).astype(BF)
        yield
        summed = dot(e_ref[...], vaug[...])
        total = summed[:, channels:]
        if not shifted:
            fits = (total > 1.0 / SAFE) & (total < SAFE)
            off_ref[...] += fold_rows(jnp.where(fits, 0.0, 1.0))
        recip = 1.0 / total
        att = summed[:, :channels] * recip
        d_att = d_out * gate
        d_gate = d_att * att * (1.0 - gate)
        d_att_b = (d_att * recip).astype(BF)
        d_att_f = d_att_b.astype(F32)
        gi = lax.broadcasted_iota(jnp.int32, (2 * channels, channels), 0) % channels
        gj = lax.broadcasted_iota(jnp.int32, (2 * channels, channels), 1)
        group = jnp.where((gi // size == gj // size) & (gj % size < 2), -1.0, 0.0).astype(BF)
        row_dot = dot(halves(d_att_f * att), group)
        row_hi = row_dot.astype(BF).astype(F32)
        row_lanes = jnp.where(lane % size == 0, row_hi, row_dot - row_hi).astype(BF)
        yield
        d_probs = dot(jnp.concatenate([d_att_b, row_lanes], axis=1), vaug[...], NT)
        ds = e_ref[...].astype(F32) * d_probs
        bacc_ref[...] += ds
        ds_ref[...] = ds.astype(BF)
        yield
        d_query = dot(ds_ref[...], kbd[...]) * (1.0 / math.sqrt(size))
        q_t, d_att_t = q_f.T.astype(BF), d_att_f.T.astype(BF)
        dk_t, dv_t = [], []
        for p in range(heads // 2):
            rows = slice(2 * p * size, 2 * (p + 1) * size)
            lanes = slice(2 * p * n, 2 * (p + 1) * n)
            both = dot(q_t[rows], ds_ref[:, lanes])
            dk_t += [both[:size, :n], both[size:, n:]]
            both = dot(d_att_t[rows], e_ref[:, lanes])
            dv_t += [both[:size, :n], both[size:, n:]]
        d_key = (jnp.concatenate(dk_t, axis=0) * LN2).T
        d_value = jnp.concatenate(dv_t, axis=0).T
        yield
        d_proj = jnp.concatenate([g.astype(BF) for g in (d_query, d_key, d_value, d_gate)], axis=1)
        dn = dot(d_proj, wpt_ref[...])
        out_ref[:, skip_out + j] = dn.reshape(src, n // src, channels).astype(BF)
        gated = gate * att
        wacc_ref[:, : 4 * channels] += dot(normed_f.T.astype(BF), d_proj)
        wacc_ref[:, 4 * channels :] += dot(gated.T.astype(BF), cot)
        sacc_ref[0] += fold_rows(d_gate)
        sacc_ref[1] += fold_rows(dn * xhat)
        sacc_ref[2] += fold_rows(dn)

    def run(first_col, shifted):
        ahead = [column(first_col + u, shifted, u) for u in range(PAIR)]
        for turn in range(STAGES + LAG * (PAIR - 1)):
            for u in range(PAIR):
                if LAG * u <= turn < STAGES + LAG * u:
                    next(ahead[u], None)

    run(step * PAIR, False)

    @pl.when(step == pl.num_programs(0) - 1)
    def _():
        @pl.when(jnp.max(off_ref[...]) > 0.0)
        def _():
            begin()

            @pl.loop(0, cols)
            def _(j):
                for _ in column(j, True, 0):
                    pass

        if last:
            for h in range(heads):
                for t in range(thirds):
                    plane = bacc_ref[t * channels : (t + 1) * channels, h * n : (h + 1) * n].T
                    out_ref[:, h * thirds + t] = plane.reshape(src, n // src, channels).astype(BF)
            for w in range(5):
                part = wacc_ref[:, w * channels : (w + 1) * channels].reshape(src, -1, channels)
                terms = []
                for _ in range(3):
                    terms.append(part.astype(BF).astype(F32))
                    part = part - terms[-1]
                out_ref[:, slots + w] = jnp.concatenate(terms, axis=1).astype(BF)


def whole(shape):
    return pl.BlockSpec(shape, lambda j: (0,) * len(shape))


def columns_call(first, last, col0, cols, length, own, moved, state, weights, heads):
    src, _, rows, channels = moved.shape
    n = src * rows
    slots = heads * n // channels
    smem = pl.BlockSpec(memory_space=pltpu.SMEM)
    plane = jax.ShapeDtypeStruct((n, heads * n), F32)
    wide = jax.ShapeDtypeStruct((channels, 5 * channels), F32)
    outs = [
        jax.ShapeDtypeStruct((src, cols + (slots + 5 if last else col0), rows, channels), BF),
        jax.ShapeDtypeStruct((3, 8, channels), F32),
    ]
    outs += ([] if last else [plane, wide]) + ([plane] if first else [])
    inputs = (moved, *state, *weights)
    return pl.pallas_call(
        functools.partial(columns_kernel, heads, first, last, col0),
        grid=(cols // PAIR,),
        in_specs=[smem, smem] + [whole(a.shape) for a in inputs],
        out_specs=[whole(o.shape) for o in outs],
        out_shape=outs,
        scratch_shapes=[
            pltpu.VMEM((PAIR, n, heads * n), BF),
            pltpu.VMEM((PAIR, n, heads * n), BF),
            pltpu.VMEM((PAIR, heads * n, channels), BF),
            pltpu.VMEM((PAIR, heads * n, 2 * channels), BF),
            pltpu.VMEM((8, channels), F32),
        ]
        + ([pltpu.VMEM(o.shape, F32) for o in (plane, wide)] if last else []),
        compiler_params=pltpu.CompilerParams(
            vmem_limit_bytes=56 * MIB, dimension_semantics=("arbitrary",)
        ),
        cost_estimate=pl.CostEstimate(
            flops=cols * 4 * 10**9, bytes_accessed=cols * n * channels * 6, transcendentals=0
        ),
    )(length, own, *inputs)


def side_kernel(heads, pair_ref, parts_ref, gain_ref, shift_ref, wbt_ref, sacc_ref, sum_ref, share_ref):
    rows, n, channels = pair_ref.shape
    thirds = n // channels
    slots = heads * thirds
    total = jnp.sum(parts_ref[:, :slots].astype(F32), axis=0).astype(BF).astype(F32)
    for h in range(heads):
        for t in range(thirds):
            sum_ref[h, :, t * channels : (t + 1) * channels] = total[h * thirds + t]
    for w in range(5):
        part = jnp.sum(parts_ref[:, slots + w].astype(F32), axis=0)
        share_ref[w] = part[:8] + part[8:16] + part[16:24]
    stats = jnp.zeros((heads, 2 * channels), F32)
    flat = jnp.zeros((heads, n), F32)
    for r in range(rows):
        xhat, _ = norm_parts(pair_ref[r])
        normed = (xhat * gain_ref[...] + shift_ref[...]).astype(BF)
        own = sum_ref[:, r, :]
        flat = flat + own
        stats = stats + dot(own.astype(BF), jnp.concatenate([normed, xhat.astype(BF)], axis=1))
    wide = wbt_ref[...].astype(F32)
    share_ref[5, 0:1, :] = jnp.sum(sacc_ref[0], axis=0, keepdims=True)
    gain_part = wide * stats[:, channels:]
    gain_all = jnp.sum(sacc_ref[1], axis=0, keepdims=True)
    share_ref[5, 1:2, :] = gain_all + jnp.sum(gain_part, axis=0, keepdims=True)
    shift_part = wide * jnp.sum(flat, axis=1, keepdims=True)
    shift_all = jnp.sum(sacc_ref[2], axis=0, keepdims=True)
    share_ref[5, 2:3, :] = shift_all + jnp.sum(shift_part, axis=0, keepdims=True)
    share_ref[5, 3 : 3 + heads, :] = stats[:, :channels]
    share_ref[5, 3 + heads :, :] = jnp.zeros((5 - heads, channels), F32)


def norm_back_kernel(first, pair_ref, sums_ref, gain_ref, wbt_ref, *refs):
    parts, out_ref, side_ref = refs[:2], refs[-2], refs[-1]
    rows, cols, channels = pair_ref.shape
    heads, n = sums_ref.shape[0], sums_ref.shape[2]
    step = pl.program_id(0)

    @pl.when(step == 0)
    def _():
        none = jnp.zeros((8 - heads, n), F32)
        span = side_ref.shape[1]
        for r in range(rows):
            own = jnp.concatenate([sums_ref[:, r, :], none], axis=0).T
            own = own[first * cols : first * cols + span, :heads].astype(BF)
            side_ref[r] = dot(own, wbt_ref[...])

    pieces = []
    for s in range(cols // rows):
        for ref, w in zip(parts, (sum(CHUNKS[:-1]), CHUNKS[-1])):
            pieces.append(ref[s, ref.shape[1] - w :].astype(F32))
    main = jnp.swapaxes(jnp.concatenate(pieces, axis=0), 0, 1)
    side = side_ref[:, pl.ds(pl.multiple_of(step * cols, cols), cols), :]
    d_normed = (main + side).astype(BF).astype(F32).reshape(rows * cols, channels)
    cells = pair_ref[...].astype(F32).reshape(rows * cols, channels).astype(BF)
    xhat, scale = norm_parts(cells)
    g = d_normed * gain_ref[...]
    dx = scale * (g - lane_mean(g) - xhat * lane_mean(g * xhat))
    out_ref[...] = dx.reshape(rows, cols, channels).astype(BF)


def final_kernel(heads, size, told_ref, proj_ref, gate_ref, biasw_ref, outw_ref, gain_ref, shift_ref):
    channels = told_ref.shape[-1]
    scale = 1.0 / size
    for w in range(5):
        part = told_ref[:, w].reshape(channels, channels) * scale
        if w < 4:
            proj_ref[:, w * channels : (w + 1) * channels] = part
        else:
            outw_ref[...] = part
    small = jnp.sum(told_ref[:, 5], axis=0) * scale
    gate_ref[...] = small[0:1]
    gain_ref[...] = small[1:2]
    shift_ref[...] = small[2:3]
    biasw_ref[...] = small[3 : 3 + heads]


def body(pair_rep, grad_out, crop_len, ln_gain, ln_bias, w_proj, gate_bias, w_bias, w_out):
    pair, cot = pair_rep[0], grad_out[0]
    rows, n, channels = pair.shape
    heads = w_bias.shape[1]
    src = n // rows
    slots = heads * n // channels
    own = (lax.axis_index("row") * rows).astype(jnp.int32).reshape(1)
    gain, shift = ln_gain.reshape(1, -1), ln_bias.reshape(1, -1)
    wbt = w_bias.T
    weights = (gain, shift, w_proj, w_proj.T, gate_bias.reshape(1, -1), w_out.T)

    def exchange(a, axis="row"):
        return lax.all_to_all(a, axis, 0, 0)

    def tell(a, axis):
        return exchange(jnp.broadcast_to(a[None], (lax.axis_size(axis), *a.shape)), axis)

    block = 2
    tile = block * rows
    group = 8
    plane = pl.pallas_call(
        functools.partial(logits_kernel, heads),
        grid=(rows // group,),
        in_specs=[pl.BlockSpec((group, n, channels), lambda j: (j, 0, 0))]
        + [whole(a.shape) for a in (gain, shift, wbt)],
        out_specs=pl.BlockSpec((slots, group, channels), lambda j: (0, j, 0)),
        out_shape=jax.ShapeDtypeStruct((slots, rows, channels), F32),
        compiler_params=pltpu.CompilerParams(vmem_limit_bytes=60 * MIB),
    )(pair, gain, shift, wbt)
    cells = pl.BlockSpec((rows, tile, channels), lambda j: (0, j, 0))

    def send(start, count, extra):
        deep = 2 * count + sum(a.shape[0] for a in extra)
        return pl.pallas_call(
            functools.partial(send_kernel, start, count),
            grid=(src // block,),
            in_specs=[cells, cells] + [whole(a.shape) for a in extra],
            out_specs=pl.BlockSpec((block, deep, rows, channels), lambda j: (j, 0, 0, 0)),
            out_shape=jax.ShapeDtypeStruct((src, deep, rows, channels), BF),
            compiler_params=pltpu.CompilerParams(vmem_limit_bytes=60 * MIB),
            cost_estimate=pl.CostEstimate(
                flops=5 * 10**9, bytes_accessed=3 * pair.size, transcendentals=0
            ),
        )(pair, cot, *extra)

    starts = [sum(CHUNKS[:c]) for c in range(len(CHUNKS))]
    sent = [send(a, w, (plane,) if a == 0 else ()) for a, w in zip(starts, CHUNKS)]
    moved = [exchange(a) for a in sent]
    state, back = (), []
    for c, (start, width, piece) in enumerate(zip(starts, CHUNKS, moved)):
        first, last = c == 0, c == len(CHUNKS) - 1
        out, sacc, *rest = columns_call(
            first, last, start, width, crop_len, own, piece, state, weights, heads
        )
        if not last:
            plane = rest[2] if first else state[0]
            state = (plane, rest[0], rest[1], sacc)
            if c == len(CHUNKS) - 2:
                early = exchange(out)
            else:
                state += (out,)
    out, early = lax.optimization_barrier((out, early))
    bundle = exchange(out)
    back = (early, bundle)

    sums, share = pl.pallas_call(
        functools.partial(side_kernel, heads),
        grid=(1,),
        in_specs=[
            whole(pair.shape),
            pl.BlockSpec((src, slots + 5, rows, channels), lambda j: (0, 0, 0, 0)),
        ]
        + [whole(a.shape) for a in (gain, shift, wbt, sacc)],
        out_specs=[whole((heads, rows, n)), whole((6, 8, channels))],
        out_shape=[
            jax.ShapeDtypeStruct((heads, rows, n), F32),
            jax.ShapeDtypeStruct((6, 8, channels), F32),
        ],
        compiler_params=pltpu.CompilerParams(vmem_limit_bytes=40 * MIB),
    )(pair, bundle, gain, shift, wbt, sacc)
    def norm_back(first, steps, *written):
        place = lambda j: (0, j + first, 0)
        inputs = (pair, sums, gain, wbt, *back)
        return pl.pallas_call(
            functools.partial(norm_back_kernel, first),
            grid=(steps,),
            in_specs=[pl.BlockSpec((rows, tile, channels), place)]
            + [whole(a.shape) for a in (sums, gain, wbt)]
            + [pl.BlockSpec((block, *a.shape[1:]), lambda j: (j + first, 0, 0, 0)) for a in back]
            + [pl.BlockSpec(memory_space=pl.ANY)] * len(written),
            out_specs=pl.BlockSpec((rows, tile, channels), place),
            out_shape=jax.ShapeDtypeStruct(pair.shape, BF),
            scratch_shapes=[pltpu.VMEM((rows, steps * tile, channels), F32)],
            input_output_aliases={len(inputs): 0} if written else {},
            compiler_params=pltpu.CompilerParams(vmem_limit_bytes=60 * MIB),
            cost_estimate=pl.CostEstimate(
                flops=6 * 10**9, bytes_accessed=2 * pair.size, transcendentals=0
            ),
        )(*inputs, *written)

    blocks = n // tile
    share = tell(share, "dp")
    pair_grad = norm_back(0, blocks // 2)
    share, pair_grad = lax.optimization_barrier((share, pair_grad))
    told = tell(jnp.sum(share, axis=0), "row")
    pair_grad = norm_back(blocks // 2, blocks - blocks // 2, pair_grad)
    proj, gate, biasw, outw, gain_sum, shift_sum = pl.pallas_call(
        functools.partial(final_kernel, heads, n),
        out_shape=[
            jax.ShapeDtypeStruct(s, F32)
            for s in (
                w_proj.shape,
                (1, channels),
                (heads, channels),
                w_out.shape,
                (1, channels),
                (1, channels),
            )
        ],
    )(told)
    return (
        pair_grad[None],
        proj,
        gate.reshape(-1),
        biasw.T,
        outw,
        gain_sum.reshape(-1),
        shift_sum.reshape(-1),
    )


def solution(mesh):
    placed = (
        P("dp", "row", None, None),
        P("dp", "row", None, None),
        P("dp"),
        P(),
        P(),
        P(),
        P(),
        P(),
        P(),
    )
    return jax.shard_map(
        body,
        mesh=mesh,
        in_specs=placed,
        out_specs=(P("dp", "row", None, None), P(), P(), P(), P(), P(), P()),
        check_vma=False,
    )
```

```python
import functools
import math

import jax
import jax.numpy as jnp
from jax import lax
from jax.experimental import pallas as pl
from jax.experimental.pallas import tpu as pltpu
from jax.sharding import PartitionSpec as P

F32, BF = jnp.float32, jnp.bfloat16
EPSILON = 1e-05
LOG2E = 1.4426950408889634
LN2 = 0.6931471805599453
NN = (((1,), (0,)), ((), ()))
NT = (((1,), (1,)), ((), ()))
TN = (((0,), (0,)), ((), ()))
MIB = 2**20
DEAD = -1e30
CHUNKS = (6, 9, 9)
SAFE = 1e28
SLOTS, STAGES, LAG = 4, 6, 2


def dot(a, b, dims=NN):
    return lax.dot_general(a, b, dims, preferred_element_type=F32)


def halves(a):
    high = a.astype(BF)
    return jnp.concatenate([high, (a - high.astype(F32)).astype(BF)], axis=1)


def lane_mean(a):
    channels = a.shape[1]
    a = a if a.dtype == BF else halves(a)
    return dot(a, jnp.full((a.shape[1], channels), 1.0 / channels, BF))


def norm_parts(x):
    centered = x.astype(F32) - lane_mean(x)
    scale = lax.rsqrt(lane_mean(centered * centered) + EPSILON)
    return centered * scale, scale


def fold_rows(a):
    return jnp.sum(a.reshape(a.shape[0] // 8, 8, a.shape[1]), axis=0)


def logits_kernel(heads, pair_ref, gain_ref, shift_ref, wbt_ref, out_ref):
    rows, n, channels = pair_ref.shape
    xhat, _ = norm_parts(pair_ref[...].astype(F32).reshape(rows * n, channels).astype(BF))
    normed = (xhat * gain_ref[...] + shift_ref[...]).astype(BF)
    logits = dot(wbt_ref[...], normed, NT)
    for r in range(rows):
        for h in range(heads):
            for t in range(n // channels):
                start = r * n + t * channels
                piece = logits[h : h + 1, start : start + channels]
                out_ref[h * (n // channels) + t, r : r + 1, :] = piece


def send_kernel(start, count, pair_ref, cot_ref, *refs):
    out = refs[-1]
    block, rows = out.shape[0], pair_ref.shape[0]
    skip = out.shape[1] - 2 * count
    if skip:
        for s in range(block):
            out[s, :skip] = refs[0][...].astype(BF)
    for a, ref in enumerate((pair_ref, cot_ref)):
        cells = ref[...].astype(F32)
        for s in range(block):
            first = s * rows + start
            own = jnp.swapaxes(cells[:, first : first + count], 0, 1)
            out[s, skip + a * count : skip + (a + 1) * count] = own.astype(BF)


def columns_kernel(heads, first, last, col0, cols, len_ref, own_ref, cells_ref, *refs):
    if not first:
        (bias_ref, bacc_in, wacc_in, sacc_in), refs = refs[:4], refs[4:]
    if not first and not last:
        early_ref, refs = refs[0], refs[1:]
    gain_ref, shift_ref, wp_ref, wpt_ref, gb_ref, wot_ref = refs[:6]
    refs = refs[6:]
    out_ref, sacc_ref = refs[:2]
    refs = refs[2:]
    if not last:
        (bacc_ref, wacc_ref), refs = refs[:2], refs[2:]
    if first:
        bias_out, refs = refs[0], refs[1:]
    e_all, ds_all, kbd_all, vaug_all, off_ref, sems = refs[:6]
    refs = refs[6:]
    if first:
        bias_ref, refs = refs[0], refs[1:]
    if last:
        bacc_ref, wacc_ref = refs
    n, channels = bacc_ref.shape[0], wp_ref.shape[0]
    size, thirds, src = channels // heads, n // channels, cells_ref.shape[0]
    slots = heads * thirds
    skip_in = slots if first else 0
    skip_out = slots + 5 if last else out_ref.shape[1] - cols
    lane = lax.broadcasted_iota(jnp.int32, (1, channels), 1)
    masks = [jnp.where(lane // size == h, 1.0, 0.0).astype(BF) for h in range(heads)]
    length = len_ref[0]

    def total_copy():
        return pltpu.make_async_copy(bacc_in, bacc_ref, sems.at[0])

    def early_copy():
        return pltpu.make_async_copy(early_ref, out_ref.at[:, :skip_out], sems.at[1])

    def plane_copy():
        return pltpu.make_async_copy(bias_ref, bias_out, sems.at[1])

    def begin():
        if first:
            bacc_ref[...] = jnp.zeros_like(bacc_ref)
            wacc_ref[...] = jnp.zeros_like(wacc_ref)
            sacc_ref[...] = jnp.zeros_like(sacc_ref)
        else:
            total_copy().start()
            wacc_ref[...] = wacc_in[...]
            sacc_ref[...] = sacc_in[...]

    begin()
    if first:
        kpos = lax.broadcasted_iota(jnp.int32, (1, n), 1)
        for h in range(heads):
            for t in range(thirds):
                plane = cells_ref[:, h * thirds + t].astype(F32).reshape(n, channels)
                bias_ref[t * channels : (t + 1) * channels, h * n : (h + 1) * n] = jnp.where(
                    kpos < length, plane.T * LOG2E, DEAD
                )
        plane_copy().start()
    elif not last:
        early_copy().start()
    off_ref[...] = jnp.zeros_like(off_ref)
    for h in range(heads):
        for u in range(SLOTS):
            vaug_all[u, h * n : (h + 1) * n, channels:] = jnp.broadcast_to(masks[h], (n, channels))

    def column(j, shifted, slot):
        e_ref, ds_ref, kbd, vaug = e_all.at[slot], ds_all.at[slot], kbd_all.at[slot], vaug_all.at[slot]
        xhat, _ = norm_parts(cells_ref[:, skip_in + j].astype(F32).reshape(n, channels).astype(BF))
        normed_f = xhat * gain_ref[...] + shift_ref[...]
        proj = dot(normed_f.astype(BF), wp_ref[...])
        q_f = proj[:, :channels] * (LOG2E / math.sqrt(size))
        k = proj[:, channels : 2 * channels].astype(BF)
        v = proj[:, 2 * channels : 3 * channels].astype(BF)
        gate = jax.nn.sigmoid(proj[:, 3 * channels :] + gb_ref[...])
        for h in range(heads):
            kbd[h * n : (h + 1) * n, :] = k * masks[h]
            vaug[h * n : (h + 1) * n, :channels] = v * masks[h]
        live = lax.broadcasted_iota(jnp.int32, (n, 1), 0) < length
        live = live & (own_ref[0] + col0 + j < length)
        cot = cells_ref[:, skip_in + cols + j].astype(F32).reshape(n, channels)
        cot = jnp.where(live, cot, 0.0).astype(BF)
        d_out = dot(cot, wot_ref[...])

        yield
        scores = dot(q_f.astype(BF), kbd[...], NT) + bias_ref[...]
        if shifted:
            for h in range(heads):
                part = scores[:, h * n : (h + 1) * n]
                part = jnp.exp2(part - jnp.max(part, axis=1, keepdims=True))
                e_ref[:, h * n : (h + 1) * n] = part.astype(BF)
        else:
            e_ref[...] = jnp.exp2(scores).astype(BF)
        yield
        summed = dot(e_ref[...], vaug[...])
        total = summed[:, channels:]
        if not shifted:
            fits = (total > 1.0 / SAFE) & (total < SAFE)
            off_ref[...] += fold_rows(jnp.where(fits, 0.0, 1.0))
        recip = 1.0 / total
        att = summed[:, :channels] * recip
        d_att = d_out * gate
        d_gate = d_att * att * (1.0 - gate)
        d_att_b = (d_att * recip).astype(BF)
        d_att_f = d_att_b.astype(F32)
        gi = lax.broadcasted_iota(jnp.int32, (2 * channels, channels), 0) % channels
        gj = lax.broadcasted_iota(jnp.int32, (2 * channels, channels), 1)
        group = jnp.where((gi // size == gj // size) & (gj % size < 2), -1.0, 0.0).astype(BF)
        row_dot = dot(halves(d_att_f * att), group)
        row_hi = row_dot.astype(BF).astype(F32)
        row_lanes = jnp.where(lane % size == 0, row_hi, row_dot - row_hi).astype(BF)
        yield
        d_probs = dot(jnp.concatenate([d_att_b, row_lanes], axis=1), vaug[...], NT)
        ds = e_ref[...].astype(F32) * d_probs
        if not first and not shifted and isinstance(j, int) and j == 0:
            total_copy().wait()
        bacc_ref[...] += ds
        ds_ref[...] = ds.astype(BF)
        yield
        d_query = dot(ds_ref[...], kbd[...]) * (1.0 / math.sqrt(size))
        q_t, d_att_t = q_f.T.astype(BF), d_att_f.T.astype(BF)
        dk_t, dv_t = [], []
        for p in range(heads // 2):
            rows = slice(2 * p * size, 2 * (p + 1) * size)
            lanes = slice(2 * p * n, 2 * (p + 1) * n)
            both = dot(q_t[rows], ds_ref[:, lanes])
            dk_t += [both[:size, :n], both[size:, n:]]
            both = dot(d_att_t[rows], e_ref[:, lanes])
            dv_t += [both[:size, :n], both[size:, n:]]
        d_key = (jnp.concatenate(dk_t, axis=0) * LN2).T
        d_value = jnp.concatenate(dv_t, axis=0).T
        yield
        d_proj = jnp.concatenate([g.astype(BF) for g in (d_query, d_key, d_value, d_gate)], axis=1)
        dn = dot(d_proj, wpt_ref[...])
        out_ref[:, skip_out + j] = dn.reshape(src, n // src, channels).astype(BF)
        gated = gate * att
        wacc_ref[:, : 4 * channels] += dot(normed_f.T.astype(BF), d_proj)
        wacc_ref[:, 4 * channels :] += dot(gated.T.astype(BF), cot)
        sacc_ref[0] += fold_rows(d_gate)
        sacc_ref[1] += fold_rows(dn * xhat)
        sacc_ref[2] += fold_rows(dn)

    ahead = [column(u, False, u % SLOTS) for u in range(cols)]
    for turn in range(STAGES + LAG * (cols - 1)):
        for u in range(cols):
            if LAG * u <= turn < STAGES + LAG * u:
                next(ahead[u], None)

    @pl.when(jnp.max(off_ref[...]) > 0.0)
    def _():
        begin()
        if not first:
            total_copy().wait()

        @pl.loop(0, cols)
        def _(j):
            for _ in column(j, True, 0):
                pass

    if first:
        plane_copy().wait()
    elif not last:
        early_copy().wait()
    if last:
        for h in range(heads):
            for t in range(thirds):
                plane = bacc_ref[t * channels : (t + 1) * channels, h * n : (h + 1) * n].T
                out_ref[:, h * thirds + t] = plane.reshape(src, n // src, channels).astype(BF)
        for w in range(5):
            part = wacc_ref[:, w * channels : (w + 1) * channels].reshape(src, -1, channels)
            terms = []
            for _ in range(3):
                terms.append(part.astype(BF).astype(F32))
                part = part - terms[-1]
            out_ref[:, slots + w] = jnp.concatenate(terms, axis=1).astype(BF)


def whole(shape):
    return pl.BlockSpec(shape, lambda j: (0,) * len(shape))


def columns_call(first, last, col0, cols, length, own, moved, state, weights, heads):
    src, _, rows, channels = moved.shape
    n = src * rows
    slots = heads * n // channels
    smem = pl.BlockSpec(memory_space=pltpu.SMEM)
    plane = jax.ShapeDtypeStruct((n, heads * n), F32)
    wide = jax.ShapeDtypeStruct((channels, 5 * channels), F32)
    outs = [
        jax.ShapeDtypeStruct((src, cols + (slots + 5 if last else col0), rows, channels), BF),
        jax.ShapeDtypeStruct((3, 8, channels), F32),
    ]
    outs += ([] if last else [plane, wide]) + ([plane] if first else [])
    inputs = (moved, *state, *weights)
    anywhere = pl.BlockSpec(memory_space=pl.ANY)
    in_specs = [smem, smem] + [whole(a.shape) for a in inputs]
    if not first:
        in_specs[4] = anywhere
    if len(state) > 4:
        in_specs[7] = anywhere
    return pl.pallas_call(
        functools.partial(columns_kernel, heads, first, last, col0, cols),
        grid=(1,),
        in_specs=in_specs,
        out_specs=[whole(o.shape) for o in outs[: -1 if first else None]]
        + ([anywhere] if first else []),
        out_shape=outs,
        scratch_shapes=[
            pltpu.VMEM((SLOTS, n, heads * n), BF),
            pltpu.VMEM((SLOTS, n, heads * n), BF),
            pltpu.VMEM((SLOTS, heads * n, channels), BF),
            pltpu.VMEM((SLOTS, heads * n, 2 * channels), BF),
            pltpu.VMEM((8, channels), F32),
            pltpu.SemaphoreType.DMA((2,)),
        ]
        + ([pltpu.VMEM(plane.shape, F32)] if first else [])
        + ([pltpu.VMEM(o.shape, F32) for o in (plane, wide)] if last else []),
        compiler_params=pltpu.CompilerParams(
            vmem_limit_bytes=56 * MIB, dimension_semantics=("arbitrary",)
        ),
        cost_estimate=pl.CostEstimate(
            flops=cols * 4 * 10**9, bytes_accessed=cols * n * channels * 6, transcendentals=0
        ),
    )(length, own, *inputs)


def side_kernel(heads, pair_ref, parts_ref, gain_ref, shift_ref, wbt_ref, sacc_ref, sum_ref, share_ref):
    rows, n, channels = pair_ref.shape
    thirds = n // channels
    slots = heads * thirds
    total = jnp.sum(parts_ref[:, :slots].astype(F32), axis=0).astype(BF).astype(F32)
    for h in range(heads):
        for t in range(thirds):
            sum_ref[h, :, t * channels : (t + 1) * channels] = total[h * thirds + t]
    for w in range(5):
        part = jnp.sum(parts_ref[:, slots + w].astype(F32), axis=0)
        share_ref[w] = part[:8] + part[8:16] + part[16:24]
    stats = jnp.zeros((heads, 2 * channels), F32)
    flat = jnp.zeros((heads, n), F32)
    for r in range(rows):
        xhat, _ = norm_parts(pair_ref[r])
        normed = (xhat * gain_ref[...] + shift_ref[...]).astype(BF)
        own = sum_ref[:, r, :]
        flat = flat + own
        stats = stats + dot(own.astype(BF), jnp.concatenate([normed, xhat.astype(BF)], axis=1))
    wide = wbt_ref[...].astype(F32)
    share_ref[5, 0:1, :] = jnp.sum(sacc_ref[0], axis=0, keepdims=True)
    gain_part = wide * stats[:, channels:]
    gain_all = jnp.sum(sacc_ref[1], axis=0, keepdims=True)
    share_ref[5, 1:2, :] = gain_all + jnp.sum(gain_part, axis=0, keepdims=True)
    shift_part = wide * jnp.sum(flat, axis=1, keepdims=True)
    shift_all = jnp.sum(sacc_ref[2], axis=0, keepdims=True)
    share_ref[5, 2:3, :] = shift_all + jnp.sum(shift_part, axis=0, keepdims=True)
    share_ref[5, 3 : 3 + heads, :] = stats[:, :channels]
    share_ref[5, 3 + heads :, :] = jnp.zeros((5 - heads, channels), F32)


def norm_back_kernel(first, pair_ref, sums_ref, gain_ref, wbt_ref, *refs):
    parts, out_ref, side_ref = refs[:2], refs[-2], refs[-1]
    rows, cols, channels = pair_ref.shape
    heads, n = sums_ref.shape[0], sums_ref.shape[2]
    step = pl.program_id(0)

    @pl.when(step == 0)
    def _():
        none = jnp.zeros((8 - heads, n), F32)
        span = side_ref.shape[1]
        for r in range(rows):
            own = jnp.concatenate([sums_ref[:, r, :], none], axis=0).T
            own = own[first * cols : first * cols + span, :heads].astype(BF)
            side_ref[r] = dot(own, wbt_ref[...])

    pieces = []
    for s in range(cols // rows):
        for ref, w in zip(parts, (sum(CHUNKS[:-1]), CHUNKS[-1])):
            pieces.append(ref[s, ref.shape[1] - w :].astype(F32))
    main = jnp.swapaxes(jnp.concatenate(pieces, axis=0), 0, 1)
    side = side_ref[:, pl.ds(pl.multiple_of(step * cols, cols), cols), :]
    d_normed = (main + side).astype(BF).astype(F32).reshape(rows * cols, channels)
    cells = pair_ref[...].astype(F32).reshape(rows * cols, channels).astype(BF)
    xhat, scale = norm_parts(cells)
    g = d_normed * gain_ref[...]
    dx = scale * (g - lane_mean(g) - xhat * lane_mean(g * xhat))
    out_ref[...] = dx.reshape(rows, cols, channels).astype(BF)


def final_kernel(heads, size, told_ref, proj_ref, gate_ref, biasw_ref, outw_ref, gain_ref, shift_ref):
    channels = told_ref.shape[-1]
    scale = 1.0 / size
    for w in range(5):
        part = told_ref[:, w].reshape(channels, channels) * scale
        if w < 4:
            proj_ref[:, w * channels : (w + 1) * channels] = part
        else:
            outw_ref[...] = part
    small = jnp.sum(told_ref[:, 5], axis=0) * scale
    gate_ref[...] = small[0:1]
    gain_ref[...] = small[1:2]
    shift_ref[...] = small[2:3]
    biasw_ref[...] = small[3 : 3 + heads]


def body(pair_rep, grad_out, crop_len, ln_gain, ln_bias, w_proj, gate_bias, w_bias, w_out):
    pair, cot = pair_rep[0], grad_out[0]
    rows, n, channels = pair.shape
    heads = w_bias.shape[1]
    src = n // rows
    slots = heads * n // channels
    own = (lax.axis_index("row") * rows).astype(jnp.int32).reshape(1)
    gain, shift = ln_gain.reshape(1, -1), ln_bias.reshape(1, -1)
    wbt = w_bias.T
    weights = (gain, shift, w_proj, w_proj.T, gate_bias.reshape(1, -1), w_out.T)

    def exchange(a, axis="row"):
        return lax.all_to_all(a, axis, 0, 0)

    def tell(a, axis):
        return exchange(jnp.broadcast_to(a[None], (lax.axis_size(axis), *a.shape)), axis)

    block = 2
    tile = block * rows
    group = 8
    plane = pl.pallas_call(
        functools.partial(logits_kernel, heads),
        grid=(rows // group,),
        in_specs=[pl.BlockSpec((group, n, channels), lambda j: (j, 0, 0))]
        + [whole(a.shape) for a in (gain, shift, wbt)],
        out_specs=pl.BlockSpec((slots, group, channels), lambda j: (0, j, 0)),
        out_shape=jax.ShapeDtypeStruct((slots, rows, channels), F32),
        compiler_params=pltpu.CompilerParams(vmem_limit_bytes=60 * MIB),
    )(pair, gain, shift, wbt)
    cells = pl.BlockSpec((rows, tile, channels), lambda j: (0, j, 0))

    def send(start, count, extra):
        deep = 2 * count + sum(a.shape[0] for a in extra)
        return pl.pallas_call(
            functools.partial(send_kernel, start, count),
            grid=(src // block,),
            in_specs=[cells, cells] + [whole(a.shape) for a in extra],
            out_specs=pl.BlockSpec((block, deep, rows, channels), lambda j: (j, 0, 0, 0)),
            out_shape=jax.ShapeDtypeStruct((src, deep, rows, channels), BF),
            compiler_params=pltpu.CompilerParams(vmem_limit_bytes=60 * MIB),
            cost_estimate=pl.CostEstimate(
                flops=5 * 10**9, bytes_accessed=3 * pair.size, transcendentals=0
            ),
        )(pair, cot, *extra)

    starts = [sum(CHUNKS[:c]) for c in range(len(CHUNKS))]
    sent = [send(a, w, (plane,) if a == 0 else ()) for a, w in zip(starts, CHUNKS)]
    moved = [exchange(a) for a in sent]
    state, back = (), []
    for c, (start, width, piece) in enumerate(zip(starts, CHUNKS, moved)):
        first, last = c == 0, c == len(CHUNKS) - 1
        out, sacc, *rest = columns_call(
            first, last, start, width, crop_len, own, piece, state, weights, heads
        )
        if not last:
            plane = rest[2] if first else state[0]
            state = (plane, rest[0], rest[1], sacc)
            if c == len(CHUNKS) - 2:
                early = exchange(out)
            else:
                state += (out,)
    out, early = lax.optimization_barrier((out, early))
    bundle = exchange(out)
    back = (early, bundle)

    sums, share = pl.pallas_call(
        functools.partial(side_kernel, heads),
        grid=(1,),
        in_specs=[
            whole(pair.shape),
            pl.BlockSpec((src, slots + 5, rows, channels), lambda j: (0, 0, 0, 0)),
        ]
        + [whole(a.shape) for a in (gain, shift, wbt, sacc)],
        out_specs=[whole((heads, rows, n)), whole((6, 8, channels))],
        out_shape=[
            jax.ShapeDtypeStruct((heads, rows, n), F32),
            jax.ShapeDtypeStruct((6, 8, channels), F32),
        ],
        compiler_params=pltpu.CompilerParams(vmem_limit_bytes=40 * MIB),
    )(pair, bundle, gain, shift, wbt, sacc)
    def norm_back(first, steps, *written):
        place = lambda j: (0, j + first, 0)
        inputs = (pair, sums, gain, wbt, *back)
        return pl.pallas_call(
            functools.partial(norm_back_kernel, first),
            grid=(steps,),
            in_specs=[pl.BlockSpec((rows, tile, channels), place)]
            + [whole(a.shape) for a in (sums, gain, wbt)]
            + [pl.BlockSpec((block, *a.shape[1:]), lambda j: (j + first, 0, 0, 0)) for a in back]
            + [pl.BlockSpec(memory_space=pl.ANY)] * len(written),
            out_specs=pl.BlockSpec((rows, tile, channels), place),
            out_shape=jax.ShapeDtypeStruct(pair.shape, BF),
            scratch_shapes=[pltpu.VMEM((rows, steps * tile, channels), F32)],
            input_output_aliases={len(inputs): 0} if written else {},
            compiler_params=pltpu.CompilerParams(vmem_limit_bytes=60 * MIB),
            cost_estimate=pl.CostEstimate(
                flops=6 * 10**9, bytes_accessed=2 * pair.size, transcendentals=0
            ),
        )(*inputs, *written)

    blocks = n // tile
    share = tell(share, "dp")
    pair_grad = norm_back(0, blocks // 2)
    share, pair_grad = lax.optimization_barrier((share, pair_grad))
    told = tell(jnp.sum(share, axis=0), "row")
    pair_grad = norm_back(blocks // 2, blocks - blocks // 2, pair_grad)
    proj, gate, biasw, outw, gain_sum, shift_sum = pl.pallas_call(
        functools.partial(final_kernel, heads, n),
        out_shape=[
            jax.ShapeDtypeStruct(s, F32)
            for s in (
                w_proj.shape,
                (1, channels),
                (heads, channels),
                w_out.shape,
                (1, channels),
                (1, channels),
            )
        ],
    )(told)
    return (
        pair_grad[None],
        proj,
        gate.reshape(-1),
        biasw.T,
        outw,
        gain_sum.reshape(-1),
        shift_sum.reshape(-1),
    )


def solution(mesh):
    placed = (
        P("dp", "row", None, None),
        P("dp", "row", None, None),
        P("dp"),
        P(),
        P(),
        P(),
        P(),
        P(),
        P(),
    )
    return jax.shard_map(
        body,
        mesh=mesh,
        in_specs=placed,
        out_specs=(P("dp", "row", None, None), P(), P(), P(), P(), P(), P()),
        check_vma=False,
    )
```

```python
import functools
import math

import jax
import jax.numpy as jnp
from jax import lax
from jax.experimental import pallas as pl
from jax.experimental.pallas import tpu as pltpu
from jax.sharding import PartitionSpec as P

F32, BF = jnp.float32, jnp.bfloat16
EPSILON = 1e-05
LOG2E = 1.4426950408889634
LN2 = 0.6931471805599453
NN = (((1,), (0,)), ((), ()))
NT = (((1,), (1,)), ((), ()))
TN = (((0,), (0,)), ((), ()))
MIB = 2**20
DEAD = -1e30
CHUNKS = (6, 9, 9)
SAFE = 1e28
GROUPS = (6, 9, 9)
SHARES = 4
SLOTS, STAGES, LAG = 4, 6, 2


def dot(a, b, dims=NN):
    return lax.dot_general(a, b, dims, preferred_element_type=F32)


def halves(a):
    high = a.astype(BF)
    return jnp.concatenate([high, (a - high.astype(F32)).astype(BF)], axis=1)


def lane_mean(a):
    channels = a.shape[1]
    a = a if a.dtype == BF else halves(a)
    return dot(a, jnp.full((a.shape[1], channels), 1.0 / channels, BF))


def norm_parts(x):
    centered = x.astype(F32) - lane_mean(x)
    scale = lax.rsqrt(lane_mean(centered * centered) + EPSILON)
    return centered * scale, scale


def fold_rows(a):
    return jnp.sum(a.reshape(a.shape[0] // 8, 8, a.shape[1]), axis=0)


def logits_kernel(heads, pair_ref, gain_ref, shift_ref, wbt_ref, out_ref):
    rows, n, channels = pair_ref.shape
    xhat, _ = norm_parts(pair_ref[...].astype(F32).reshape(rows * n, channels).astype(BF))
    normed = (xhat * gain_ref[...] + shift_ref[...]).astype(BF)
    logits = dot(wbt_ref[...], normed, NT)
    for r in range(rows):
        for h in range(heads):
            for t in range(n // channels):
                start = r * n + t * channels
                piece = logits[h : h + 1, start : start + channels]
                out_ref[h * (n // channels) + t, r : r + 1, :] = piece


def send_kernel(start, count, pair_ref, cot_ref, *refs):
    out = refs[-1]
    block, rows = out.shape[0], pair_ref.shape[0]
    skip = out.shape[1] - 2 * count
    if skip:
        for s in range(block):
            out[s, :skip] = refs[0][...].astype(BF)
    for a, ref in enumerate((pair_ref, cot_ref)):
        cells = ref[...].astype(F32)
        for s in range(block):
            first = s * rows + start
            own = jnp.swapaxes(cells[:, first : first + count], 0, 1)
            out[s, skip + a * count : skip + (a + 1) * count] = own.astype(BF)


def columns_kernel(heads, first, last, col0, cols, group, len_ref, own_ref, cells_ref, *refs):
    if not first:
        (bias_ref, bacc_in, wacc_in, sacc_in), refs = refs[:4], refs[4:]
    if not first and not last:
        early_ref, refs = refs[0], refs[1:]
    gain_ref, shift_ref, wp_ref, wpt_ref, gb_ref, wot_ref = refs[:6]
    refs = refs[6:]
    out_ref, sacc_ref = refs[:2]
    refs = refs[2:]
    if not last:
        (bacc_ref, wacc_ref), refs = refs[:2], refs[2:]
    if first:
        bias_ref, refs = refs[0], refs[1:]
    e_all, ds_all, kbd_all, vaug_all, off_ref, sems = refs[:6]
    refs = refs[6:]
    if last:
        bacc_ref, wacc_ref = refs
    step = pl.program_id(0)
    n, channels = bacc_ref.shape[0], wp_ref.shape[0]
    size, thirds, src = channels // heads, n // channels, cells_ref.shape[0]
    slots = heads * thirds
    skip_in = slots if first else 0
    skip_out = slots + SHARES if last else out_ref.shape[1] - cols
    lane = lax.broadcasted_iota(jnp.int32, (1, channels), 1)
    masks = [jnp.where(lane // size == h, 1.0, 0.0).astype(BF) for h in range(heads)]
    length = len_ref[0]

    def total_copy():
        return pltpu.make_async_copy(bacc_in, bacc_ref, sems.at[0])

    def early_copy():
        return pltpu.make_async_copy(early_ref, out_ref.at[:, :skip_out], sems.at[1])

    def begin():
        if first:
            bacc_ref[...] = jnp.zeros_like(bacc_ref)
            wacc_ref[...] = jnp.zeros_like(wacc_ref)
            sacc_ref[...] = jnp.zeros_like(sacc_ref)
        else:
            total_copy().start()
            wacc_ref[...] = wacc_in[...]
            sacc_ref[...] = sacc_in[...]

    @pl.when(step == 0)
    def _():
        begin()
        if first:
            kpos = lax.broadcasted_iota(jnp.int32, (1, n), 1)
            for h in range(heads):
                for t in range(thirds):
                    plane = cells_ref[:, h * thirds + t].astype(F32).reshape(n, channels)
                    bias_ref[t * channels : (t + 1) * channels, h * n : (h + 1) * n] = jnp.where(
                        kpos < length, plane.T * LOG2E, DEAD
                    )
        elif not last:
            early_copy().start()
        off_ref[...] = jnp.zeros_like(off_ref)
        for h in range(heads):
            for u in range(SLOTS):
                vaug_all[u, h * n : (h + 1) * n, channels:] = jnp.broadcast_to(masks[h], (n, channels))

    def column(j, shifted, slot, wait=False):
        e_ref, ds_ref, kbd, vaug = e_all.at[slot], ds_all.at[slot], kbd_all.at[slot], vaug_all.at[slot]
        xhat, _ = norm_parts(cells_ref[:, skip_in + j].astype(F32).reshape(n, channels).astype(BF))
        normed_f = xhat * gain_ref[...] + shift_ref[...]
        proj = dot(normed_f.astype(BF), wp_ref[...])
        q_f = proj[:, :channels] * (LOG2E / math.sqrt(size))
        k = proj[:, channels : 2 * channels].astype(BF)
        v = proj[:, 2 * channels : 3 * channels].astype(BF)
        gate = jax.nn.sigmoid(proj[:, 3 * channels :] + gb_ref[...])
        for h in range(heads):
            kbd[h * n : (h + 1) * n, :] = k * masks[h]
            vaug[h * n : (h + 1) * n, :channels] = v * masks[h]
        live = lax.broadcasted_iota(jnp.int32, (n, 1), 0) < length
        live = live & (own_ref[0] + col0 + j < length)
        cot = cells_ref[:, skip_in + cols + j].astype(F32).reshape(n, channels)
        cot = jnp.where(live, cot, 0.0).astype(BF)
        d_out = dot(cot, wot_ref[...])

        yield
        scores = dot(q_f.astype(BF), kbd[...], NT) + bias_ref[...]
        if shifted:
            for h in range(heads):
                part = scores[:, h * n : (h + 1) * n]
                part = jnp.exp2(part - jnp.max(part, axis=1, keepdims=True))
                e_ref[:, h * n : (h + 1) * n] = part.astype(BF)
        else:
            e_ref[...] = jnp.exp2(scores).astype(BF)
        yield
        summed = dot(e_ref[...], vaug[...])
        total = summed[:, channels:]
        if not shifted:
            fits = (total > 1.0 / SAFE) & (total < SAFE)
            off_ref[...] += fold_rows(jnp.where(fits, 0.0, 1.0))
        recip = 1.0 / total
        att = summed[:, :channels] * recip
        d_att = d_out * gate
        d_gate = d_att * att * (1.0 - gate)
        d_att_b = (d_att * recip).astype(BF)
        d_att_f = d_att_b.astype(F32)
        gi = lax.broadcasted_iota(jnp.int32, (2 * channels, channels), 0) % channels
        gj = lax.broadcasted_iota(jnp.int32, (2 * channels, channels), 1)
        group = jnp.where((gi // size == gj // size) & (gj % size < 2), -1.0, 0.0).astype(BF)
        row_dot = dot(halves(d_att_f * att), group)
        row_hi = row_dot.astype(BF).astype(F32)
        row_lanes = jnp.where(lane % size == 0, row_hi, row_dot - row_hi).astype(BF)
        yield
        d_probs = dot(jnp.concatenate([d_att_b, row_lanes], axis=1), vaug[...], NT)
        ds = e_ref[...].astype(F32) * d_probs
        if wait:
            total_copy().wait()
        bacc_ref[...] += ds
        ds_ref[...] = ds.astype(BF)
        yield
        d_query = dot(ds_ref[...], kbd[...]) * (1.0 / math.sqrt(size))
        q_t, d_att_t = q_f.T.astype(BF), d_att_f.T.astype(BF)
        dk_t, dv_t = [], []
        for p in range(heads // 2):
            rows = slice(2 * p * size, 2 * (p + 1) * size)
            lanes = slice(2 * p * n, 2 * (p + 1) * n)
            both = dot(q_t[rows], ds_ref[:, lanes])
            dk_t += [both[:size, :n], both[size:, n:]]
            both = dot(d_att_t[rows], e_ref[:, lanes])
            dv_t += [both[:size, :n], both[size:, n:]]
        d_key = (jnp.concatenate(dk_t, axis=0) * LN2).T
        d_value = jnp.concatenate(dv_t, axis=0).T
        yield
        d_proj = jnp.concatenate([g.astype(BF) for g in (d_query, d_key, d_value, d_gate)], axis=1)
        dn = dot(d_proj, wpt_ref[...])
        out_ref[:, skip_out + j] = dn.reshape(src, n // src, channels).astype(BF)
        gated = gate * att
        wacc_ref[:, : 4 * channels] += dot(normed_f.T.astype(BF), d_proj)
        wacc_ref[:, 4 * channels :] += dot(gated.T.astype(BF), cot)
        sacc_ref[0] += fold_rows(d_gate)
        sacc_ref[1] += fold_rows(dn * xhat)
        sacc_ref[2] += fold_rows(dn)

    ahead = [
        column(step * group + u, False, u % SLOTS, not first and u == 0) for u in range(group)
    ]
    for turn in range(STAGES + LAG * (group - 1)):
        for u in range(group):
            if LAG * u <= turn < STAGES + LAG * u:
                next(ahead[u], None)

    @pl.when(step == cols // group - 1)
    def _():
        @pl.when(jnp.max(off_ref[...]) > 0.0)
        def _():
            begin()
            if not first:
                total_copy().wait()

            @pl.loop(0, cols)
            def _(j):
                for _ in column(j, True, 0):
                    pass

        if not first and not last:
            early_copy().wait()
        if last:
            for h in range(heads):
                for t in range(thirds):
                    plane = bacc_ref[t * channels : (t + 1) * channels, h * n : (h + 1) * n].T
                    out_ref[:, h * thirds + t] = plane.reshape(src, n // src, channels).astype(BF)
            terms = []
            for w in range(5):
                part = wacc_ref[:, w * channels : (w + 1) * channels].reshape(src, -1, channels)
                terms.append(part.astype(BF).astype(F32))
                terms.append(part - terms[-1])
            terms += [jnp.zeros_like(terms[0])] * 2
            for w in range(SHARES):
                three = jnp.concatenate(terms[3 * w : 3 * w + 3], axis=1)
                out_ref[:, slots + w] = three.astype(BF)


def whole(shape):
    return pl.BlockSpec(shape, lambda j: (0,) * len(shape))


def columns_call(first, last, col0, cols, group, length, own, moved, state, weights, heads):
    src, _, rows, channels = moved.shape
    n = src * rows
    slots = heads * n // channels
    smem = pl.BlockSpec(memory_space=pltpu.SMEM)
    plane = jax.ShapeDtypeStruct((n, heads * n), F32)
    wide = jax.ShapeDtypeStruct((channels, 5 * channels), F32)
    outs = [
        jax.ShapeDtypeStruct((src, cols + (slots + SHARES if last else col0), rows, channels), BF),
        jax.ShapeDtypeStruct((3, 8, channels), F32),
    ]
    outs += ([] if last else [plane, wide]) + ([plane] if first else [])
    inputs = (moved, *state, *weights)
    anywhere = pl.BlockSpec(memory_space=pl.ANY)
    in_specs = [smem, smem] + [whole(a.shape) for a in inputs]
    if not first:
        in_specs[4] = anywhere
    if len(state) > 4:
        in_specs[7] = anywhere
    return pl.pallas_call(
        functools.partial(columns_kernel, heads, first, last, col0, cols, group),
        grid=(cols // group,),
        in_specs=in_specs,
        out_specs=[whole(o.shape) for o in outs],
        out_shape=outs,
        scratch_shapes=[
            pltpu.VMEM((SLOTS, n, heads * n), BF),
            pltpu.VMEM((SLOTS, n, heads * n), BF),
            pltpu.VMEM((SLOTS, heads * n, channels), BF),
            pltpu.VMEM((SLOTS, heads * n, 2 * channels), BF),
            pltpu.VMEM((8, channels), F32),
            pltpu.SemaphoreType.DMA((2,)),
        ]
        + ([pltpu.VMEM(o.shape, F32) for o in (plane, wide)] if last else []),
        compiler_params=pltpu.CompilerParams(
            vmem_limit_bytes=56 * MIB, dimension_semantics=("arbitrary",)
        ),
        cost_estimate=pl.CostEstimate(
            flops=cols * 4 * 10**9, bytes_accessed=cols * n * channels * 6, transcendentals=0
        ),
    )(length, own, *inputs)


def side_kernel(heads, pair_ref, parts_ref, gain_ref, shift_ref, wbt_ref, sacc_ref, sum_ref, share_ref):
    rows, n, channels = pair_ref.shape
    thirds = n // channels
    slots = heads * thirds
    total = jnp.sum(parts_ref[:, :slots].astype(F32), axis=0).astype(BF).astype(F32)
    for h in range(heads):
        for t in range(thirds):
            sum_ref[h, :, t * channels : (t + 1) * channels] = total[h * thirds + t]
    terms = []
    for w in range(SHARES):
        part = jnp.sum(parts_ref[:, slots + w].astype(F32), axis=0)
        terms += [part[:8], part[8:16], part[16:24]]
    for w in range(5):
        share_ref[w] = terms[2 * w] + terms[2 * w + 1]
    stats = jnp.zeros((heads, 2 * channels), F32)
    flat = jnp.zeros((heads, n), F32)
    for r in range(rows):
        xhat, _ = norm_parts(pair_ref[r])
        normed = (xhat * gain_ref[...] + shift_ref[...]).astype(BF)
        own = sum_ref[:, r, :]
        flat = flat + own
        stats = stats + dot(own.astype(BF), jnp.concatenate([normed, xhat.astype(BF)], axis=1))
    wide = wbt_ref[...].astype(F32)
    share_ref[5, 0:1, :] = jnp.sum(sacc_ref[0], axis=0, keepdims=True)
    gain_part = wide * stats[:, channels:]
    gain_all = jnp.sum(sacc_ref[1], axis=0, keepdims=True)
    share_ref[5, 1:2, :] = gain_all + jnp.sum(gain_part, axis=0, keepdims=True)
    shift_part = wide * jnp.sum(flat, axis=1, keepdims=True)
    shift_all = jnp.sum(sacc_ref[2], axis=0, keepdims=True)
    share_ref[5, 2:3, :] = shift_all + jnp.sum(shift_part, axis=0, keepdims=True)
    share_ref[5, 3 : 3 + heads, :] = stats[:, :channels]
    share_ref[5, 3 + heads :, :] = jnp.zeros((5 - heads, channels), F32)


def norm_back_kernel(first, pair_ref, sums_ref, gain_ref, wbt_ref, *refs):
    parts, out_ref, side_ref = refs[:2], refs[-2], refs[-1]
    rows, cols, channels = pair_ref.shape
    heads, n = sums_ref.shape[0], sums_ref.shape[2]
    step = pl.program_id(0)

    @pl.when(step == 0)
    def _():
        none = jnp.zeros((8 - heads, n), F32)
        span = side_ref.shape[1]
        for r in range(rows):
            own = jnp.concatenate([sums_ref[:, r, :], none], axis=0).T
            own = own[first * cols : first * cols + span, :heads].astype(BF)
            side_ref[r] = dot(own, wbt_ref[...])

    pieces = []
    for s in range(cols // rows):
        for ref, w in zip(parts, (sum(CHUNKS[:-1]), CHUNKS[-1])):
            pieces.append(ref[s, ref.shape[1] - w :].astype(F32))
    main = jnp.swapaxes(jnp.concatenate(pieces, axis=0), 0, 1)
    side = side_ref[:, pl.ds(pl.multiple_of(step * cols, cols), cols), :]
    d_normed = (main + side).astype(BF).astype(F32).reshape(rows * cols, channels)
    cells = pair_ref[...].astype(F32).reshape(rows * cols, channels).astype(BF)
    xhat, scale = norm_parts(cells)
    g = d_normed * gain_ref[...]
    dx = scale * (g - lane_mean(g) - xhat * lane_mean(g * xhat))
    out_ref[...] = dx.reshape(rows, cols, channels).astype(BF)


def final_kernel(heads, size, told_ref, proj_ref, gate_ref, biasw_ref, outw_ref, gain_ref, shift_ref):
    channels = told_ref.shape[-1]
    scale = 1.0 / size
    for w in range(5):
        part = told_ref[:, w].reshape(channels, channels) * scale
        if w < 4:
            proj_ref[:, w * channels : (w + 1) * channels] = part
        else:
            outw_ref[...] = part
    small = jnp.sum(told_ref[:, 5], axis=0) * scale
    gate_ref[...] = small[0:1]
    gain_ref[...] = small[1:2]
    shift_ref[...] = small[2:3]
    biasw_ref[...] = small[3 : 3 + heads]


def body(pair_rep, grad_out, crop_len, ln_gain, ln_bias, w_proj, gate_bias, w_bias, w_out):
    pair, cot = pair_rep[0], grad_out[0]
    rows, n, channels = pair.shape
    heads = w_bias.shape[1]
    src = n // rows
    slots = heads * n // channels
    own = (lax.axis_index("row") * rows).astype(jnp.int32).reshape(1)
    gain, shift = ln_gain.reshape(1, -1), ln_bias.reshape(1, -1)
    wbt = w_bias.T
    weights = (gain, shift, w_proj, w_proj.T, gate_bias.reshape(1, -1), w_out.T)

    def exchange(a, axis="row"):
        return lax.all_to_all(a, axis, 0, 0)

    def tell(a, axis):
        return exchange(jnp.broadcast_to(a[None], (lax.axis_size(axis), *a.shape)), axis)

    block = 2
    tile = block * rows
    lines = 8
    plane = pl.pallas_call(
        functools.partial(logits_kernel, heads),
        grid=(rows // lines,),
        in_specs=[pl.BlockSpec((lines, n, channels), lambda j: (j, 0, 0))]
        + [whole(a.shape) for a in (gain, shift, wbt)],
        out_specs=pl.BlockSpec((slots, lines, channels), lambda j: (0, j, 0)),
        out_shape=jax.ShapeDtypeStruct((slots, rows, channels), F32),
        compiler_params=pltpu.CompilerParams(vmem_limit_bytes=60 * MIB),
    )(pair, gain, shift, wbt)
    many = src // 2
    cells = pl.BlockSpec((rows, many * rows, channels), lambda j: (0, j, 0))

    def send(start, count, extra):
        deep = 2 * count + sum(a.shape[0] for a in extra)
        return pl.pallas_call(
            functools.partial(send_kernel, start, count),
            grid=(src // many,),
            in_specs=[cells, cells] + [whole(a.shape) for a in extra],
            out_specs=pl.BlockSpec((many, deep, rows, channels), lambda j: (j, 0, 0, 0)),
            out_shape=jax.ShapeDtypeStruct((src, deep, rows, channels), BF),
            compiler_params=pltpu.CompilerParams(vmem_limit_bytes=60 * MIB),
            cost_estimate=pl.CostEstimate(
                flops=5 * 10**9, bytes_accessed=3 * pair.size, transcendentals=0
            ),
        )(pair, cot, *extra)

    starts = [sum(CHUNKS[:c]) for c in range(len(CHUNKS))]
    sent = [send(a, w, (plane,) if a == 0 else ()) for a, w in zip(starts, CHUNKS)]
    moved = [exchange(a) for a in sent]
    state, back = (), []
    for c, (start, width, group, piece) in enumerate(zip(starts, CHUNKS, GROUPS, moved)):
        first, last = c == 0, c == len(CHUNKS) - 1
        out, sacc, *rest = columns_call(
            first, last, start, width, group, crop_len, own, piece, state, weights, heads
        )
        if not last:
            plane = rest[2] if first else state[0]
            state = (plane, rest[0], rest[1], sacc)
            if c == len(CHUNKS) - 2:
                early = exchange(out)
            else:
                state += (out,)
    out, early = lax.optimization_barrier((out, early))
    bundle = exchange(out)
    back = (early, bundle)

    sums, share = pl.pallas_call(
        functools.partial(side_kernel, heads),
        grid=(1,),
        in_specs=[
            whole(pair.shape),
            pl.BlockSpec((src, slots + SHARES, rows, channels), lambda j: (0, 0, 0, 0)),
        ]
        + [whole(a.shape) for a in (gain, shift, wbt, sacc)],
        out_specs=[whole((heads, rows, n)), whole((6, 8, channels))],
        out_shape=[
            jax.ShapeDtypeStruct((heads, rows, n), F32),
            jax.ShapeDtypeStruct((6, 8, channels), F32),
        ],
        compiler_params=pltpu.CompilerParams(vmem_limit_bytes=40 * MIB),
    )(pair, bundle, gain, shift, wbt, sacc)
    def norm_back(first, steps, *written):
        place = lambda j: (0, j + first, 0)
        inputs = (pair, sums, gain, wbt, *back)
        return pl.pallas_call(
            functools.partial(norm_back_kernel, first),
            grid=(steps,),
            in_specs=[pl.BlockSpec((rows, tile, channels), place)]
            + [whole(a.shape) for a in (sums, gain, wbt)]
            + [pl.BlockSpec((block, *a.shape[1:]), lambda j: (j + first, 0, 0, 0)) for a in back]
            + [pl.BlockSpec(memory_space=pl.ANY)] * len(written),
            out_specs=pl.BlockSpec((rows, tile, channels), place),
            out_shape=jax.ShapeDtypeStruct(pair.shape, BF),
            scratch_shapes=[pltpu.VMEM((rows, steps * tile, channels), F32)],
            input_output_aliases={len(inputs): 0} if written else {},
            compiler_params=pltpu.CompilerParams(vmem_limit_bytes=60 * MIB),
            cost_estimate=pl.CostEstimate(
                flops=6 * 10**9, bytes_accessed=2 * pair.size, transcendentals=0
            ),
        )(*inputs, *written)

    blocks = n // tile
    share = tell(share, "dp")
    pair_grad = norm_back(0, blocks // 2)
    share, pair_grad = lax.optimization_barrier((share, pair_grad))
    told = tell(jnp.sum(share, axis=0), "row")
    pair_grad = norm_back(blocks // 2, blocks - blocks // 2, pair_grad)
    proj, gate, biasw, outw, gain_sum, shift_sum = pl.pallas_call(
        functools.partial(final_kernel, heads, n),
        out_shape=[
            jax.ShapeDtypeStruct(s, F32)
            for s in (
                w_proj.shape,
                (1, channels),
                (heads, channels),
                w_out.shape,
                (1, channels),
                (1, channels),
            )
        ],
    )(told)
    return (
        pair_grad[None],
        proj,
        gate.reshape(-1),
        biasw.T,
        outw,
        gain_sum.reshape(-1),
        shift_sum.reshape(-1),
    )


def solution(mesh):
    placed = (
        P("dp", "row", None, None),
        P("dp", "row", None, None),
        P("dp"),
        P(),
        P(),
        P(),
        P(),
        P(),
        P(),
    )
    return jax.shard_map(
        body,
        mesh=mesh,
        in_specs=placed,
        out_specs=(P("dp", "row", None, None), P(), P(), P(), P(), P(), P()),
        check_vma=False,
    )
```

```python
import functools
import math

import jax
import jax.numpy as jnp
from jax import lax
from jax.experimental import pallas as pl
from jax.experimental.pallas import tpu as pltpu
from jax.sharding import PartitionSpec as P

F32, BF = jnp.float32, jnp.bfloat16
EPSILON = 1e-05
LOG2E = 1.4426950408889634
LN2 = 0.6931471805599453
NN = (((1,), (0,)), ((), ()))
NT = (((1,), (1,)), ((), ()))
TN = (((0,), (0,)), ((), ()))
MIB = 2**20
DEAD = -1e30
CHUNKS = (6, 9, 9)
SAFE = 1e28
GROUPS = (3, 9, 9)
SHARES = 4
SLOTS, STAGES, LAG = 4, 6, 2


def dot(a, b, dims=NN):
    return lax.dot_general(a, b, dims, preferred_element_type=F32)


def halves(a):
    high = a.astype(BF)
    return jnp.concatenate([high, (a - high.astype(F32)).astype(BF)], axis=1)


def lane_mean(a):
    channels = a.shape[1]
    a = a if a.dtype == BF else halves(a)
    return dot(a, jnp.full((a.shape[1], channels), 1.0 / channels, BF))


def norm_parts(x):
    centered = x.astype(F32) - lane_mean(x)
    scale = lax.rsqrt(lane_mean(centered * centered) + EPSILON)
    return centered * scale, scale


def fold_rows(a):
    return jnp.sum(a.reshape(a.shape[0] // 8, 8, a.shape[1]), axis=0)


def logits_kernel(heads, pair_ref, gain_ref, shift_ref, wbt_ref, out_ref):
    rows, n, channels = pair_ref.shape
    xhat, _ = norm_parts(pair_ref[...].astype(F32).reshape(rows * n, channels).astype(BF))
    normed = (xhat * gain_ref[...] + shift_ref[...]).astype(BF)
    logits = dot(wbt_ref[...], normed, NT)
    for r in range(rows):
        for h in range(heads):
            for t in range(n // channels):
                start = r * n + t * channels
                piece = logits[h : h + 1, start : start + channels]
                out_ref[h * (n // channels) + t, r : r + 1, :] = piece


def send_kernel(start, count, pair_ref, cot_ref, *refs):
    out = refs[-1]
    block, rows = out.shape[0], pair_ref.shape[0]
    skip = out.shape[1] - 2 * count
    if skip:
        for s in range(block):
            out[s, :skip] = refs[0][...].astype(BF)
    for a, ref in enumerate((pair_ref, cot_ref)):
        cells = ref[...].astype(F32)
        for s in range(block):
            first = s * rows + start
            own = jnp.swapaxes(cells[:, first : first + count], 0, 1)
            out[s, skip + a * count : skip + (a + 1) * count] = own.astype(BF)


def columns_kernel(heads, first, last, col0, cols, group, len_ref, own_ref, cells_ref, *refs):
    if not first:
        (bias_ref, bacc_in, wacc_in, sacc_in), refs = refs[:4], refs[4:]
    if not first and not last:
        early_ref, refs = refs[0], refs[1:]
    gain_ref, shift_ref, wp_ref, wpt_ref, gb_ref, wot_ref = refs[:6]
    refs = refs[6:]
    out_ref, sacc_ref = refs[:2]
    refs = refs[2:]
    if not last:
        (bacc_ref, wacc_ref), refs = refs[:2], refs[2:]
    if first:
        bias_ref, refs = refs[0], refs[1:]
    e_all, ds_all, kbd_all, vaug_all, off_ref, sems = refs[:6]
    refs = refs[6:]
    if last:
        bacc_ref, wacc_ref = refs
    step = pl.program_id(0)
    n, channels = bacc_ref.shape[0], wp_ref.shape[0]
    size, thirds, src = channels // heads, n // channels, cells_ref.shape[0]
    slots = heads * thirds
    skip_in = slots if first else 0
    skip_out = slots + SHARES if last else out_ref.shape[1] - cols
    lane = lax.broadcasted_iota(jnp.int32, (1, channels), 1)
    masks = [jnp.where(lane // size == h, 1.0, 0.0).astype(BF) for h in range(heads)]
    length = len_ref[0]

    def total_copy():
        return pltpu.make_async_copy(bacc_in, bacc_ref, sems.at[0])

    def early_copy():
        return pltpu.make_async_copy(early_ref, out_ref.at[:, :skip_out], sems.at[1])

    def begin():
        if first:
            bacc_ref[...] = jnp.zeros_like(bacc_ref)
            wacc_ref[...] = jnp.zeros_like(wacc_ref)
            sacc_ref[...] = jnp.zeros_like(sacc_ref)
        else:
            total_copy().start()
            wacc_ref[...] = wacc_in[...]
            sacc_ref[...] = sacc_in[...]

    @pl.when(step == 0)
    def _():
        begin()
        if first:
            kpos = lax.broadcasted_iota(jnp.int32, (1, n), 1)
            for h in range(heads):
                for t in range(thirds):
                    plane = cells_ref[:, h * thirds + t].astype(F32).reshape(n, channels)
                    bias_ref[t * channels : (t + 1) * channels, h * n : (h + 1) * n] = jnp.where(
                        kpos < length, plane.T * LOG2E, DEAD
                    )
        elif not last:
            early_copy().start()
        off_ref[...] = jnp.zeros_like(off_ref)
        for h in range(heads):
            for u in range(SLOTS):
                vaug_all[u, h * n : (h + 1) * n, channels:] = jnp.broadcast_to(masks[h], (n, channels))

    def column(j, shifted, slot, wait=False):
        e_ref, ds_ref, kbd, vaug = e_all.at[slot], ds_all.at[slot], kbd_all.at[slot], vaug_all.at[slot]
        xhat, _ = norm_parts(cells_ref[:, skip_in + j].astype(F32).reshape(n, channels).astype(BF))
        normed_f = xhat * gain_ref[...] + shift_ref[...]
        proj = dot(normed_f.astype(BF), wp_ref[...])
        q_f = proj[:, :channels] * (LOG2E / math.sqrt(size))
        k = proj[:, channels : 2 * channels].astype(BF)
        v = proj[:, 2 * channels : 3 * channels].astype(BF)
        gate = jax.nn.sigmoid(proj[:, 3 * channels :] + gb_ref[...])
        for h in range(heads):
            kbd[h * n : (h + 1) * n, :] = k * masks[h]
            vaug[h * n : (h + 1) * n, :channels] = v * masks[h]
        live = lax.broadcasted_iota(jnp.int32, (n, 1), 0) < length
        live = live & (own_ref[0] + col0 + j < length)
        cot = cells_ref[:, skip_in + cols + j].astype(F32).reshape(n, channels)
        cot = jnp.where(live, cot, 0.0).astype(BF)
        d_out = dot(cot, wot_ref[...])

        yield
        scores = dot(q_f.astype(BF), kbd[...], NT) + bias_ref[...]
        if shifted:
            for h in range(heads):
                part = scores[:, h * n : (h + 1) * n]
                part = jnp.exp2(part - jnp.max(part, axis=1, keepdims=True))
                e_ref[:, h * n : (h + 1) * n] = part.astype(BF)
        else:
            e_ref[...] = jnp.exp2(scores).astype(BF)
        yield
        summed = dot(e_ref[...], vaug[...])
        total = summed[:, channels:]
        if not shifted:
            fits = (total > 1.0 / SAFE) & (total < SAFE)
            off_ref[...] += fold_rows(jnp.where(fits, 0.0, 1.0))
        recip = 1.0 / total
        att = summed[:, :channels] * recip
        d_att = d_out * gate
        d_gate = d_att * att * (1.0 - gate)
        d_att_b = (d_att * recip).astype(BF)
        d_att_f = d_att_b.astype(F32)
        gi = lax.broadcasted_iota(jnp.int32, (2 * channels, channels), 0) % channels
        gj = lax.broadcasted_iota(jnp.int32, (2 * channels, channels), 1)
        group = jnp.where((gi // size == gj // size) & (gj % size < 2), -1.0, 0.0).astype(BF)
        row_dot = dot(halves(d_att_f * att), group)
        row_hi = row_dot.astype(BF).astype(F32)
        row_lanes = jnp.where(lane % size == 0, row_hi, row_dot - row_hi).astype(BF)
        yield
        d_probs = dot(jnp.concatenate([d_att_b, row_lanes], axis=1), vaug[...], NT)
        ds = e_ref[...].astype(F32) * d_probs
        if wait:
            total_copy().wait()
        bacc_ref[...] += ds
        ds_ref[...] = ds.astype(BF)
        yield
        d_query = dot(ds_ref[...], kbd[...]) * (1.0 / math.sqrt(size))
        q_t, d_att_t = q_f.T.astype(BF), d_att_f.T.astype(BF)
        dk_t, dv_t = [], []
        for p in range(heads // 2):
            rows = slice(2 * p * size, 2 * (p + 1) * size)
            lanes = slice(2 * p * n, 2 * (p + 1) * n)
            both = dot(q_t[rows], ds_ref[:, lanes])
            dk_t += [both[:size, :n], both[size:, n:]]
            both = dot(d_att_t[rows], e_ref[:, lanes])
            dv_t += [both[:size, :n], both[size:, n:]]
        d_key = (jnp.concatenate(dk_t, axis=0) * LN2).T
        d_value = jnp.concatenate(dv_t, axis=0).T
        yield
        d_proj = jnp.concatenate([g.astype(BF) for g in (d_query, d_key, d_value, d_gate)], axis=1)
        dn = dot(d_proj, wpt_ref[...])
        out_ref[:, skip_out + j] = dn.reshape(src, n // src, channels).astype(BF)
        gated = gate * att
        wacc_ref[:, : 4 * channels] += dot(normed_f.T.astype(BF), d_proj)
        wacc_ref[:, 4 * channels :] += dot(gated.T.astype(BF), cot)
        sacc_ref[0] += fold_rows(d_gate)
        sacc_ref[1] += fold_rows(dn * xhat)
        sacc_ref[2] += fold_rows(dn)

    ahead = [
        column(step * group + u, False, u % SLOTS, not first and u == 0) for u in range(group)
    ]
    for turn in range(STAGES + LAG * (group - 1)):
        for u in range(group):
            if LAG * u <= turn < STAGES + LAG * u:
                next(ahead[u], None)

    @pl.when(step == cols // group - 1)
    def _():
        @pl.when(jnp.max(off_ref[...]) > 0.0)
        def _():
            begin()
            if not first:
                total_copy().wait()

            @pl.loop(0, cols)
            def _(j):
                for _ in column(j, True, 0):
                    pass

        if not first and not last:
            early_copy().wait()
        if last:
            for h in range(heads):
                for t in range(thirds):
                    plane = bacc_ref[t * channels : (t + 1) * channels, h * n : (h + 1) * n].T
                    out_ref[:, h * thirds + t] = plane.reshape(src, n // src, channels).astype(BF)
            terms = []
            for w in range(5):
                part = wacc_ref[:, w * channels : (w + 1) * channels].reshape(src, -1, channels)
                terms.append(part.astype(BF).astype(F32))
                terms.append(part - terms[-1])
            terms += [jnp.zeros_like(terms[0])] * 2
            for w in range(SHARES):
                three = jnp.concatenate(terms[3 * w : 3 * w + 3], axis=1)
                out_ref[:, slots + w] = three.astype(BF)


def whole(shape):
    return pl.BlockSpec(shape, lambda j: (0,) * len(shape))


def columns_call(first, last, col0, cols, group, length, own, moved, state, weights, heads):
    src, _, rows, channels = moved.shape
    n = src * rows
    slots = heads * n // channels
    smem = pl.BlockSpec(memory_space=pltpu.SMEM)
    plane = jax.ShapeDtypeStruct((n, heads * n), F32)
    wide = jax.ShapeDtypeStruct((channels, 5 * channels), F32)
    outs = [
        jax.ShapeDtypeStruct((src, cols + (slots + SHARES if last else col0), rows, channels), BF),
        jax.ShapeDtypeStruct((3, 8, channels), F32),
    ]
    outs += ([] if last else [plane, wide]) + ([plane] if first else [])
    inputs = (moved, *state, *weights)
    anywhere = pl.BlockSpec(memory_space=pl.ANY)
    in_specs = [smem, smem] + [whole(a.shape) for a in inputs]
    if not first:
        in_specs[4] = anywhere
    if len(state) > 4:
        in_specs[7] = anywhere
    return pl.pallas_call(
        functools.partial(columns_kernel, heads, first, last, col0, cols, group),
        grid=(cols // group,),
        in_specs=in_specs,
        out_specs=[whole(o.shape) for o in outs],
        out_shape=outs,
        scratch_shapes=[
            pltpu.VMEM((SLOTS, n, heads * n), BF),
            pltpu.VMEM((SLOTS, n, heads * n), BF),
            pltpu.VMEM((SLOTS, heads * n, channels), BF),
            pltpu.VMEM((SLOTS, heads * n, 2 * channels), BF),
            pltpu.VMEM((8, channels), F32),
            pltpu.SemaphoreType.DMA((2,)),
        ]
        + ([pltpu.VMEM(o.shape, F32) for o in (plane, wide)] if last else []),
        compiler_params=pltpu.CompilerParams(
            vmem_limit_bytes=56 * MIB, dimension_semantics=("arbitrary",)
        ),
        cost_estimate=pl.CostEstimate(
            flops=cols * 4 * 10**9, bytes_accessed=cols * n * channels * 6, transcendentals=0
        ),
    )(length, own, *inputs)


def side_kernel(heads, pair_ref, parts_ref, gain_ref, shift_ref, wbt_ref, sacc_ref, sum_ref, share_ref):
    rows, n, channels = pair_ref.shape
    thirds = n // channels
    slots = heads * thirds
    total = jnp.sum(parts_ref[:, :slots].astype(F32), axis=0).astype(BF).astype(F32)
    for h in range(heads):
        for t in range(thirds):
            sum_ref[h, :, t * channels : (t + 1) * channels] = total[h * thirds + t]
    terms = []
    for w in range(SHARES):
        part = jnp.sum(parts_ref[:, slots + w].astype(F32), axis=0)
        terms += [part[:8], part[8:16], part[16:24]]
    for w in range(5):
        share_ref[w] = terms[2 * w] + terms[2 * w + 1]
    stats = jnp.zeros((heads, 2 * channels), F32)
    flat = jnp.zeros((heads, n), F32)
    for r in range(rows):
        xhat, _ = norm_parts(pair_ref[r])
        normed = (xhat * gain_ref[...] + shift_ref[...]).astype(BF)
        own = sum_ref[:, r, :]
        flat = flat + own
        stats = stats + dot(own.astype(BF), jnp.concatenate([normed, xhat.astype(BF)], axis=1))
    wide = wbt_ref[...].astype(F32)
    share_ref[5, 0:1, :] = jnp.sum(sacc_ref[0], axis=0, keepdims=True)
    gain_part = wide * stats[:, channels:]
    gain_all = jnp.sum(sacc_ref[1], axis=0, keepdims=True)
    share_ref[5, 1:2, :] = gain_all + jnp.sum(gain_part, axis=0, keepdims=True)
    shift_part = wide * jnp.sum(flat, axis=1, keepdims=True)
    shift_all = jnp.sum(sacc_ref[2], axis=0, keepdims=True)
    share_ref[5, 2:3, :] = shift_all + jnp.sum(shift_part, axis=0, keepdims=True)
    share_ref[5, 3 : 3 + heads, :] = stats[:, :channels]
    share_ref[5, 3 + heads :, :] = jnp.zeros((5 - heads, channels), F32)


def norm_back_kernel(first, pair_ref, sums_ref, gain_ref, wbt_ref, *refs):
    parts, out_ref, side_ref = refs[:2], refs[-2], refs[-1]
    rows, cols, channels = pair_ref.shape
    heads, n = sums_ref.shape[0], sums_ref.shape[2]
    step = pl.program_id(0)

    @pl.when(step == 0)
    def _():
        none = jnp.zeros((8 - heads, n), F32)
        span = side_ref.shape[1]
        for r in range(rows):
            own = jnp.concatenate([sums_ref[:, r, :], none], axis=0).T
            own = own[first * cols : first * cols + span, :heads].astype(BF)
            side_ref[r] = dot(own, wbt_ref[...])

    pieces = []
    for s in range(cols // rows):
        for ref, w in zip(parts, (sum(CHUNKS[:-1]), CHUNKS[-1])):
            pieces.append(ref[s, ref.shape[1] - w :].astype(F32))
    main = jnp.swapaxes(jnp.concatenate(pieces, axis=0), 0, 1)
    side = side_ref[:, pl.ds(pl.multiple_of(step * cols, cols), cols), :]
    d_normed = (main + side).astype(BF).astype(F32).reshape(rows * cols, channels)
    cells = pair_ref[...].astype(F32).reshape(rows * cols, channels).astype(BF)
    xhat, scale = norm_parts(cells)
    g = d_normed * gain_ref[...]
    dx = scale * (g - lane_mean(g) - xhat * lane_mean(g * xhat))
    out_ref[...] = dx.reshape(rows, cols, channels).astype(BF)


def final_kernel(heads, size, told_ref, proj_ref, gate_ref, biasw_ref, outw_ref, gain_ref, shift_ref):
    channels = told_ref.shape[-1]
    scale = 1.0 / size
    for w in range(5):
        part = told_ref[:, w].reshape(channels, channels) * scale
        if w < 4:
            proj_ref[:, w * channels : (w + 1) * channels] = part
        else:
            outw_ref[...] = part
    small = jnp.sum(told_ref[:, 5], axis=0) * scale
    gate_ref[...] = small[0:1]
    gain_ref[...] = small[1:2]
    shift_ref[...] = small[2:3]
    biasw_ref[...] = small[3 : 3 + heads]


def body(pair_rep, grad_out, crop_len, ln_gain, ln_bias, w_proj, gate_bias, w_bias, w_out):
    pair, cot = pair_rep[0], grad_out[0]
    rows, n, channels = pair.shape
    heads = w_bias.shape[1]
    src = n // rows
    slots = heads * n // channels
    own = (lax.axis_index("row") * rows).astype(jnp.int32).reshape(1)
    gain, shift = ln_gain.reshape(1, -1), ln_bias.reshape(1, -1)
    wbt = w_bias.T
    weights = (gain, shift, w_proj, w_proj.T, gate_bias.reshape(1, -1), w_out.T)

    def exchange(a, axis="row"):
        return lax.all_to_all(a, axis, 0, 0)

    def tell(a, axis):
        return exchange(jnp.broadcast_to(a[None], (lax.axis_size(axis), *a.shape)), axis)

    block = 2
    tile = block * rows
    lines = 8
    plane = pl.pallas_call(
        functools.partial(logits_kernel, heads),
        grid=(rows // lines,),
        in_specs=[pl.BlockSpec((lines, n, channels), lambda j: (j, 0, 0))]
        + [whole(a.shape) for a in (gain, shift, wbt)],
        out_specs=pl.BlockSpec((slots, lines, channels), lambda j: (0, j, 0)),
        out_shape=jax.ShapeDtypeStruct((slots, rows, channels), F32),
        compiler_params=pltpu.CompilerParams(vmem_limit_bytes=60 * MIB),
    )(pair, gain, shift, wbt)
    many = src // 2
    cells = pl.BlockSpec((rows, many * rows, channels), lambda j: (0, j, 0))

    def send(start, count, extra):
        deep = 2 * count + sum(a.shape[0] for a in extra)
        return pl.pallas_call(
            functools.partial(send_kernel, start, count),
            grid=(src // many,),
            in_specs=[cells, cells] + [whole(a.shape) for a in extra],
            out_specs=pl.BlockSpec((many, deep, rows, channels), lambda j: (j, 0, 0, 0)),
            out_shape=jax.ShapeDtypeStruct((src, deep, rows, channels), BF),
            compiler_params=pltpu.CompilerParams(vmem_limit_bytes=60 * MIB),
            cost_estimate=pl.CostEstimate(
                flops=5 * 10**9, bytes_accessed=3 * pair.size, transcendentals=0
            ),
        )(pair, cot, *extra)

    starts = [sum(CHUNKS[:c]) for c in range(len(CHUNKS))]
    sent = [send(a, w, (plane,) if a == 0 else ()) for a, w in zip(starts, CHUNKS)]
    moved = [exchange(a) for a in sent]
    state, back = (), []
    for c, (start, width, group, piece) in enumerate(zip(starts, CHUNKS, GROUPS, moved)):
        first, last = c == 0, c == len(CHUNKS) - 1
        out, sacc, *rest = columns_call(
            first, last, start, width, group, crop_len, own, piece, state, weights, heads
        )
        if not last:
            plane = rest[2] if first else state[0]
            state = (plane, rest[0], rest[1], sacc)
            if c == len(CHUNKS) - 2:
                early = exchange(out)
            else:
                state += (out,)
    out, early = lax.optimization_barrier((out, early))
    bundle = exchange(out)
    back = (early, bundle)

    sums, share = pl.pallas_call(
        functools.partial(side_kernel, heads),
        grid=(1,),
        in_specs=[
            whole(pair.shape),
            pl.BlockSpec((src, slots + SHARES, rows, channels), lambda j: (0, 0, 0, 0)),
        ]
        + [whole(a.shape) for a in (gain, shift, wbt, sacc)],
        out_specs=[whole((heads, rows, n)), whole((6, 8, channels))],
        out_shape=[
            jax.ShapeDtypeStruct((heads, rows, n), F32),
            jax.ShapeDtypeStruct((6, 8, channels), F32),
        ],
        compiler_params=pltpu.CompilerParams(vmem_limit_bytes=40 * MIB),
    )(pair, bundle, gain, shift, wbt, sacc)
    def norm_back(first, steps, *written):
        place = lambda j: (0, j + first, 0)
        inputs = (pair, sums, gain, wbt, *back)
        return pl.pallas_call(
            functools.partial(norm_back_kernel, first),
            grid=(steps,),
            in_specs=[pl.BlockSpec((rows, tile, channels), place)]
            + [whole(a.shape) for a in (sums, gain, wbt)]
            + [pl.BlockSpec((block, *a.shape[1:]), lambda j: (j + first, 0, 0, 0)) for a in back]
            + [pl.BlockSpec(memory_space=pl.ANY)] * len(written),
            out_specs=pl.BlockSpec((rows, tile, channels), place),
            out_shape=jax.ShapeDtypeStruct(pair.shape, BF),
            scratch_shapes=[pltpu.VMEM((rows, steps * tile, channels), F32)],
            input_output_aliases={len(inputs): 0} if written else {},
            compiler_params=pltpu.CompilerParams(vmem_limit_bytes=60 * MIB),
            cost_estimate=pl.CostEstimate(
                flops=6 * 10**9, bytes_accessed=2 * pair.size, transcendentals=0
            ),
        )(*inputs, *written)

    blocks = n // tile
    share = tell(share, "dp")
    pair_grad = norm_back(0, blocks // 2)
    share, pair_grad = lax.optimization_barrier((share, pair_grad))
    told = tell(jnp.sum(share, axis=0), "row")
    pair_grad = norm_back(blocks // 2, blocks - blocks // 2, pair_grad)
    proj, gate, biasw, outw, gain_sum, shift_sum = pl.pallas_call(
        functools.partial(final_kernel, heads, n),
        out_shape=[
            jax.ShapeDtypeStruct(s, F32)
            for s in (
                w_proj.shape,
                (1, channels),
                (heads, channels),
                w_out.shape,
                (1, channels),
                (1, channels),
            )
        ],
    )(told)
    return (
        pair_grad[None],
        proj,
        gate.reshape(-1),
        biasw.T,
        outw,
        gain_sum.reshape(-1),
        shift_sum.reshape(-1),
    )


def solution(mesh):
    placed = (
        P("dp", "row", None, None),
        P("dp", "row", None, None),
        P("dp"),
        P(),
        P(),
        P(),
        P(),
        P(),
        P(),
    )
    return jax.shard_map(
        body,
        mesh=mesh,
        in_specs=placed,
        out_specs=(P("dp", "row", None, None), P(), P(), P(), P(), P(), P()),
        check_vma=False,
    )
```

```python
import functools
import math

import jax
import jax.numpy as jnp
from jax import lax
from jax.experimental import pallas as pl
from jax.experimental.pallas import tpu as pltpu
from jax.sharding import PartitionSpec as P

F32, BF = jnp.float32, jnp.bfloat16
EPSILON = 1e-05
LOG2E = 1.4426950408889634
LN2 = 0.6931471805599453
NN = (((1,), (0,)), ((), ()))
NT = (((1,), (1,)), ((), ()))
TN = (((0,), (0,)), ((), ()))
MIB = 2**20
DEAD = -1e30
CHUNKS = (6, 9, 9)
SAFE = 1e28
GROUPS = (3, 9, 9)
SHARES = 4
SLOTS, STAGES, LAG = 4, 6, 2


def dot(a, b, dims=NN):
    return lax.dot_general(a, b, dims, preferred_element_type=F32)


def halves(a):
    high = a.astype(BF)
    return jnp.concatenate([high, (a - high.astype(F32)).astype(BF)], axis=1)


def lane_mean(a):
    channels = a.shape[1]
    a = a if a.dtype == BF else halves(a)
    return dot(a, jnp.full((a.shape[1], channels), 1.0 / channels, BF))


def norm_parts(x):
    centered = x.astype(F32) - lane_mean(x)
    scale = lax.rsqrt(lane_mean(centered * centered) + EPSILON)
    return centered * scale, scale


def fold_rows(a):
    return jnp.sum(a.reshape(a.shape[0] // 8, 8, a.shape[1]), axis=0)


def logits_kernel(heads, pair_ref, gain_ref, shift_ref, wbt_ref, out_ref):
    rows, n, channels = pair_ref.shape
    xhat, _ = norm_parts(pair_ref[...].astype(F32).reshape(rows * n, channels).astype(BF))
    normed = (xhat * gain_ref[...] + shift_ref[...]).astype(BF)
    logits = dot(wbt_ref[...], normed, NT)
    for r in range(rows):
        for h in range(heads):
            for t in range(n // channels):
                start = r * n + t * channels
                piece = logits[h : h + 1, start : start + channels]
                out_ref[h * (n // channels) + t, r : r + 1, :] = piece


def send_kernel(start, count, pair_ref, cot_ref, *refs):
    out = refs[-1]
    block, rows = out.shape[0], pair_ref.shape[0]
    skip = out.shape[1] - 2 * count
    if skip:
        for s in range(block):
            out[s, :skip] = refs[0][...].astype(BF)
    for a, ref in enumerate((pair_ref, cot_ref)):
        cells = ref[...].astype(F32)
        for s in range(block):
            first = s * rows + start
            own = jnp.swapaxes(cells[:, first : first + count], 0, 1)
            out[s, skip + a * count : skip + (a + 1) * count] = own.astype(BF)


def columns_kernel(heads, first, last, col0, cols, group, len_ref, own_ref, cells_ref, *refs):
    if not first:
        (bias_ref, bacc_in, wacc_in, sacc_in), refs = refs[:4], refs[4:]
    if not first and not last:
        early_ref, refs = refs[0], refs[1:]
    gain_ref, shift_ref, wp_ref, wpt_ref, gb_ref, wot_ref = refs[:6]
    refs = refs[6:]
    out_ref, sacc_ref = refs[:2]
    refs = refs[2:]
    if not last:
        (bacc_ref, wacc_ref), refs = refs[:2], refs[2:]
    if first:
        bias_ref, refs = refs[0], refs[1:]
    e_all, ds_all, kbd_all, vaug_all, off_ref, sems = refs[:6]
    refs = refs[6:]
    if last:
        bacc_ref, wacc_ref = refs
    step = pl.program_id(0)
    n, channels = bacc_ref.shape[0], wp_ref.shape[0]
    size, thirds, src = channels // heads, n // channels, cells_ref.shape[0]
    slots = heads * thirds
    skip_in = slots if first else 0
    skip_out = slots + SHARES if last else out_ref.shape[1] - cols
    lane = lax.broadcasted_iota(jnp.int32, (1, channels), 1)
    masks = [jnp.where(lane // size == h, 1.0, 0.0).astype(BF) for h in range(heads)]
    length = len_ref[0]

    def total_copy():
        return pltpu.make_async_copy(bacc_in, bacc_ref, sems.at[0])

    def early_copy():
        return pltpu.make_async_copy(early_ref, out_ref.at[:, :skip_out], sems.at[1])

    def begin():
        if first:
            bacc_ref[...] = jnp.zeros_like(bacc_ref)
            wacc_ref[...] = jnp.zeros_like(wacc_ref)
            sacc_ref[...] = jnp.zeros_like(sacc_ref)
        else:
            total_copy().start()
            wacc_ref[...] = wacc_in[...]
            sacc_ref[...] = sacc_in[...]

    @pl.when(step == 0)
    def _():
        begin()
        if first:
            kpos = lax.broadcasted_iota(jnp.int32, (1, n), 1)
            for h in range(heads):
                for t in range(thirds):
                    plane = cells_ref[:, h * thirds + t].astype(F32).reshape(n, channels)
                    bias_ref[t * channels : (t + 1) * channels, h * n : (h + 1) * n] = jnp.where(
                        kpos < length, plane.T * LOG2E, DEAD
                    )
        elif not last:
            early_copy().start()
        off_ref[...] = jnp.zeros_like(off_ref)
        for h in range(heads):
            for u in range(SLOTS):
                vaug_all[u, h * n : (h + 1) * n, channels:] = jnp.broadcast_to(masks[h], (n, channels))

    def column(j, shifted, slot, wait=False):
        e_ref, ds_ref, kbd, vaug = e_all.at[slot], ds_all.at[slot], kbd_all.at[slot], vaug_all.at[slot]
        xhat, _ = norm_parts(cells_ref[:, skip_in + j].astype(F32).reshape(n, channels).astype(BF))
        normed_f = xhat * gain_ref[...] + shift_ref[...]
        proj = dot(normed_f.astype(BF), wp_ref[...])
        q_f = proj[:, :channels] * (LOG2E / math.sqrt(size))
        k = proj[:, channels : 2 * channels].astype(BF)
        v = proj[:, 2 * channels : 3 * channels].astype(BF)
        gate = jax.nn.sigmoid(proj[:, 3 * channels :] + gb_ref[...])
        for h in range(heads):
            kbd[h * n : (h + 1) * n, :] = k * masks[h]
            vaug[h * n : (h + 1) * n, :channels] = v * masks[h]
        live = lax.broadcasted_iota(jnp.int32, (n, 1), 0) < length
        live = live & (own_ref[0] + col0 + j < length)
        cot = cells_ref[:, skip_in + cols + j].astype(F32).reshape(n, channels)
        cot = jnp.where(live, cot, 0.0).astype(BF)
        d_out = dot(cot, wot_ref[...])

        yield
        scores = dot(q_f.astype(BF), kbd[...], NT) + bias_ref[...]
        if shifted:
            for h in range(heads):
                part = scores[:, h * n : (h + 1) * n]
                part = jnp.exp2(part - jnp.max(part, axis=1, keepdims=True))
                e_ref[:, h * n : (h + 1) * n] = part.astype(BF)
        else:
            e_ref[...] = jnp.exp2(scores).astype(BF)
        yield
        summed = dot(e_ref[...], vaug[...])
        total = summed[:, channels:]
        if not shifted:
            fits = (total > 1.0 / SAFE) & (total < SAFE)
            off_ref[...] += fold_rows(jnp.where(fits, 0.0, 1.0))
        recip = 1.0 / total
        att = summed[:, :channels] * recip
        d_att = d_out * gate
        d_gate = d_att * att * (1.0 - gate)
        d_att_b = (d_att * recip).astype(BF)
        d_att_f = d_att_b.astype(F32)
        gi = lax.broadcasted_iota(jnp.int32, (2 * channels, channels), 0) % channels
        gj = lax.broadcasted_iota(jnp.int32, (2 * channels, channels), 1)
        group = jnp.where((gi // size == gj // size) & (gj % size < 2), -1.0, 0.0).astype(BF)
        row_dot = dot(halves(d_att_f * att), group)
        row_hi = row_dot.astype(BF).astype(F32)
        row_lanes = jnp.where(lane % size == 0, row_hi, row_dot - row_hi).astype(BF)
        yield
        d_probs = dot(jnp.concatenate([d_att_b, row_lanes], axis=1), vaug[...], NT)
        ds = e_ref[...].astype(F32) * d_probs
        if wait:
            total_copy().wait()
        bacc_ref[...] += ds
        ds_ref[...] = ds.astype(BF)
        yield
        d_query = dot(ds_ref[...], kbd[...]) * (1.0 / math.sqrt(size))
        q_t, d_att_t = q_f.T.astype(BF), d_att_f.T.astype(BF)
        dk_t, dv_t = [], []
        for p in range(heads // 2):
            rows = slice(2 * p * size, 2 * (p + 1) * size)
            lanes = slice(2 * p * n, 2 * (p + 1) * n)
            both = dot(q_t[rows], ds_ref[:, lanes])
            dk_t += [both[:size, :n], both[size:, n:]]
            both = dot(d_att_t[rows], e_ref[:, lanes])
            dv_t += [both[:size, :n], both[size:, n:]]
        d_key = (jnp.concatenate(dk_t, axis=0) * LN2).T
        d_value = jnp.concatenate(dv_t, axis=0).T
        yield
        d_proj = jnp.concatenate([g.astype(BF) for g in (d_query, d_key, d_value, d_gate)], axis=1)
        dn = dot(d_proj, wpt_ref[...])
        out_ref[:, skip_out + j] = dn.reshape(src, n // src, channels).astype(BF)
        gated = gate * att
        wacc_ref[:, : 4 * channels] += dot(normed_f.T.astype(BF), d_proj)
        wacc_ref[:, 4 * channels :] += dot(gated.T.astype(BF), cot)
        sacc_ref[0] += fold_rows(d_gate)
        sacc_ref[1] += fold_rows(dn * xhat)
        sacc_ref[2] += fold_rows(dn)

    ahead = [
        column(step * group + u, False, u % SLOTS, not first and u == 0) for u in range(group)
    ]
    for turn in range(STAGES + LAG * (group - 1)):
        for u in range(group):
            if LAG * u <= turn < STAGES + LAG * u:
                next(ahead[u], None)

    @pl.when(step == cols // group - 1)
    def _():
        @pl.when(jnp.max(off_ref[...]) > 0.0)
        def _():
            begin()
            if not first:
                total_copy().wait()

            @pl.loop(0, cols)
            def _(j):
                for _ in column(j, True, 0):
                    pass

        if not first and not last:
            early_copy().wait()
        if last:
            for h in range(heads):
                for t in range(thirds):
                    plane = bacc_ref[t * channels : (t + 1) * channels, h * n : (h + 1) * n].T
                    out_ref[:, h * thirds + t] = plane.reshape(src, n // src, channels).astype(BF)
            terms = []
            for w in range(5):
                part = wacc_ref[:, w * channels : (w + 1) * channels].reshape(src, -1, channels)
                terms.append(part.astype(BF).astype(F32))
                terms.append(part - terms[-1])
            terms += [jnp.zeros_like(terms[0])] * 2
            for w in range(SHARES):
                three = jnp.concatenate(terms[3 * w : 3 * w + 3], axis=1)
                out_ref[:, slots + w] = three.astype(BF)


def whole(shape):
    return pl.BlockSpec(shape, lambda j: (0,) * len(shape))


def columns_call(first, last, col0, cols, group, length, own, moved, state, weights, heads):
    src, _, rows, channels = moved.shape
    n = src * rows
    slots = heads * n // channels
    smem = pl.BlockSpec(memory_space=pltpu.SMEM)
    plane = jax.ShapeDtypeStruct((n, heads * n), F32)
    wide = jax.ShapeDtypeStruct((channels, 5 * channels), F32)
    outs = [
        jax.ShapeDtypeStruct((src, cols + (slots + SHARES if last else col0), rows, channels), BF),
        jax.ShapeDtypeStruct((3, 8, channels), F32),
    ]
    outs += ([] if last else [plane, wide]) + ([plane] if first else [])
    inputs = (moved, *state, *weights)
    anywhere = pl.BlockSpec(memory_space=pl.ANY)
    in_specs = [smem, smem] + [whole(a.shape) for a in inputs]
    if not first:
        in_specs[4] = anywhere
    if len(state) > 4:
        in_specs[7] = anywhere
    return pl.pallas_call(
        functools.partial(columns_kernel, heads, first, last, col0, cols, group),
        grid=(cols // group,),
        in_specs=in_specs,
        out_specs=[whole(o.shape) for o in outs],
        out_shape=outs,
        scratch_shapes=[
            pltpu.VMEM((SLOTS, n, heads * n), BF),
            pltpu.VMEM((SLOTS, n, heads * n), BF),
            pltpu.VMEM((SLOTS, heads * n, channels), BF),
            pltpu.VMEM((SLOTS, heads * n, 2 * channels), BF),
            pltpu.VMEM((8, channels), F32),
            pltpu.SemaphoreType.DMA((2,)),
        ]
        + ([pltpu.VMEM(o.shape, F32) for o in (plane, wide)] if last else []),
        compiler_params=pltpu.CompilerParams(
            vmem_limit_bytes=56 * MIB, dimension_semantics=("arbitrary",)
        ),
        cost_estimate=pl.CostEstimate(
            flops=cols * 4 * 10**9, bytes_accessed=cols * n * channels * 6, transcendentals=0
        ),
    )(length, own, *inputs)


def normed_kernel(pair_ref, gain_ref, shift_ref, out_ref):
    rows, n, channels = pair_ref.shape
    xhat, _ = norm_parts(pair_ref[...].astype(F32).reshape(rows * n, channels).astype(BF))
    normed = xhat * gain_ref[...] + shift_ref[...]
    out_ref[:, :, :channels] = normed.reshape(rows, n, channels).astype(BF)
    out_ref[:, :, channels:] = xhat.reshape(rows, n, channels).astype(BF)


def side_kernel(heads, normed_ref, parts_ref, wbt_ref, sacc_ref, sum_ref, told_ref):
    rows, n, channels = parts_ref.shape[2], sum_ref.shape[2], parts_ref.shape[3]
    thirds = n // channels
    slots = heads * thirds
    share_ref = told_ref.at[0]
    total = jnp.sum(parts_ref[:, :slots].astype(F32), axis=0).astype(BF).astype(F32)
    for h in range(heads):
        for t in range(thirds):
            sum_ref[h, :, t * channels : (t + 1) * channels] = total[h * thirds + t]
    terms = []
    for w in range(SHARES):
        part = jnp.sum(parts_ref[:, slots + w].astype(F32), axis=0)
        terms += [part[:8], part[8:16], part[16:24]]
    for w in range(5):
        share_ref[w] = terms[2 * w] + terms[2 * w + 1]
    stats = jnp.zeros((heads, 2 * channels), F32)
    flat = jnp.zeros((heads, n), F32)
    for r in range(rows):
        own = sum_ref[:, r, :]
        flat = flat + own
        stats = stats + dot(own.astype(BF), normed_ref[r])
    wide = wbt_ref[...].astype(F32)
    share_ref[5, 0:1, :] = jnp.sum(sacc_ref[0], axis=0, keepdims=True)
    gain_part = wide * stats[:, channels:]
    gain_all = jnp.sum(sacc_ref[1], axis=0, keepdims=True)
    share_ref[5, 1:2, :] = gain_all + jnp.sum(gain_part, axis=0, keepdims=True)
    shift_part = wide * jnp.sum(flat, axis=1, keepdims=True)
    shift_all = jnp.sum(sacc_ref[2], axis=0, keepdims=True)
    share_ref[5, 2:3, :] = shift_all + jnp.sum(shift_part, axis=0, keepdims=True)
    share_ref[5, 3 : 3 + heads, :] = stats[:, :channels]
    share_ref[5, 3 + heads :, :] = jnp.zeros((5 - heads, channels), F32)
    for d in range(1, told_ref.shape[0]):
        told_ref[d] = share_ref[...]


def norm_back_kernel(first, pair_ref, sums_ref, gain_ref, wbt_ref, *refs):
    parts, out_ref, side_ref = refs[:2], refs[-2], refs[-1]
    rows, cols, channels = pair_ref.shape
    heads, n = sums_ref.shape[0], sums_ref.shape[2]
    step = pl.program_id(0)

    @pl.when(step == 0)
    def _():
        none = jnp.zeros((8 - heads, n), F32)
        span = side_ref.shape[1]
        for r in range(rows):
            own = jnp.concatenate([sums_ref[:, r, :], none], axis=0).T
            own = own[first * cols : first * cols + span, :heads].astype(BF)
            side_ref[r] = dot(own, wbt_ref[...])

    pieces = []
    for s in range(cols // rows):
        for ref, w in zip(parts, (sum(CHUNKS[:-1]), CHUNKS[-1])):
            pieces.append(ref[s, ref.shape[1] - w :].astype(F32))
    main = jnp.swapaxes(jnp.concatenate(pieces, axis=0), 0, 1)
    side = side_ref[:, pl.ds(pl.multiple_of(step * cols, cols), cols), :]
    d_normed = (main + side).astype(BF).astype(F32).reshape(rows * cols, channels)
    cells = pair_ref[...].astype(F32).reshape(rows * cols, channels).astype(BF)
    xhat, scale = norm_parts(cells)
    g = d_normed * gain_ref[...]
    dx = scale * (g - lane_mean(g) - xhat * lane_mean(g * xhat))
    out_ref[...] = dx.reshape(rows, cols, channels).astype(BF)


def final_kernel(heads, size, told_ref, proj_ref, gate_ref, biasw_ref, outw_ref, gain_ref, shift_ref):
    channels = told_ref.shape[-1]
    scale = 1.0 / size
    for w in range(5):
        part = told_ref[:, w].reshape(channels, channels) * scale
        if w < 4:
            proj_ref[:, w * channels : (w + 1) * channels] = part
        else:
            outw_ref[...] = part
    small = jnp.sum(told_ref[:, 5], axis=0) * scale
    gate_ref[...] = small[0:1]
    gain_ref[...] = small[1:2]
    shift_ref[...] = small[2:3]
    biasw_ref[...] = small[3 : 3 + heads]


def body(pair_rep, grad_out, crop_len, ln_gain, ln_bias, w_proj, gate_bias, w_bias, w_out):
    pair, cot = pair_rep[0], grad_out[0]
    rows, n, channels = pair.shape
    heads = w_bias.shape[1]
    src = n // rows
    slots = heads * n // channels
    own = (lax.axis_index("row") * rows).astype(jnp.int32).reshape(1)
    gain, shift = ln_gain.reshape(1, -1), ln_bias.reshape(1, -1)
    wbt = w_bias.T
    weights = (gain, shift, w_proj, w_proj.T, gate_bias.reshape(1, -1), w_out.T)

    def exchange(a, axis="row"):
        return lax.all_to_all(a, axis, 0, 0)

    def tell(a, axis):
        return exchange(jnp.broadcast_to(a[None], (lax.axis_size(axis), *a.shape)), axis)

    block = 2
    tile = block * rows
    lines = 8
    plane = pl.pallas_call(
        functools.partial(logits_kernel, heads),
        grid=(rows // lines,),
        in_specs=[pl.BlockSpec((lines, n, channels), lambda j: (j, 0, 0))]
        + [whole(a.shape) for a in (gain, shift, wbt)],
        out_specs=pl.BlockSpec((slots, lines, channels), lambda j: (0, j, 0)),
        out_shape=jax.ShapeDtypeStruct((slots, rows, channels), F32),
        compiler_params=pltpu.CompilerParams(vmem_limit_bytes=60 * MIB),
    )(pair, gain, shift, wbt)
    many = src // 2
    both = pl.pallas_call(
        normed_kernel,
        grid=(rows // lines,),
        in_specs=[pl.BlockSpec((lines, n, channels), lambda j: (j, 0, 0))]
        + [whole(a.shape) for a in (gain, shift)],
        out_specs=pl.BlockSpec((lines, n, 2 * channels), lambda j: (j, 0, 0)),
        out_shape=jax.ShapeDtypeStruct((rows, n, 2 * channels), BF),
        compiler_params=pltpu.CompilerParams(vmem_limit_bytes=60 * MIB),
        cost_estimate=pl.CostEstimate(
            flops=5 * 10**9, bytes_accessed=6 * pair.size, transcendentals=0
        ),
    )(pair, gain, shift)
    cells = pl.BlockSpec((rows, many * rows, channels), lambda j: (0, j, 0))

    def send(start, count, extra):
        deep = 2 * count + sum(a.shape[0] for a in extra)
        return pl.pallas_call(
            functools.partial(send_kernel, start, count),
            grid=(src // many,),
            in_specs=[cells, cells] + [whole(a.shape) for a in extra],
            out_specs=pl.BlockSpec((many, deep, rows, channels), lambda j: (j, 0, 0, 0)),
            out_shape=jax.ShapeDtypeStruct((src, deep, rows, channels), BF),
            compiler_params=pltpu.CompilerParams(vmem_limit_bytes=60 * MIB),
            cost_estimate=pl.CostEstimate(
                flops=5 * 10**9, bytes_accessed=3 * pair.size, transcendentals=0
            ),
        )(pair, cot, *extra)

    starts = [sum(CHUNKS[:c]) for c in range(len(CHUNKS))]
    sent = [send(a, w, (plane,) if a == 0 else ()) for a, w in zip(starts, CHUNKS)]
    moved = [exchange(a) for a in sent]
    state, back = (), []
    for c, (start, width, group, piece) in enumerate(zip(starts, CHUNKS, GROUPS, moved)):
        first, last = c == 0, c == len(CHUNKS) - 1
        out, sacc, *rest = columns_call(
            first, last, start, width, group, crop_len, own, piece, state, weights, heads
        )
        if not last:
            plane = rest[2] if first else state[0]
            state = (plane, rest[0], rest[1], sacc)
            if c == len(CHUNKS) - 2:
                early = exchange(out)
            else:
                state += (out,)
    out, early = lax.optimization_barrier((out, early))
    bundle = exchange(out)
    back = (early, bundle)

    copies = lax.axis_size("dp")
    sums, share = pl.pallas_call(
        functools.partial(side_kernel, heads),
        grid=(1,),
        in_specs=[
            whole(both.shape),
            pl.BlockSpec((src, slots + SHARES, rows, channels), lambda j: (0, 0, 0, 0)),
        ]
        + [whole(a.shape) for a in (wbt, sacc)],
        out_specs=[whole((heads, rows, n)), whole((copies, 6, 8, channels))],
        out_shape=[
            jax.ShapeDtypeStruct((heads, rows, n), F32),
            jax.ShapeDtypeStruct((copies, 6, 8, channels), F32),
        ],
        compiler_params=pltpu.CompilerParams(vmem_limit_bytes=40 * MIB),
    )(both, bundle, wbt, sacc)
    def norm_back(first, steps, *written):
        place = lambda j: (0, j + first, 0)
        inputs = (pair, sums, gain, wbt, *back)
        return pl.pallas_call(
            functools.partial(norm_back_kernel, first),
            grid=(steps,),
            in_specs=[pl.BlockSpec((rows, tile, channels), place)]
            + [whole(a.shape) for a in (sums, gain, wbt)]
            + [pl.BlockSpec((block, *a.shape[1:]), lambda j: (j + first, 0, 0, 0)) for a in back]
            + [pl.BlockSpec(memory_space=pl.ANY)] * len(written),
            out_specs=pl.BlockSpec((rows, tile, channels), place),
            out_shape=jax.ShapeDtypeStruct(pair.shape, BF),
            scratch_shapes=[pltpu.VMEM((rows, steps * tile, channels), F32)],
            input_output_aliases={len(inputs): 0} if written else {},
            compiler_params=pltpu.CompilerParams(vmem_limit_bytes=60 * MIB),
            cost_estimate=pl.CostEstimate(
                flops=6 * 10**9, bytes_accessed=2 * pair.size, transcendentals=0
            ),
        )(*inputs, *written)

    blocks = n // tile
    share = exchange(share, "dp")
    pair_grad = norm_back(0, blocks // 2)
    share, pair_grad = lax.optimization_barrier((share, pair_grad))
    told = tell(jnp.sum(share, axis=0), "row")
    pair_grad = norm_back(blocks // 2, blocks - blocks // 2, pair_grad)
    proj, gate, biasw, outw, gain_sum, shift_sum = pl.pallas_call(
        functools.partial(final_kernel, heads, n),
        out_shape=[
            jax.ShapeDtypeStruct(s, F32)
            for s in (
                w_proj.shape,
                (1, channels),
                (heads, channels),
                w_out.shape,
                (1, channels),
                (1, channels),
            )
        ],
    )(told)
    return (
        pair_grad[None],
        proj,
        gate.reshape(-1),
        biasw.T,
        outw,
        gain_sum.reshape(-1),
        shift_sum.reshape(-1),
    )


def solution(mesh):
    placed = (
        P("dp", "row", None, None),
        P("dp", "row", None, None),
        P("dp"),
        P(),
        P(),
        P(),
        P(),
        P(),
        P(),
    )
    return jax.shard_map(
        body,
        mesh=mesh,
        in_specs=placed,
        out_specs=(P("dp", "row", None, None), P(), P(), P(), P(), P(), P()),
        check_vma=False,
    )
```

```python
import functools
import math

import jax
import jax.numpy as jnp
from jax import lax
from jax.experimental import pallas as pl
from jax.experimental.pallas import tpu as pltpu
from jax.sharding import PartitionSpec as P

F32, BF = jnp.float32, jnp.bfloat16
EPSILON = 1e-05
LOG2E = 1.4426950408889634
LN2 = 0.6931471805599453
NN = (((1,), (0,)), ((), ()))
NT = (((1,), (1,)), ((), ()))
TN = (((0,), (0,)), ((), ()))
MIB = 2**20
DEAD = -1e30
CHUNKS = (6, 9, 9)
SAFE = 1e28
GROUPS = (3, 9, 9)
SHARES = 4
SLOTS, STAGES, LAG = 4, 6, 2


def dot(a, b, dims=NN):
    return lax.dot_general(a, b, dims, preferred_element_type=F32)


def halves(a):
    high = a.astype(BF)
    return jnp.concatenate([high, (a - high.astype(F32)).astype(BF)], axis=1)


def lane_mean(a):
    channels = a.shape[1]
    a = a if a.dtype == BF else halves(a)
    return dot(a, jnp.full((a.shape[1], channels), 1.0 / channels, BF))


def norm_parts(x):
    centered = x.astype(F32) - lane_mean(x)
    scale = lax.rsqrt(lane_mean(centered * centered) + EPSILON)
    return centered * scale, scale


def fold_rows(a):
    return jnp.sum(a.reshape(a.shape[0] // 8, 8, a.shape[1]), axis=0)


def logits_kernel(heads, pair_ref, gain_ref, shift_ref, wbt_ref, out_ref):
    rows, n, channels = pair_ref.shape
    xhat, _ = norm_parts(pair_ref[...].astype(F32).reshape(rows * n, channels).astype(BF))
    normed = (xhat * gain_ref[...] + shift_ref[...]).astype(BF)
    logits = dot(wbt_ref[...], normed, NT)
    for r in range(rows):
        for h in range(heads):
            for t in range(n // channels):
                start = r * n + t * channels
                piece = logits[h : h + 1, start : start + channels]
                out_ref[h * (n // channels) + t, r : r + 1, :] = piece


def send_kernel(start, count, pair_ref, cot_ref, *refs):
    out = refs[-1]
    block, rows = out.shape[0], pair_ref.shape[0]
    skip = out.shape[1] - 2 * count
    if skip:
        for s in range(block):
            out[s, :skip] = refs[0][...].astype(BF)
    for a, ref in enumerate((pair_ref, cot_ref)):
        cells = ref[...].astype(F32)
        for s in range(block):
            first = s * rows + start
            own = jnp.swapaxes(cells[:, first : first + count], 0, 1)
            out[s, skip + a * count : skip + (a + 1) * count] = own.astype(BF)


def columns_kernel(heads, first, last, col0, cols, group, len_ref, own_ref, cells_ref, *refs):
    if not first:
        (bias_ref, bacc_in, wacc_in, sacc_in), refs = refs[:4], refs[4:]
    if not first and not last:
        early_ref, refs = refs[0], refs[1:]
    gain_ref, shift_ref, wp_ref, wpt_ref, gb_ref, wot_ref = refs[:6]
    refs = refs[6:]
    out_ref, sacc_ref = refs[:2]
    refs = refs[2:]
    if not last:
        (bacc_ref, wacc_ref), refs = refs[:2], refs[2:]
    if first:
        bias_ref, refs = refs[0], refs[1:]
    e_all, ds_all, kbd_all, vaug_all, off_ref, sems = refs[:6]
    refs = refs[6:]
    if last:
        bacc_ref, wacc_ref = refs
    step = pl.program_id(0)
    n, channels = bacc_ref.shape[0], wp_ref.shape[0]
    size, thirds, src = channels // heads, n // channels, cells_ref.shape[0]
    slots = heads * thirds
    skip_in = slots if first else 0
    skip_out = slots + SHARES if last else out_ref.shape[1] - cols
    lane = lax.broadcasted_iota(jnp.int32, (1, channels), 1)
    masks = [jnp.where(lane // size == h, 1.0, 0.0).astype(BF) for h in range(heads)]
    length = len_ref[0]

    def total_copy():
        return pltpu.make_async_copy(bacc_in, bacc_ref, sems.at[0])

    def early_copy():
        return pltpu.make_async_copy(early_ref, out_ref.at[:, :skip_out], sems.at[1])

    def begin():
        if first:
            bacc_ref[...] = jnp.zeros_like(bacc_ref)
            wacc_ref[...] = jnp.zeros_like(wacc_ref)
            sacc_ref[...] = jnp.zeros_like(sacc_ref)
        else:
            total_copy().start()
            wacc_ref[...] = wacc_in[...]
            sacc_ref[...] = sacc_in[...]

    @pl.when(step == 0)
    def _():
        begin()
        if first:
            kpos = lax.broadcasted_iota(jnp.int32, (1, n), 1)
            for h in range(heads):
                for t in range(thirds):
                    plane = cells_ref[:, h * thirds + t].astype(F32).reshape(n, channels)
                    bias_ref[t * channels : (t + 1) * channels, h * n : (h + 1) * n] = jnp.where(
                        kpos < length, plane.T * LOG2E, DEAD
                    )
        elif not last:
            early_copy().start()
        off_ref[...] = jnp.zeros_like(off_ref)
        for h in range(heads):
            for u in range(SLOTS):
                vaug_all[u, h * n : (h + 1) * n, channels:] = jnp.broadcast_to(masks[h], (n, channels))

    def column(j, shifted, slot, wait=False):
        e_ref, ds_ref, kbd, vaug = e_all.at[slot], ds_all.at[slot], kbd_all.at[slot], vaug_all.at[slot]
        xhat, _ = norm_parts(cells_ref[:, skip_in + j].astype(F32).reshape(n, channels).astype(BF))
        normed_f = xhat * gain_ref[...] + shift_ref[...]
        proj = dot(normed_f.astype(BF), wp_ref[...])
        q_f = proj[:, :channels] * (LOG2E / math.sqrt(size))
        k = proj[:, channels : 2 * channels].astype(BF)
        v = proj[:, 2 * channels : 3 * channels].astype(BF)
        gate = jax.nn.sigmoid(proj[:, 3 * channels :] + gb_ref[...])
        for h in range(heads):
            kbd[h * n : (h + 1) * n, :] = k * masks[h]
            vaug[h * n : (h + 1) * n, :channels] = v * masks[h]
        live = lax.broadcasted_iota(jnp.int32, (n, 1), 0) < length
        live = live & (own_ref[0] + col0 + j < length)
        cot = cells_ref[:, skip_in + cols + j].astype(F32).reshape(n, channels)
        cot = jnp.where(live, cot, 0.0).astype(BF)
        d_out = dot(cot, wot_ref[...])

        yield
        scores = dot(q_f.astype(BF), kbd[...], NT) + bias_ref[...]
        if shifted:
            for h in range(heads):
                part = scores[:, h * n : (h + 1) * n]
                part = jnp.exp2(part - jnp.max(part, axis=1, keepdims=True))
                e_ref[:, h * n : (h + 1) * n] = part.astype(BF)
        else:
            e_ref[...] = jnp.exp2(scores).astype(BF)
        yield
        summed = dot(e_ref[...], vaug[...])
        total = summed[:, channels:]
        if not shifted:
            fits = (total > 1.0 / SAFE) & (total < SAFE)
            off_ref[...] += fold_rows(jnp.where(fits, 0.0, 1.0))
        recip = 1.0 / total
        att = summed[:, :channels] * recip
        d_att = d_out * gate
        d_gate = d_att * att * (1.0 - gate)
        d_att_b = (d_att * recip).astype(BF)
        d_att_f = d_att_b.astype(F32)
        gi = lax.broadcasted_iota(jnp.int32, (2 * channels, channels), 0) % channels
        gj = lax.broadcasted_iota(jnp.int32, (2 * channels, channels), 1)
        group = jnp.where((gi // size == gj // size) & (gj % size < 2), -1.0, 0.0).astype(BF)
        row_dot = dot(halves(d_att_f * att), group)
        row_hi = row_dot.astype(BF).astype(F32)
        row_lanes = jnp.where(lane % size == 0, row_hi, row_dot - row_hi).astype(BF)
        yield
        d_probs = dot(jnp.concatenate([d_att_b, row_lanes], axis=1), vaug[...], NT)
        ds = e_ref[...].astype(F32) * d_probs
        if wait:
            total_copy().wait()
        bacc_ref[...] += ds
        ds_ref[...] = ds.astype(BF)
        yield
        d_query = dot(ds_ref[...], kbd[...]) * (1.0 / math.sqrt(size))
        q_t, d_att_t = q_f.T.astype(BF), d_att_f.T.astype(BF)
        dk_t, dv_t = [], []
        for p in range(heads // 2):
            rows = slice(2 * p * size, 2 * (p + 1) * size)
            lanes = slice(2 * p * n, 2 * (p + 1) * n)
            both = dot(q_t[rows], ds_ref[:, lanes])
            dk_t += [both[:size, :n], both[size:, n:]]
            both = dot(d_att_t[rows], e_ref[:, lanes])
            dv_t += [both[:size, :n], both[size:, n:]]
        d_key = (jnp.concatenate(dk_t, axis=0) * LN2).T
        d_value = jnp.concatenate(dv_t, axis=0).T
        yield
        d_proj = jnp.concatenate([g.astype(BF) for g in (d_query, d_key, d_value, d_gate)], axis=1)
        dn = dot(d_proj, wpt_ref[...])
        out_ref[:, skip_out + j] = dn.reshape(src, n // src, channels).astype(BF)
        gated = gate * att
        wacc_ref[:, : 4 * channels] += dot(normed_f.T.astype(BF), d_proj)
        wacc_ref[:, 4 * channels :] += dot(gated.T.astype(BF), cot)
        sacc_ref[0] += fold_rows(d_gate)
        sacc_ref[1] += fold_rows(dn * xhat)
        sacc_ref[2] += fold_rows(dn)

    ahead = [
        column(step * group + u, False, u % SLOTS, not first and u == 0) for u in range(group)
    ]
    for turn in range(STAGES + LAG * (group - 1)):
        for u in range(group):
            if LAG * u <= turn < STAGES + LAG * u:
                next(ahead[u], None)

    @pl.when(step == cols // group - 1)
    def _():
        @pl.when(jnp.max(off_ref[...]) > 0.0)
        def _():
            begin()
            if not first:
                total_copy().wait()

            @pl.loop(0, cols)
            def _(j):
                for _ in column(j, True, 0):
                    pass

        if not first and not last:
            early_copy().wait()
        if last:
            for h in range(heads):
                for t in range(thirds):
                    plane = bacc_ref[t * channels : (t + 1) * channels, h * n : (h + 1) * n].T
                    out_ref[:, h * thirds + t] = plane.reshape(src, n // src, channels).astype(BF)
            terms = []
            for w in range(5):
                part = wacc_ref[:, w * channels : (w + 1) * channels].reshape(src, -1, channels)
                terms.append(part.astype(BF).astype(F32))
                terms.append(part - terms[-1])
            terms += [jnp.zeros_like(terms[0])] * 2
            for w in range(SHARES):
                three = jnp.concatenate(terms[3 * w : 3 * w + 3], axis=1)
                out_ref[:, slots + w] = three.astype(BF)


def whole(shape):
    return pl.BlockSpec(shape, lambda j: (0,) * len(shape))


def columns_call(first, last, col0, cols, group, length, own, moved, state, weights, heads):
    src, _, rows, channels = moved.shape
    n = src * rows
    slots = heads * n // channels
    smem = pl.BlockSpec(memory_space=pltpu.SMEM)
    plane = jax.ShapeDtypeStruct((n, heads * n), F32)
    wide = jax.ShapeDtypeStruct((channels, 5 * channels), F32)
    outs = [
        jax.ShapeDtypeStruct((src, cols + (slots + SHARES if last else col0), rows, channels), BF),
        jax.ShapeDtypeStruct((3, 8, channels), F32),
    ]
    outs += ([] if last else [plane, wide]) + ([plane] if first else [])
    inputs = (moved, *state, *weights)
    anywhere = pl.BlockSpec(memory_space=pl.ANY)
    in_specs = [smem, smem] + [whole(a.shape) for a in inputs]
    if not first:
        in_specs[4] = anywhere
    if len(state) > 4:
        in_specs[7] = anywhere
    return pl.pallas_call(
        functools.partial(columns_kernel, heads, first, last, col0, cols, group),
        grid=(cols // group,),
        in_specs=in_specs,
        out_specs=[whole(o.shape) for o in outs],
        out_shape=outs,
        scratch_shapes=[
            pltpu.VMEM((SLOTS, n, heads * n), BF),
            pltpu.VMEM((SLOTS, n, heads * n), BF),
            pltpu.VMEM((SLOTS, heads * n, channels), BF),
            pltpu.VMEM((SLOTS, heads * n, 2 * channels), BF),
            pltpu.VMEM((8, channels), F32),
            pltpu.SemaphoreType.DMA((2,)),
        ]
        + ([pltpu.VMEM(o.shape, F32) for o in (plane, wide)] if last else []),
        compiler_params=pltpu.CompilerParams(
            vmem_limit_bytes=56 * MIB, dimension_semantics=("arbitrary",)
        ),
        cost_estimate=pl.CostEstimate(
            flops=cols * 4 * 10**9, bytes_accessed=cols * n * channels * 6, transcendentals=0
        ),
    )(length, own, *inputs)


def normed_kernel(pair_ref, gain_ref, shift_ref, out_ref):
    rows, n, channels = pair_ref.shape
    xhat, _ = norm_parts(pair_ref[...].astype(F32).reshape(rows * n, channels).astype(BF))
    normed = xhat * gain_ref[...] + shift_ref[...]
    out_ref[:, :, :channels] = normed.reshape(rows, n, channels).astype(BF)
    out_ref[:, :, channels:] = xhat.reshape(rows, n, channels).astype(BF)


def side_kernel(heads, normed_ref, parts_ref, wbt_ref, sacc_ref, sum_ref, told_ref):
    rows, n, channels = parts_ref.shape[2], sum_ref.shape[2], parts_ref.shape[3]
    thirds = n // channels
    slots = heads * thirds
    share_ref = told_ref.at[0]
    total = jnp.sum(parts_ref[:, :slots].astype(F32), axis=0).astype(BF).astype(F32)
    for h in range(heads):
        for t in range(thirds):
            sum_ref[h, :, t * channels : (t + 1) * channels] = total[h * thirds + t]
    terms = []
    for w in range(SHARES):
        part = jnp.sum(parts_ref[:, slots + w].astype(F32), axis=0)
        terms += [part[:8], part[8:16], part[16:24]]
    for w in range(5):
        share_ref[w] = terms[2 * w] + terms[2 * w + 1]
    stats = jnp.zeros((heads, 2 * channels), F32)
    flat = jnp.zeros((heads, n), F32)
    for r in range(rows):
        own = sum_ref[:, r, :]
        flat = flat + own
        stats = stats + dot(own.astype(BF), normed_ref[r])
    wide = wbt_ref[...].astype(F32)
    share_ref[5, 0:1, :] = jnp.sum(sacc_ref[0], axis=0, keepdims=True)
    gain_part = wide * stats[:, channels:]
    gain_all = jnp.sum(sacc_ref[1], axis=0, keepdims=True)
    share_ref[5, 1:2, :] = gain_all + jnp.sum(gain_part, axis=0, keepdims=True)
    shift_part = wide * jnp.sum(flat, axis=1, keepdims=True)
    shift_all = jnp.sum(sacc_ref[2], axis=0, keepdims=True)
    share_ref[5, 2:3, :] = shift_all + jnp.sum(shift_part, axis=0, keepdims=True)
    share_ref[5, 3 : 3 + heads, :] = stats[:, :channels]
    share_ref[5, 3 + heads :, :] = jnp.zeros((5 - heads, channels), F32)
    for d in range(1, told_ref.shape[0]):
        told_ref[d] = share_ref[...]


def norm_back_kernel(first, pair_ref, sums_ref, gain_ref, wbt_ref, *refs):
    parts, out_ref, side_ref = refs[:2], refs[-2], refs[-1]
    rows, cols, channels = pair_ref.shape
    heads, n = sums_ref.shape[0], sums_ref.shape[2]
    step = pl.program_id(0)

    @pl.when(step == 0)
    def _():
        none = jnp.zeros((8 - heads, n), F32)
        span = side_ref.shape[1]
        for r in range(rows):
            own = jnp.concatenate([sums_ref[:, r, :], none], axis=0).T
            own = own[first * cols : first * cols + span, :heads].astype(BF)
            side_ref[r] = dot(own, wbt_ref[...])

    pieces = []
    for s in range(cols // rows):
        for ref, w in zip(parts, (sum(CHUNKS[:-1]), CHUNKS[-1])):
            pieces.append(ref[s, ref.shape[1] - w :].astype(F32))
    main = jnp.swapaxes(jnp.concatenate(pieces, axis=0), 0, 1)
    side = side_ref[:, pl.ds(pl.multiple_of(step * cols, cols), cols), :]
    d_normed = (main + side).astype(BF).astype(F32).reshape(rows * cols, channels)
    cells = pair_ref[...].astype(F32).reshape(rows * cols, channels).astype(BF)
    xhat, scale = norm_parts(cells)
    g = d_normed * gain_ref[...]
    dx = scale * (g - lane_mean(g) - xhat * lane_mean(g * xhat))
    out_ref[...] = dx.reshape(rows, cols, channels).astype(BF)


def final_kernel(heads, size, told_ref, proj_ref, gate_ref, biasw_ref, outw_ref, gain_ref, shift_ref):
    channels = told_ref.shape[-1]
    scale = 1.0 / size
    for w in range(5):
        part = told_ref[:, w].reshape(channels, channels) * scale
        if w < 4:
            proj_ref[:, w * channels : (w + 1) * channels] = part
        else:
            outw_ref[...] = part
    small = jnp.sum(told_ref[:, 5], axis=0) * scale
    gate_ref[...] = small[0:1]
    gain_ref[...] = small[1:2]
    shift_ref[...] = small[2:3]
    biasw_ref[...] = small[3 : 3 + heads]


def body(pair_rep, grad_out, crop_len, ln_gain, ln_bias, w_proj, gate_bias, w_bias, w_out):
    pair, cot = pair_rep[0], grad_out[0]
    rows, n, channels = pair.shape
    heads = w_bias.shape[1]
    src = n // rows
    slots = heads * n // channels
    own = (lax.axis_index("row") * rows).astype(jnp.int32).reshape(1)
    gain, shift = ln_gain.reshape(1, -1), ln_bias.reshape(1, -1)
    wbt = w_bias.T
    weights = (gain, shift, w_proj, w_proj.T, gate_bias.reshape(1, -1), w_out.T)

    def exchange(a, axis="row"):
        return lax.all_to_all(a, axis, 0, 0)

    def tell(a, axis):
        return exchange(jnp.broadcast_to(a[None], (lax.axis_size(axis), *a.shape)), axis)

    block = 2
    tile = block * rows
    lines = 8
    plane = pl.pallas_call(
        functools.partial(logits_kernel, heads),
        grid=(rows // lines,),
        in_specs=[pl.BlockSpec((lines, n, channels), lambda j: (j, 0, 0))]
        + [whole(a.shape) for a in (gain, shift, wbt)],
        out_specs=pl.BlockSpec((slots, lines, channels), lambda j: (0, j, 0)),
        out_shape=jax.ShapeDtypeStruct((slots, rows, channels), F32),
        compiler_params=pltpu.CompilerParams(vmem_limit_bytes=60 * MIB),
    )(pair, gain, shift, wbt)
    many = src // 2
    both = pl.pallas_call(
        normed_kernel,
        grid=(rows // lines,),
        in_specs=[pl.BlockSpec((lines, n, channels), lambda j: (j, 0, 0))]
        + [whole(a.shape) for a in (gain, shift)],
        out_specs=pl.BlockSpec((lines, n, 2 * channels), lambda j: (j, 0, 0)),
        out_shape=jax.ShapeDtypeStruct((rows, n, 2 * channels), BF),
        compiler_params=pltpu.CompilerParams(vmem_limit_bytes=60 * MIB),
        cost_estimate=pl.CostEstimate(
            flops=5 * 10**9, bytes_accessed=6 * pair.size, transcendentals=0
        ),
    )(pair, gain, shift)
    cells = pl.BlockSpec((rows, many * rows, channels), lambda j: (0, j, 0))

    def send(start, count, extra):
        deep = 2 * count + sum(a.shape[0] for a in extra)
        return pl.pallas_call(
            functools.partial(send_kernel, start, count),
            grid=(src // many,),
            in_specs=[cells, cells] + [whole(a.shape) for a in extra],
            out_specs=pl.BlockSpec((many, deep, rows, channels), lambda j: (j, 0, 0, 0)),
            out_shape=jax.ShapeDtypeStruct((src, deep, rows, channels), BF),
            compiler_params=pltpu.CompilerParams(vmem_limit_bytes=60 * MIB),
            cost_estimate=pl.CostEstimate(
                flops=5 * 10**9, bytes_accessed=3 * pair.size, transcendentals=0
            ),
        )(pair, cot, *extra)

    starts = [sum(CHUNKS[:c]) for c in range(len(CHUNKS))]
    sent = [send(a, w, (plane,) if a == 0 else ()) for a, w in zip(starts, CHUNKS)]
    moved = [exchange(a) for a in sent]
    state, back = (), []
    for c, (start, width, group, piece) in enumerate(zip(starts, CHUNKS, GROUPS, moved)):
        first, last = c == 0, c == len(CHUNKS) - 1
        out, sacc, *rest = columns_call(
            first, last, start, width, group, crop_len, own, piece, state, weights, heads
        )
        if not last:
            plane = rest[2] if first else state[0]
            state = (plane, rest[0], rest[1], sacc)
            if c == len(CHUNKS) - 2:
                early = exchange(out)
            else:
                state += (out,)
    out, early = lax.optimization_barrier((out, early))
    bundle = exchange(out)
    back = (early, bundle)

    copies = lax.axis_size("dp")
    sums, share = pl.pallas_call(
        functools.partial(side_kernel, heads),
        grid=(1,),
        in_specs=[
            whole(both.shape),
            pl.BlockSpec((src, slots + SHARES, rows, channels), lambda j: (0, 0, 0, 0)),
        ]
        + [whole(a.shape) for a in (wbt, sacc)],
        out_specs=[whole((heads, rows, n)), whole((copies, 6, 8, channels))],
        out_shape=[
            jax.ShapeDtypeStruct((heads, rows, n), F32),
            jax.ShapeDtypeStruct((copies, 6, 8, channels), F32),
        ],
        compiler_params=pltpu.CompilerParams(vmem_limit_bytes=60 * MIB),
    )(both, bundle, wbt, sacc)
    def norm_back(first, steps, *written):
        place = lambda j: (0, j + first, 0)
        inputs = (pair, sums, gain, wbt, *back)
        return pl.pallas_call(
            functools.partial(norm_back_kernel, first),
            grid=(steps,),
            in_specs=[pl.BlockSpec((rows, tile, channels), place)]
            + [whole(a.shape) for a in (sums, gain, wbt)]
            + [pl.BlockSpec((block, *a.shape[1:]), lambda j: (j + first, 0, 0, 0)) for a in back]
            + [pl.BlockSpec(memory_space=pl.ANY)] * len(written),
            out_specs=pl.BlockSpec((rows, tile, channels), place),
            out_shape=jax.ShapeDtypeStruct(pair.shape, BF),
            scratch_shapes=[pltpu.VMEM((rows, steps * tile, channels), F32)],
            input_output_aliases={len(inputs): 0} if written else {},
            compiler_params=pltpu.CompilerParams(vmem_limit_bytes=60 * MIB),
            cost_estimate=pl.CostEstimate(
                flops=6 * 10**9, bytes_accessed=2 * pair.size, transcendentals=0
            ),
        )(*inputs, *written)

    blocks = n // tile
    share = exchange(share, "dp")
    pair_grad = norm_back(0, blocks // 2)
    share, pair_grad = lax.optimization_barrier((share, pair_grad))
    told = tell(jnp.sum(share, axis=0), "row")
    pair_grad = norm_back(blocks // 2, blocks - blocks // 2, pair_grad)
    proj, gate, biasw, outw, gain_sum, shift_sum = pl.pallas_call(
        functools.partial(final_kernel, heads, n),
        out_shape=[
            jax.ShapeDtypeStruct(s, F32)
            for s in (
                w_proj.shape,
                (1, channels),
                (heads, channels),
                w_out.shape,
                (1, channels),
                (1, channels),
            )
        ],
    )(told)
    return (
        pair_grad[None],
        proj,
        gate.reshape(-1),
        biasw.T,
        outw,
        gain_sum.reshape(-1),
        shift_sum.reshape(-1),
    )


def solution(mesh):
    placed = (
        P("dp", "row", None, None),
        P("dp", "row", None, None),
        P("dp"),
        P(),
        P(),
        P(),
        P(),
        P(),
        P(),
    )
    return jax.shard_map(
        body,
        mesh=mesh,
        in_specs=placed,
        out_specs=(P("dp", "row", None, None), P(), P(), P(), P(), P(), P()),
        check_vma=False,
    )
```
